32 devices in a mesh: span: 4 (over z), head: 2 (over x), rep: 4 (over y, core).
Axes of the slice: x: 2, y: 2, z: 4, core: 2. Of those that a mesh axis runs over, the one named last changes fastest.
Arguments:
- queries: bfloat16 [2048, 6144], P(('rep', 'span', 'head')), parts along dimension 0, may hold values from -10 to 10
- key_value: bfloat16 [2048, 2, 1024], P(('rep', 'span', 'head')), parts along dimension 0, may hold values from -4 to 4
- w_out: bfloat16 [6144, 6144], P('head'), may hold values from -0.078125 to 0.078125
- gate_table: bfloat16 [64, 6144], replicated, may hold values from 0.25 to 2
- levels: int32 [16], P('rep'), parts along dimension 0, may hold values from 0 to 63
- span_mask: int32 [16, 4], P('rep'), parts along dimension 0, may hold values from 0 to 1, as said below
- counts: int32 [16], P('rep'), parts along dimension 0, may hold values from 64 to 128, as said below
Outputs:
- output: bfloat16 [2048, 6144], P(('rep', 'span', 'head')), parts along dimension 0
The draws below stay inside these ranges and needn't reach their ends.
There are 4 independent parts, one for each index of `rep`. The reference program is written for one: setup_inputs(seed, part) draws one part's arguments, and reference() takes and returns one part's arrays. A program takes and returns all parts, laid end to end along the dimension named above; an argument that names none is the same for every part. Nothing has to cross between parts.
Inputs may be any that keep to these rules, and one draw needn't show every extreme that they name: span_mask[i, i] = 1 and span_mask[i, i - 1] = 1; span_mask[i, j] = 0 for j > i; the entries for j < i - 1 are drawn. `counts`: in every video one span has exactly 128 live tokens and another exactly 64.
All inputs are finite; a program needn't handle non-finite values.
Results may differ from the reference program's by a relative error of at most 0.024.
Values may be sent and summed in bfloat16 or wider, within the bound.
No kernel may reach another device: no remote copies, remote signals or barrier semaphores. Data moves between devices by JAX's collectives and lax.ppermute only.
A program may use at most 128 MiB of HBM per device.

```python
import jax
import jax.numpy as jnp
from jax import lax

D = 6144
HEADS = 48
HD = 128
KV_GROUPS = 8
LEVELS = 64
SPAN_TOKENS = 128
SPANS = 4
TOKENS = 512
KV_COLS = 1024
N_HEAD = 2


def draw_queries(key, part):
    key = jax.random.fold_in(key, 11)
    noise_key = jax.random.fold_in(key, 0)
    drawn = jnp.clip(jax.random.normal(noise_key, (TOKENS, D), jnp.float32), -4.0, 4.0) * 2.5
    return drawn.astype(jnp.bfloat16)


def draw_key_value(key, part):
    key = jax.random.fold_in(key, 14)
    noise_key = jax.random.fold_in(key, 0)
    drawn = jnp.clip(jax.random.normal(noise_key, (TOKENS, 2, KV_COLS), jnp.float32), -4.0, 4.0)
    return drawn.astype(jnp.bfloat16)


def draw_span_mask(key, part):
    key = jax.random.fold_in(key, 12)
    row_ids = jnp.arange(SPANS, dtype=jnp.int32)[:, None]
    col_ids = jnp.arange(SPANS, dtype=jnp.int32)[None, :]
    drawn = jax.random.randint(key, (SPANS, SPANS), 0, 2, dtype=jnp.int32)
    nearby = (col_ids == row_ids) | (col_ids == row_ids - 1)
    return jnp.where(nearby, 1, jnp.where(col_ids < row_ids, drawn, 0)).astype(jnp.int32)


def draw_counts(key, part):
    key = jax.random.fold_in(key, 13)
    first_key, second_key, third_key = jax.random.split(key, 3)
    drawn = jax.random.randint(first_key, (SPANS,), SPAN_TOKENS // 2, SPAN_TOKENS + 1, dtype=jnp.int32)
    full_id = jax.random.randint(second_key, (), 0, SPANS, dtype=jnp.int32)
    half_id = (full_id + 1 + jax.random.randint(third_key, (), 0, SPANS - 1, dtype=jnp.int32)) % SPANS
    span_ids = jnp.arange(SPANS, dtype=jnp.int32)
    drawn = jnp.where(span_ids == half_id, SPAN_TOKENS // 2, drawn)
    return jnp.where(span_ids == full_id, SPAN_TOKENS, drawn).astype(jnp.int32)


def place_ends(values, own_key, low, top_value):
    place = [jax.random.randint(jax.random.fold_in(own_key, axis), (), 0, length) for axis, length in enumerate(values.shape)]
    widest = values.shape.index(max(values.shape))
    neighbour = place[:widest] + [(place[widest] + 1) % values.shape[widest]] + place[widest + 1:]
    return values.at[tuple(place)].set(low).at[tuple(neighbour)].set(top_value)


def block_scale(rng, shape, pieces, smallest, top_value):
    def one(dim, parts):
        draws = jax.random.uniform(jax.random.fold_in(jax.random.fold_in(rng, 6), dim), (parts,), jnp.float32, smallest / len(pieces), top_value / len(pieces))
        return jnp.repeat(jnp.exp(draws), shape[dim] // parts).reshape((-1,) + (1,) * (len(shape) - dim - 1))

    loudness = one(*pieces[0])
    for cut in pieces[1:]:
        loudness = loudness * one(*cut)
    return loudness


def noise(key, shape, deviation, most, cuts=(), kind=jnp.bfloat16):
    factor_of = block_scale(key, shape, cuts, -0.22, 0.18) if cuts else 1.0
    result = jax.random.normal(key, shape, jnp.float32) * deviation * factor_of
    return jnp.minimum(jnp.maximum(result, -most), most).astype(kind)


def setup_inputs(seed: int = 0, part: int = 0) -> dict:
    keys = jax.random.split(jax.random.key(seed), 8)
    part_splits = jax.random.split(jax.random.fold_in(keys[7], part), 8)
    return {
        "queries": draw_queries(jax.random.fold_in(jax.random.fold_in(keys[7], part), 71), part),
        "key_value": draw_key_value(jax.random.fold_in(jax.random.fold_in(keys[7], part), 71), part),
        "w_out": noise(keys[2], (D, D), D ** -0.5, 0.078125, ((0, 2),)),
        "gate_table": jnp.clip(jax.random.uniform(keys[3], (LEVELS, D), jnp.float32, 0.25, 2.0), 0.25, 2.0).astype(jnp.bfloat16),
        "levels": place_ends(jax.random.randint(part_splits[4], (SPANS,), 0, LEVELS), jax.random.fold_in(part_splits[4], 1), 0, LEVELS - 1).astype(jnp.int32),
        "span_mask": draw_span_mask(jax.random.fold_in(jax.random.fold_in(keys[7], part), 71), part),
        "counts": draw_counts(jax.random.fold_in(jax.random.fold_in(keys[7], part), 71), part),
    }


NEG_FILL = -1e30


def reference(queries, key_value, w_out, gate_table, levels, span_mask, counts):
    score_scale = HD ** -0.5
    share = HEADS // KV_GROUPS
    token_ids = jnp.arange(TOKENS, dtype=jnp.int32)
    key_span = token_ids // SPAN_TOKENS
    key_pos = token_ids % SPAN_TOKENS
    key_limit = counts[key_span]
    key_rows = key_value[:, 0].reshape(TOKENS, KV_GROUPS, HD).transpose(1, 0, 2)
    value_rows = key_value[:, 1].reshape(TOKENS, KV_GROUPS, HD).transpose(1, 0, 2)
    group = D // N_HEAD
    head_ids = jnp.arange(HEADS, dtype=jnp.int32)
    outputs = []
    for source in range(SPANS):
        usable = (span_mask[source][key_span] > 0) & (key_pos < key_limit)
        query_block = queries[source * SPAN_TOKENS:(source + 1) * SPAN_TOKENS]
        query_block = query_block.reshape(SPAN_TOKENS, HEADS, HD).transpose(1, 0, 2)

        def one_head(operands):
            query, head_id = operands
            keyset = key_rows[head_id // share]
            valueset = value_rows[head_id // share]
            scores = jnp.dot(query, keyset.T, preferred_element_type=jnp.float32) * score_scale
            scores = jnp.where(usable[None, :], scores, NEG_FILL)
            highest = jnp.max(scores, axis=1, keepdims=True)
            weights = jnp.where(usable[None, :], jnp.exp(scores - highest), 0.0)
            totals = jnp.sum(weights, axis=1, keepdims=True)
            summed = jnp.dot(weights.astype(jnp.bfloat16), valueset, preferred_element_type=jnp.float32)
            return summed / totals

        attended = lax.map(one_head, (query_block, head_ids))
        attended = attended.transpose(1, 0, 2).reshape(SPAN_TOKENS, D).astype(jnp.bfloat16)
        projected = jnp.zeros((SPAN_TOKENS, D), jnp.float32)
        for shard in range(N_HEAD):
            partial_value = jnp.dot(attended[:, shard * group:(shard + 1) * group],
                              w_out[shard * group:(shard + 1) * group],
                              preferred_element_type=jnp.float32)
            projected = projected + lax.optimization_barrier(partial_value.astype(jnp.bfloat16)).astype(jnp.float32)
        gate_row = gate_table[levels[source]].astype(jnp.float32)
        live = jnp.arange(SPAN_TOKENS, dtype=jnp.int32) < counts[source]
        outputs.append(jnp.where(live[:, None], projected * gate_row[None, :], 0.0).astype(jnp.bfloat16))
    return jnp.concatenate(outputs, axis=0)
```

```python
import functools
import math

import jax
import jax.numpy as jnp
from jax import lax
from jax.experimental import pallas as pl
from jax.experimental.pallas import tpu as pltpu
from jax.sharding import PartitionSpec as P

HEADS = 48
HD = 128
KV_GROUPS = 8

NEG_FILL = -1e30
EXP_SCALE = HD ** (-0.5) * math.log2(math.e)
VMEM_LIMIT = 48 * 1024 * 1024

VMEM = pl.BlockSpec(memory_space=pltpu.VMEM)
SMEM = pl.BlockSpec(memory_space=pltpu.SMEM)


def split_kernel(group_width, starts_ref, kv_ref, *out_refs):
    for j, out_ref in enumerate(out_refs):
        columns = pl.ds(pl.multiple_of(starts_ref[j], HD), group_width)
        out_ref[:, :group_width] = kv_ref[:, 0, columns]
        out_ref[:, group_width:] = kv_ref[:, 1, columns]


def split_key_value(key_value, starts, pieces, group_width):
    rows = key_value.shape[0]
    shape = jax.ShapeDtypeStruct((rows, 2 * group_width), key_value.dtype)
    return pl.pallas_call(
        functools.partial(split_kernel, group_width),
        out_shape=[shape] * pieces,
        in_specs=[SMEM, VMEM],
        out_specs=[VMEM] * pieces,
        compiler_params=pltpu.CompilerParams(vmem_limit_bytes=VMEM_LIMIT),
        cost_estimate=pl.CostEstimate(
            flops=0, bytes_accessed=4 * key_value.size, transcendentals=0
        ),
        name="split_key_value",
    )(starts, key_value)


def softmax_block(query, keys, values, usable):
    scores = lax.dot_general(
        query, keys, (((1,), (1,)), ((), ())), preferred_element_type=jnp.float32
    )
    scores = jnp.where(usable, scores, NEG_FILL)
    highest = jnp.max(scores, axis=1, keepdims=True)
    weights = jnp.exp2((scores - highest) * EXP_SCALE)
    totals = jnp.sum(weights, axis=1, keepdims=True)
    summed = jnp.dot(weights.astype(jnp.bfloat16), values, preferred_element_type=jnp.float32)
    return summed / totals


def attention_kernel(n_query, n_kv, groups, sharing, row_tile, start_ref, usable_ref, *refs):
    query_refs, kv_refs, out_ref = refs[:n_query], refs[n_query : n_query + n_kv], refs[-1]
    group_width = groups * HD
    span = sharing * HD
    usable = usable_ref[...] > 0
    for g in range(groups):
        keys = jnp.concatenate([r[:, g * HD : (g + 1) * HD] for r in kv_refs], axis=0)
        values = jnp.concatenate(
            [r[:, group_width + g * HD : group_width + (g + 1) * HD] for r in kv_refs], axis=0
        )
        done = 0
        for i, query_ref in enumerate(query_refs):
            rows = query_ref.shape[0]
            column = pl.multiple_of(start_ref[i] + g * span, HD)
            for first in range(0, rows, row_tile):
                tile = min(row_tile, rows - first)
                block = query_ref[first : first + tile, pl.ds(column, span)]
                query = jnp.concatenate(
                    [block[:, h * HD : (h + 1) * HD] for h in range(sharing)], axis=0
                )
                result = softmax_block(query, keys, values, usable).astype(jnp.bfloat16)
                for h in range(sharing):
                    out_ref[
                        done + first : done + first + tile,
                        g * span + h * HD : g * span + (h + 1) * HD,
                    ] = result[h * tile : (h + 1) * tile]
            done += rows


def attention(query_pieces, starts, kv_pieces, usable, groups, sharing):
    rows = sum(p.shape[0] for p in query_pieces)
    keys = usable.shape[1]
    width = groups * sharing * HD
    return pl.pallas_call(
        functools.partial(
            attention_kernel, len(query_pieces), len(kv_pieces), groups, sharing, 64
        ),
        out_shape=jax.ShapeDtypeStruct((rows, width), jnp.bfloat16),
        in_specs=[SMEM, VMEM] + [VMEM] * (len(query_pieces) + len(kv_pieces)),
        out_specs=VMEM,
        compiler_params=pltpu.CompilerParams(vmem_limit_bytes=VMEM_LIMIT),
        cost_estimate=pl.CostEstimate(
            flops=4 * rows * width * keys,
            bytes_accessed=4 * rows * width + 4 * groups * HD * keys,
            transcendentals=rows * keys * groups * sharing,
        ),
        name="attention",
    )(starts, usable, *query_pieces, *kv_pieces)


def project_kernel(own_rows, attended_ref, weight_ref, own_ref, other_ref):
    product = jnp.dot(attended_ref[...], weight_ref[...], preferred_element_type=jnp.float32)
    own_ref[...] = product[:own_rows]
    other_ref[...] = product[own_rows:].astype(jnp.bfloat16)


def project(attended, w_out, first, count, block, own_rows):
    rows, depth = attended.shape
    other_rows = rows - own_rows
    base = first // block
    return pl.pallas_call(
        functools.partial(project_kernel, own_rows),
        grid=(count // block,),
        out_shape=[
            jax.ShapeDtypeStruct((own_rows, count), jnp.float32),
            jax.ShapeDtypeStruct((other_rows, count), jnp.bfloat16),
        ],
        in_specs=[
            pl.BlockSpec((rows, depth), lambda j: (0, 0)),
            pl.BlockSpec((depth, block), lambda j: (0, base + j)),
        ],
        out_specs=[
            pl.BlockSpec((own_rows, block), lambda j: (0, j)),
            pl.BlockSpec((other_rows, block), lambda j: (0, j)),
        ],
        compiler_params=pltpu.CompilerParams(vmem_limit_bytes=VMEM_LIMIT),
        cost_estimate=pl.CostEstimate(
            flops=2 * rows * depth * count, bytes_accessed=2 * depth * count, transcendentals=0
        ),
        name="project",
    )(attended, w_out)


def combine_kernel(n_chunks, live_ref, gate_ref, *refs):
    own_refs, other_refs, out_ref = refs[:n_chunks], refs[n_chunks : 2 * n_chunks], refs[-1]
    rows = out_ref.shape[0]
    live = lax.broadcasted_iota(jnp.int32, (rows, 1), 0) < live_ref[0]
    first = 0
    for own_ref, other_ref in zip(own_refs, other_refs):
        columns = slice(first, first + own_ref.shape[1])
        total = own_ref[...] + other_ref[...].astype(jnp.float32)
        gated = total * gate_ref[:, columns].astype(jnp.float32)
        out_ref[:, columns] = jnp.where(live, gated, 0.0).astype(jnp.bfloat16)
        first += own_ref.shape[1]


def combine(own_parts, other_parts, gate_row, live):
    rows = own_parts[0].shape[0]
    width = sum(p.shape[1] for p in own_parts)
    return pl.pallas_call(
        functools.partial(combine_kernel, len(own_parts)),
        out_shape=jax.ShapeDtypeStruct((rows, width), jnp.bfloat16),
        in_specs=[SMEM, VMEM] + [VMEM] * (2 * len(own_parts)),
        out_specs=VMEM,
        compiler_params=pltpu.CompilerParams(vmem_limit_bytes=VMEM_LIMIT),
        cost_estimate=pl.CostEstimate(
            flops=2 * rows * width, bytes_accessed=8 * rows * width, transcendentals=0
        ),
        name="combine",
    )(live, gate_row, *own_parts, *other_parts)


def usable_row(positions, own_span, span_mask, counts):
    spans = span_mask.shape[0]
    rows = []
    for back in range(spans):
        source = jnp.maximum(own_span - back, 0)
        allowed = (span_mask[own_span, source] > 0) & (own_span >= back)
        rows.append(allowed & (positions < counts[source]))
    return jnp.concatenate(rows).astype(jnp.int32)[None, :]


def local(queries, key_value, w_out, gate_table, levels, span_mask, counts):
    tokens = queries.shape[0]
    shards = lax.axis_size("head")
    spans = lax.axis_size("span")
    own_shard = lax.axis_index("head")
    own_span = lax.axis_index("span")
    head_count = HEADS // shards
    share = HEADS // KV_GROUPS
    sharing = min(share, head_count)
    groups = head_count // sharing
    group_width = groups * HD
    width = head_count * HD
    local_ids = jnp.arange(tokens, dtype=jnp.int32)

    if shards == 2:
        order = jnp.stack([own_shard, 1 - own_shard]).astype(jnp.int32)
        swap = [(0, 1), (1, 0)]
        own_kv, sent_kv = split_key_value(key_value, order * group_width, 2, group_width)
        kv_pieces = [own_kv, lax.ppermute(sent_kv, "head", swap)]
        sent_queries = lax.dynamic_slice_in_dim(queries, order[1] * width, width, 1)
        query_pieces = [queries, lax.ppermute(sent_queries, "head", swap)]
        starts = jnp.stack([order[0] * width, jnp.int32(0)])
        positions = jnp.concatenate([order[0] * tokens + local_ids, order[1] * tokens + local_ids])
    else:
        first_group = (jnp.arange(shards, dtype=jnp.int32) * head_count) // share
        pieces = split_key_value(key_value, first_group * HD, shards, group_width)
        swapped = lax.all_to_all(jnp.stack(pieces), "head", split_axis=0, concat_axis=0)
        kv_pieces = [swapped.reshape(shards * tokens, 2 * group_width)]
        by_shard = queries.reshape(tokens, shards, width).transpose(1, 0, 2)
        swapped = lax.all_to_all(by_shard, "head", split_axis=0, concat_axis=0)
        query_pieces = [swapped.reshape(shards * tokens, width)]
        starts = jnp.zeros((1,), jnp.int32)
        positions = jnp.arange(shards * tokens, dtype=jnp.int32)

    blocks = list(kv_pieces)
    for back in range(1, spans):
        upward = [(i, i + back) for i in range(spans - back)]
        blocks += [lax.ppermute(piece, "span", upward) for piece in kv_pieces]
    usable = usable_row(positions, own_span, span_mask, counts)
    attended = attention(query_pieces, starts, blocks, usable, groups, sharing)

    gate_row = lax.dynamic_slice_in_dim(gate_table, levels[own_span], 1, 0)
    live = jnp.maximum(counts[own_span] - own_shard * tokens, 0).astype(jnp.int32)[None]
    columns = w_out.shape[1]
    if shards == 2:
        sizes = [columns // 12, columns // 6, columns // 4, columns // 4, columns // 4]
        own_parts, other_parts = [], []
        first = 0
        for size in sizes:
            own, other = project(attended, w_out, first, size, columns // 12, tokens)
            own_parts.append(own)
            other_parts.append(lax.ppermute(other, "head", swap))
            first += size
    else:
        partial = jnp.dot(attended, w_out, preferred_element_type=jnp.float32)
        summed = lax.psum_scatter(
            partial.astype(jnp.bfloat16), "head", scatter_dimension=0, tiled=True
        )
        own_parts, other_parts = [jnp.zeros(summed.shape, jnp.float32)], [summed]
    return combine(own_parts, other_parts, gate_row, live)


def solution(mesh):
    in_specs = (
        P(("rep", "span", "head"), None),
        P(("rep", "span", "head"), None, None),
        P("head", None),
        P(),
        P("rep"),
        P("rep", None),
        P("rep"),
    )
    out_specs = P(("rep", "span", "head"), None)
    return jax.shard_map(local, mesh=mesh, in_specs=in_specs, out_specs=out_specs, check_vma=False)
```

```python
import functools
import math

import jax
import jax.numpy as jnp
from jax import lax
from jax.experimental import pallas as pl
from jax.experimental.pallas import tpu as pltpu
from jax.sharding import PartitionSpec as P

HEADS = 48
HD = 128
KV_GROUPS = 8

NEG_FILL = -1e30
EXP_SCALE = HD ** (-0.5) * math.log2(math.e)
VMEM_LIMIT = 48 * 1024 * 1024

VMEM = pl.BlockSpec(memory_space=pltpu.VMEM)
SMEM = pl.BlockSpec(memory_space=pltpu.SMEM)
ANY = pl.BlockSpec(memory_space=pl.ANY)


def column_starts(place_ref, pieces, width):
    if pieces == 2:
        own = place_ref[1]
        return [pl.multiple_of(own * width, HD), pl.multiple_of((1 - own) * width, HD)]
    return [piece * width for piece in range(pieces)]


def split_kv_kernel(group_width, copies, n_after, place_ref, kv_ref, *refs):
    out_refs = refs[n_after:]
    if copies == 1:
        starts = column_starts(place_ref, len(out_refs), group_width)
    else:
        starts = [piece // copies * group_width for piece in range(len(out_refs))]
    for start, out_ref in zip(starts, out_refs):
        out_ref[:, :group_width] = kv_ref[:, 0, pl.ds(start, group_width)]
        out_ref[:, group_width:] = kv_ref[:, 1, pl.ds(start, group_width)]


def split_queries_kernel(n_after, place_ref, query_ref, *refs):
    out_refs = refs[n_after:]
    width = out_refs[0].shape[1]
    for start, out_ref in zip(column_starts(place_ref, len(out_refs), width), out_refs):
        out_ref[...] = query_ref[:, pl.ds(start, width)]


def split(kernel, place, array, pieces, width, after, name):
    shape = jax.ShapeDtypeStruct((array.shape[0], width), array.dtype)
    return pl.pallas_call(
        functools.partial(kernel, len(after)),
        out_shape=[shape] * pieces,
        in_specs=[SMEM, VMEM] + [ANY] * len(after),
        out_specs=[VMEM] * pieces,
        compiler_params=pltpu.CompilerParams(vmem_limit_bytes=VMEM_LIMIT),
        cost_estimate=pl.CostEstimate(
            flops=0, bytes_accessed=4 * array.size, transcendentals=0
        ),
        name=name,
    )(place, array, *after)


def softmax_block(query, keys, values, usable):
    scores = lax.dot_general(
        query, keys, (((1,), (1,)), ((), ())), preferred_element_type=jnp.float32
    )
    scores = jnp.where(usable, scores, NEG_FILL)
    highest = jnp.max(scores, axis=1, keepdims=True)
    weights = jnp.exp2((scores - highest) * EXP_SCALE)
    totals = jnp.sum(weights, axis=1, keepdims=True)
    summed = jnp.dot(weights.astype(jnp.bfloat16), values, preferred_element_type=jnp.float32)
    return summed / totals


def usable_row(place_ref, mask_ref, counts_ref, piece_rows, piece_count):
    own_span, own_shard = place_ref[0], place_ref[1]
    row = []
    for back in range(mask_ref.shape[0]):
        source = jnp.maximum(own_span - back, 0)
        allowed = (mask_ref[own_span, source] > 0) & (own_span >= back)
        limit = jnp.where(allowed, counts_ref[source], 0)
        for piece in range(piece_count):
            first = 0
            if piece_count == 2:
                first = (own_shard if piece == 0 else 1 - own_shard) * piece_rows
            positions = first + lax.broadcasted_iota(jnp.int32, (1, piece_rows), 1)
            row.append((positions < limit).astype(jnp.int32))
    return jnp.concatenate(row, axis=1) > 0


def attention_kernel(n_query, groups, sharing, row_tile, place_ref, mask_ref, counts_ref, *refs):
    query_refs, kv_refs, out_ref = refs[:n_query], refs[n_query:-1], refs[-1]
    group_width = groups * HD
    span = sharing * HD
    usable = usable_row(place_ref, mask_ref, counts_ref, kv_refs[0].shape[0], n_query)
    for g in range(groups):
        keys = jnp.concatenate([r[:, g * HD : (g + 1) * HD] for r in kv_refs], axis=0)
        values = jnp.concatenate(
            [r[:, group_width + g * HD : group_width + (g + 1) * HD] for r in kv_refs], axis=0
        )
        done = 0
        for query_ref in query_refs:
            rows = query_ref.shape[0]
            for first in range(0, rows, row_tile):
                tile = min(row_tile, rows - first)
                query = jnp.concatenate(
                    [
                        query_ref[first : first + tile, g * span + h * HD : g * span + (h + 1) * HD]
                        for h in range(sharing)
                    ],
                    axis=0,
                )
                result = softmax_block(query, keys, values, usable).astype(jnp.bfloat16)
                for h in range(sharing):
                    out_ref[
                        done + first : done + first + tile,
                        g * span + h * HD : g * span + (h + 1) * HD,
                    ] = result[h * tile : (h + 1) * tile]
            done += rows


def attention(place, span_mask, counts, query_pieces, kv_pieces, groups, sharing):
    rows = sum(p.shape[0] for p in query_pieces)
    keys = sum(p.shape[0] for p in kv_pieces)
    width = groups * sharing * HD
    return pl.pallas_call(
        functools.partial(attention_kernel, len(query_pieces), groups, sharing, 64),
        out_shape=jax.ShapeDtypeStruct((rows, width), jnp.bfloat16),
        in_specs=[SMEM] * 3 + [VMEM] * (len(query_pieces) + len(kv_pieces)),
        out_specs=VMEM,
        compiler_params=pltpu.CompilerParams(vmem_limit_bytes=VMEM_LIMIT),
        cost_estimate=pl.CostEstimate(
            flops=4 * rows * width * keys,
            bytes_accessed=4 * rows * width + 4 * groups * HD * keys,
            transcendentals=rows * keys * groups * sharing,
        ),
        name="attention",
    )(place, span_mask, counts, *query_pieces, *kv_pieces)


def project_kernel(own_rows, attended_ref, weight_ref, *refs):
    own_ref, other_ref = refs[-2:]
    product = jnp.dot(attended_ref[...], weight_ref[...], preferred_element_type=jnp.float32)
    own_ref[...] = product[:own_rows]
    other_ref[...] = product[own_rows:].astype(jnp.bfloat16)


def project(attended, w_out, first, count, block, own_rows, after):
    rows, depth = attended.shape
    other_rows = rows - own_rows
    base = first // block
    return pl.pallas_call(
        functools.partial(project_kernel, own_rows),
        grid=(count // block,),
        out_shape=[
            jax.ShapeDtypeStruct((own_rows, count), jnp.float32),
            jax.ShapeDtypeStruct((other_rows, count), jnp.bfloat16),
        ],
        in_specs=[
            pl.BlockSpec((rows, depth), lambda j: (0, 0)),
            pl.BlockSpec((depth, block), lambda j: (0, base + j)),
        ]
        + [ANY] * len(after),
        out_specs=[
            pl.BlockSpec((own_rows, block), lambda j: (0, j)),
            pl.BlockSpec((other_rows, block), lambda j: (0, j)),
        ],
        compiler_params=pltpu.CompilerParams(vmem_limit_bytes=VMEM_LIMIT),
        cost_estimate=pl.CostEstimate(
            flops=2 * rows * depth * count, bytes_accessed=2 * depth * count, transcendentals=0
        ),
        name="project",
    )(attended, w_out, *after)


def combine_kernel(n_chunks, place_ref, levels_ref, counts_ref, gate_ref, *refs):
    own_refs, other_refs, out_ref = refs[:n_chunks], refs[n_chunks : 2 * n_chunks], refs[-1]
    rows = out_ref.shape[0]
    own_span, own_shard = place_ref[0], place_ref[1]
    positions = own_shard * rows + lax.broadcasted_iota(jnp.int32, (rows, 1), 0)
    live = positions < counts_ref[own_span]
    chosen = lax.broadcasted_iota(jnp.int32, (gate_ref.shape[0], 1), 0) == levels_ref[own_span]
    first = 0
    for own_ref, other_ref in zip(own_refs, other_refs):
        columns = slice(first, first + own_ref.shape[1])
        gate = jnp.where(chosen, gate_ref[:, columns].astype(jnp.float32), 0.0)
        total = own_ref[...] + other_ref[...].astype(jnp.float32)
        gated = total * jnp.sum(gate, axis=0, keepdims=True)
        out_ref[:, columns] = jnp.where(live, gated, 0.0).astype(jnp.bfloat16)
        first += own_ref.shape[1]


def combine(place, levels, counts, gate_table, own_parts, other_parts):
    rows = own_parts[0].shape[0]
    width = sum(p.shape[1] for p in own_parts)
    return pl.pallas_call(
        functools.partial(combine_kernel, len(own_parts)),
        out_shape=jax.ShapeDtypeStruct((rows, width), jnp.bfloat16),
        in_specs=[SMEM] * 3 + [VMEM] * (1 + 2 * len(own_parts)),
        out_specs=VMEM,
        compiler_params=pltpu.CompilerParams(vmem_limit_bytes=VMEM_LIMIT),
        cost_estimate=pl.CostEstimate(
            flops=2 * rows * width, bytes_accessed=8 * rows * width, transcendentals=0
        ),
        name="combine",
    )(place, levels, counts, gate_table, *own_parts, *other_parts)


def local(queries, key_value, w_out, gate_table, levels, span_mask, counts):
    tokens = queries.shape[0]
    shards = lax.axis_size("head")
    spans = lax.axis_size("span")
    place = jnp.stack([lax.axis_index("span"), lax.axis_index("head")]).astype(jnp.int32)
    head_count = HEADS // shards
    share = HEADS // KV_GROUPS
    sharing = min(share, head_count)
    copies = max(1, share // head_count)
    groups = head_count // sharing
    group_width = groups * HD
    width = head_count * HD
    swap = [(0, 1), (1, 0)]

    split_kv = functools.partial(split_kv_kernel, group_width, copies)
    kv_parts = split(split_kv, place, key_value, shards, 2 * group_width, [], "split_kv")
    if shards == 2:
        kv_pieces = [kv_parts[0], lax.ppermute(kv_parts[1], "head", swap)]
        query_parts = split(
            split_queries_kernel, place, queries, shards, width, kv_pieces[1:], "split_queries"
        )
        query_pieces = [query_parts[0], lax.ppermute(query_parts[1], "head", swap)]
    else:
        swapped = lax.all_to_all(jnp.stack(kv_parts), "head", split_axis=0, concat_axis=0)
        kv_pieces = [swapped.reshape(shards * tokens, 2 * group_width)]
        query_parts = split(
            split_queries_kernel, place, queries, shards, width, [], "split_queries"
        )
        swapped = lax.all_to_all(jnp.stack(query_parts), "head", split_axis=0, concat_axis=0)
        query_pieces = [swapped.reshape(shards * tokens, width)]

    blocks = list(kv_pieces)
    for back in range(1, spans):
        upward = [(i, i + back) for i in range(spans - back)]
        blocks += [lax.ppermute(piece, "span", upward) for piece in kv_pieces]
    attended = attention(place, span_mask, counts, query_pieces, blocks, groups, sharing)

    columns = w_out.shape[1]
    if shards == 2:
        unit = columns // 12
        own_parts, other_parts = [], []
        first = 0
        for chunk, units in enumerate([1, 2, 3, 3, 3]):
            after = other_parts[chunk - 2 : chunk - 1] if chunk >= 2 else []
            own, other = project(attended, w_out, first, units * unit, unit, tokens, after)
            own_parts.append(own)
            other_parts.append(lax.ppermute(other, "head", swap))
            first += units * unit
    else:
        partial = jnp.dot(attended, w_out, preferred_element_type=jnp.float32)
        summed = lax.psum_scatter(
            partial.astype(jnp.bfloat16), "head", scatter_dimension=0, tiled=True
        )
        own_parts, other_parts = [jnp.zeros(summed.shape, jnp.float32)], [summed]
    return combine(place, levels, counts, gate_table, own_parts, other_parts)


def solution(mesh):
    in_specs = (
        P(("rep", "span", "head"), None),
        P(("rep", "span", "head"), None, None),
        P("head", None),
        P(),
        P("rep"),
        P("rep", None),
        P("rep"),
    )
    out_specs = P(("rep", "span", "head"), None)
    return jax.shard_map(local, mesh=mesh, in_specs=in_specs, out_specs=out_specs, check_vma=False)
```

```python
import functools
import math

import jax
import jax.numpy as jnp
from jax import lax
from jax.experimental import pallas as pl
from jax.experimental.pallas import tpu as pltpu
from jax.sharding import PartitionSpec as P

HEADS = 48
HD = 128
KV_GROUPS = 8

NEG_FILL = -1e30
EXP_SCALE = HD ** (-0.5) * math.log2(math.e)
VMEM_LIMIT = 14 * 1024 * 1024

FETCH_COPIES = 8

VMEM = pl.BlockSpec(memory_space=pltpu.VMEM)
SMEM = pl.BlockSpec(memory_space=pltpu.SMEM)
ANY = pl.BlockSpec(memory_space=pl.ANY)


def vmem_out(shape, dtype):
    return pltpu.VMEM(shape, dtype)


def in_vmem(array):
    return pltpu.with_memory_space_constraint(array, pltpu.VMEM)


def in_hbm(array):
    return pltpu.with_memory_space_constraint(array, pltpu.HBM)


def column_starts(place_ref, pieces, width):
    if pieces == 2:
        own = place_ref[1]
        return [pl.multiple_of(own * width, HD), pl.multiple_of((1 - own) * width, HD)]
    return [piece * width for piece in range(pieces)]


def split_kv(starts, group_width, kv_ref, out_refs):
    for start, out_ref in zip(starts, out_refs):
        first = out_ref.shape[1] - 2 * group_width
        out_ref[:, first : first + group_width] = kv_ref[:, 0, pl.ds(start, group_width)]
        out_ref[:, first + group_width :] = kv_ref[:, 1, pl.ds(start, group_width)]


def pair_kernel(width, group_width, place_ref, kv_hbm, query_hbm, *refs):
    own_kv_ref, sent_kv_ref, own_ref, sent_ref, kv_ref, query_ref, sems = refs
    get_kv = pltpu.make_async_copy(kv_hbm, kv_ref, sems.at[0])
    get_queries = pltpu.make_async_copy(query_hbm, query_ref, sems.at[1])
    get_kv.start()
    get_queries.start()
    get_kv.wait()
    split_kv(column_starts(place_ref, 2, group_width), group_width, kv_ref, [own_kv_ref, sent_kv_ref])
    sent_ref[:, width:] = sent_kv_ref[...]
    get_queries.wait()
    own_start, sent_start = column_starts(place_ref, 2, width)
    own_ref[...] = query_ref[:, pl.ds(own_start, width)]
    sent_ref[:, :width] = query_ref[:, pl.ds(sent_start, width)]


def split_pair(place, key_value, queries, width, group_width):
    rows = queries.shape[0]
    widths = [2 * group_width, 2 * group_width, width, width + 2 * group_width]
    return pl.pallas_call(
        functools.partial(pair_kernel, width, group_width),
        out_shape=[vmem_out((rows, w), queries.dtype) for w in widths],
        in_specs=[SMEM, ANY, ANY],
        out_specs=[VMEM] * 4,
        scratch_shapes=[
            pltpu.VMEM(key_value.shape, key_value.dtype),
            pltpu.VMEM(queries.shape, queries.dtype),
            pltpu.SemaphoreType.DMA((2,)),
        ],
        compiler_params=pltpu.CompilerParams(vmem_limit_bytes=VMEM_LIMIT),
        cost_estimate=pl.CostEstimate(
            flops=0, bytes_accessed=4 * (queries.size + key_value.size), transcendentals=0
        ),
        name="split_pair",
    )(place, in_hbm(key_value), in_hbm(queries))


def all_kernel(group_width, copies, kv_ref, *out_refs):
    starts = [piece // copies * group_width for piece in range(len(out_refs))]
    split_kv(starts, group_width, kv_ref, out_refs)


def split_all(key_value, pieces, group_width, copies):
    shape = jax.ShapeDtypeStruct((key_value.shape[0], 2 * group_width), key_value.dtype)
    return pl.pallas_call(
        functools.partial(all_kernel, group_width, copies),
        out_shape=[shape] * pieces,
        in_specs=[VMEM],
        out_specs=[VMEM] * pieces,
        compiler_params=pltpu.CompilerParams(vmem_limit_bytes=VMEM_LIMIT),
        name="split_all",
    )(key_value)


def fetch_copies(weight_hbm, first, out_refs, sems):
    parts = FETCH_COPIES
    copies = []
    for k, out_ref in enumerate(out_refs):
        depth, count = out_ref.shape
        rows = depth // parts
        for i in range(parts):
            part = pl.ds(i * rows, rows)
            copies.append(
                pltpu.make_async_copy(
                    weight_hbm.at[part, pl.ds(first, count)],
                    out_ref.at[part, :],
                    sems.at[k * parts + i],
                )
            )
        first += count
    return copies


def fetch_kernel(n_after, info_ref, gate_ref, weight_hbm, *refs):
    gate_row_ref, *out_refs, sems = refs[n_after:]
    pending = fetch_copies(weight_hbm, 0, out_refs, sems)
    for copy in pending:
        copy.start()
    level = info_ref[2 + info_ref[0]]
    chosen = lax.broadcasted_iota(jnp.int32, (gate_ref.shape[0], 1), 0) == level
    gate = jnp.where(chosen, gate_ref[...].astype(jnp.float32), 0.0)
    gate_row_ref[...] = jnp.sum(gate, axis=0, keepdims=True)
    for copy in pending:
        copy.wait()


def fetch(info, gate_table, w_out, counts, after):
    depth = w_out.shape[0]
    return pl.pallas_call(
        functools.partial(fetch_kernel, len(after)),
        out_shape=[
            vmem_out((1, gate_table.shape[1]), jnp.float32),
            *[vmem_out((depth, count), w_out.dtype) for count in counts],
        ],
        in_specs=[SMEM, VMEM] + [ANY] * (1 + len(after)),
        out_specs=[VMEM] * (1 + len(counts)),
        scratch_shapes=[pltpu.SemaphoreType.DMA((max(1, FETCH_COPIES * len(counts)),))],
        compiler_params=pltpu.CompilerParams(vmem_limit_bytes=VMEM_LIMIT),
        cost_estimate=pl.CostEstimate(
            flops=0, bytes_accessed=4 * depth * sum(counts), transcendentals=0
        ),
        name="fetch",
    )(info, gate_table, in_hbm(w_out), *after)


def softmax_block(query, keys, values, usable):
    scores = lax.dot_general(
        query, keys, (((1,), (1,)), ((), ())), preferred_element_type=jnp.float32
    )
    scores = jnp.where(usable, scores, NEG_FILL)
    highest = jnp.max(scores, axis=1, keepdims=True)
    weights = jnp.exp2((scores - highest) * EXP_SCALE)
    totals = jnp.sum(weights, axis=1, keepdims=True)
    summed = jnp.dot(weights.astype(jnp.bfloat16), values, preferred_element_type=jnp.float32)
    return summed / totals


def usable_row(spans, info_ref, piece_rows, piece_count):
    own_span, own_shard = info_ref[0], info_ref[1]
    row = []
    for back in range(spans):
        source = jnp.maximum(own_span - back, 0)
        allowed = (info_ref[2 + 2 * spans + own_span * spans + source] > 0) & (own_span >= back)
        limit = jnp.where(allowed, info_ref[2 + spans + source], 0)
        for piece in range(piece_count):
            first = 0
            if piece_count == 2:
                first = (own_shard if piece == 0 else 1 - own_shard) * piece_rows
            positions = first + lax.broadcasted_iota(jnp.int32, (1, piece_rows), 1)
            row.append((positions < limit).astype(jnp.int32))
    return jnp.concatenate(row, axis=1) > 0


def attend(usable, groups, sharing, row_tile, query_refs, kv_refs, out_ref):
    group_width = groups * HD
    span = sharing * HD
    key_firsts = [r.shape[1] - 2 * group_width for r in kv_refs]
    value_firsts = [r.shape[1] - group_width for r in kv_refs]
    for g in range(groups):
        keys = jnp.concatenate(
            [r[:, a + g * HD : a + (g + 1) * HD] for r, a in zip(kv_refs, key_firsts)], axis=0
        )
        values = jnp.concatenate(
            [r[:, a + g * HD : a + (g + 1) * HD] for r, a in zip(kv_refs, value_firsts)], axis=0
        )
        done = 0
        for query_ref in query_refs:
            rows = query_ref.shape[0]
            for first in range(0, rows, row_tile):
                tile = min(row_tile, rows - first)
                query = jnp.concatenate(
                    [
                        query_ref[first : first + tile, g * span + h * HD : g * span + (h + 1) * HD]
                        for h in range(sharing)
                    ],
                    axis=0,
                )
                result = softmax_block(query, keys, values, usable).astype(jnp.bfloat16)
                for h in range(sharing):
                    out_ref[
                        done + first : done + first + tile,
                        g * span + h * HD : g * span + (h + 1) * HD,
                    ] = result[h * tile : (h + 1) * tile]
            done += rows


def attention_kernel(
    n_query, n_kv, n_after, spans, groups, sharing, row_tile, fetch_first, info_ref, *refs
):
    query_refs, kv_refs = refs[:n_query], refs[n_query : n_query + n_kv]
    rest = refs[n_query + n_kv + n_after :]
    pending = []
    if fetch_first is None:
        (out_ref,) = rest
    else:
        weight_hbm, out_ref, weight_ref, sems = rest
        pending = fetch_copies(weight_hbm, fetch_first, [weight_ref], sems)
    for copy in pending:
        copy.start()
    usable = usable_row(spans, info_ref, kv_refs[0].shape[0], n_query)
    attend(usable, groups, sharing, row_tile, query_refs, kv_refs, out_ref)
    for copy in pending:
        copy.wait()


def attention(info, spans, query_pieces, kv_pieces, groups, sharing, after, w_out, fetch_first):
    rows = sum(p.shape[0] for p in query_pieces)
    keys = sum(p.shape[0] for p in kv_pieces)
    width = groups * sharing * HD
    row_tile = 64
    scores_bytes = 4 * sharing * row_tile * keys
    out_shape = [jax.ShapeDtypeStruct((rows, width), jnp.bfloat16)]
    operands = [*query_pieces, *kv_pieces]
    in_specs = [SMEM] + [VMEM] * (len(operands) + len(after))
    operands += after
    scratch = []
    if fetch_first is not None:
        depth, columns = w_out.shape
        out_shape.append(vmem_out((depth, columns - fetch_first), w_out.dtype))
        in_specs.append(ANY)
        operands.append(in_hbm(w_out))
        scratch.append(pltpu.SemaphoreType.DMA((FETCH_COPIES,)))
    return pl.pallas_call(
        functools.partial(
            attention_kernel,
            len(query_pieces),
            len(kv_pieces),
            len(after),
            spans,
            groups,
            sharing,
            row_tile,
            fetch_first,
        ),
        out_shape=out_shape,
        in_specs=in_specs,
        out_specs=[VMEM] * len(out_shape),
        scratch_shapes=scratch,
        compiler_params=pltpu.CompilerParams(
            vmem_limit_bytes=max(VMEM_LIMIT, 12 * scores_bytes)
        ),
        cost_estimate=pl.CostEstimate(
            flops=4 * rows * width * keys,
            bytes_accessed=4 * rows * width + 4 * groups * HD * keys,
            transcendentals=rows * keys * groups * sharing,
        ),
        name="attention",
    )(info, *operands)


def project_kernel(own_rows, tile, attended_ref, weight_ref, *refs):
    own_ref, other_ref = refs[-2:]
    attended = attended_ref[...]
    for first in range(0, weight_ref.shape[1], tile):
        columns = slice(first, first + tile)
        product = jnp.dot(attended, weight_ref[:, columns], preferred_element_type=jnp.float32)
        own_ref[:, columns] = product[:own_rows]
        other_ref[:, columns] = product[own_rows:].astype(jnp.bfloat16)


def project(attended, weights, own_rows, after):
    rows, depth = attended.shape
    count = weights.shape[1]
    other_rows = rows - own_rows
    return pl.pallas_call(
        functools.partial(project_kernel, own_rows, 512),
        out_shape=[
            jax.ShapeDtypeStruct((own_rows, count), jnp.float32),
            jax.ShapeDtypeStruct((other_rows, count), jnp.bfloat16),
        ],
        in_specs=[VMEM, VMEM] + [ANY] * len(after),
        out_specs=[VMEM, VMEM],
        compiler_params=pltpu.CompilerParams(vmem_limit_bytes=VMEM_LIMIT),
        cost_estimate=pl.CostEstimate(
            flops=2 * rows * depth * count, bytes_accessed=2 * depth * count, transcendentals=0
        ),
        name="project",
    )(attended, in_vmem(weights), *after)


def combine_kernel(n_chunks, spans, info_ref, gate_ref, *refs):
    own_refs, other_refs, out_ref = refs[:n_chunks], refs[n_chunks : 2 * n_chunks], refs[-1]
    rows = out_ref.shape[0]
    own_span, own_shard = info_ref[0], info_ref[1]
    positions = own_shard * rows + lax.broadcasted_iota(jnp.int32, (rows, 1), 0)
    live = positions < info_ref[2 + spans + own_span]
    first = 0
    for own_ref, other_ref in zip(own_refs, other_refs):
        columns = slice(first, first + own_ref.shape[1])
        gated = (own_ref[...] + other_ref[...].astype(jnp.float32)) * gate_ref[:, columns]
        out_ref[:, columns] = jnp.where(live, gated, 0.0).astype(jnp.bfloat16)
        first += own_ref.shape[1]


def combine(info, spans, gate_row, own_parts, other_parts):
    rows = own_parts[0].shape[0]
    width = sum(p.shape[1] for p in own_parts)
    return pl.pallas_call(
        functools.partial(combine_kernel, len(own_parts), spans),
        out_shape=jax.ShapeDtypeStruct((rows, width), jnp.bfloat16),
        in_specs=[SMEM] + [VMEM] * (1 + 2 * len(own_parts)),
        out_specs=VMEM,
        compiler_params=pltpu.CompilerParams(vmem_limit_bytes=VMEM_LIMIT),
        cost_estimate=pl.CostEstimate(
            flops=2 * rows * width, bytes_accessed=8 * rows * width, transcendentals=0
        ),
        name="combine",
    )(info, gate_row, *own_parts, *other_parts)


def local(queries, key_value, w_out, gate_table, levels, span_mask, counts):
    tokens = queries.shape[0]
    shards = lax.axis_size("head")
    spans = lax.axis_size("span")
    place = jnp.stack([lax.axis_index("span"), lax.axis_index("head")]).astype(jnp.int32)
    info = jnp.concatenate([place, levels, counts, span_mask.reshape(-1)])
    head_count = HEADS // shards
    share = HEADS // KV_GROUPS
    sharing = min(share, head_count)
    copies = max(1, share // head_count)
    groups = head_count // sharing
    group_width = groups * HD
    width = head_count * HD
    columns = w_out.shape[1]

    if shards == 2:
        own_kv, sent_kv, own_queries, sent = split_pair(
            place, key_value, queries, width, group_width
        )
        received = lax.ppermute(sent, "head", [(0, 1), (1, 0)])
        blocks = [own_kv, received]
        for back in range(1, spans):
            for piece, other in ((own_kv, 0), (sent_kv, 1)):
                pairs = [
                    (i * 2 + j, (i + back) * 2 + (j ^ other))
                    for i in range(spans - back)
                    for j in range(2)
                ]
                blocks.append(lax.ppermute(piece, ("span", "head"), pairs))
        chunks = [units * columns // 12 for units in (1, 2, 3, 3, 3)]
        gate_row, *weights = fetch(info, gate_table, w_out, chunks[:-1], [own_kv, sent])
        attended, last_weights = attention(
            info,
            spans,
            [own_queries, received],
            blocks,
            groups,
            sharing,
            [gate_row],
            w_out,
            columns - chunks[-1],
        )
        own_parts, other_parts = [], []
        for chunk, chunk_weights in enumerate([*weights, last_weights]):
            after = other_parts[chunk - 2 : chunk - 1] if chunk >= 2 else []
            own, other = project(attended, chunk_weights, tokens, after)
            own_parts.append(own)
            other_parts.append(lax.ppermute(other, "head", [(0, 1), (1, 0)]))
    else:
        kv_parts = split_all(key_value, shards, group_width, copies)
        swapped = lax.all_to_all(jnp.stack(kv_parts), "head", split_axis=0, concat_axis=0)
        kv_piece = swapped.reshape(shards * tokens, 2 * group_width)
        by_shard = queries.reshape(tokens, shards, width).transpose(1, 0, 2)
        swapped = lax.all_to_all(by_shard, "head", split_axis=0, concat_axis=0)
        query_piece = swapped.reshape(shards * tokens, width)
        blocks = [kv_piece]
        for back in range(1, spans):
            upward = [(i, i + back) for i in range(spans - back)]
            blocks.append(lax.ppermute(kv_piece, "span", upward))
        (gate_row,) = fetch(info, gate_table, w_out, [], [])
        (attended,) = attention(
            info, spans, [query_piece], blocks, groups, sharing, [], w_out, None
        )
        partial = jnp.dot(attended, w_out, preferred_element_type=jnp.float32)
        summed = lax.psum_scatter(
            partial.astype(jnp.bfloat16), "head", scatter_dimension=0, tiled=True
        )
        own_parts, other_parts = [jnp.zeros(summed.shape, jnp.float32)], [summed]
    return combine(info, spans, gate_row, own_parts, other_parts)


def solution(mesh):
    in_specs = (
        P(("rep", "span", "head"), None),
        P(("rep", "span", "head"), None, None),
        P("head", None),
        P(),
        P("rep"),
        P("rep", None),
        P("rep"),
    )
    out_specs = P(("rep", "span", "head"), None)
    return jax.shard_map(local, mesh=mesh, in_specs=in_specs, out_specs=out_specs, check_vma=False)
```

```python
import functools
import math

import jax
import jax.numpy as jnp
from jax import lax
from jax.experimental import pallas as pl
from jax.experimental.pallas import tpu as pltpu
from jax.sharding import PartitionSpec as P

HEADS = 48
HD = 128
KV_GROUPS = 8

NEG_FILL = -1e30
EXP_SCALE = HD ** (-0.5) * math.log2(math.e)
VMEM_LIMIT = 8 * 1024 * 1024

FETCH_COPIES = 8

VMEM = pl.BlockSpec(memory_space=pltpu.VMEM)
SMEM = pl.BlockSpec(memory_space=pltpu.SMEM)
ANY = pl.BlockSpec(memory_space=pl.ANY)


def vmem_out(shape, dtype):
    return pltpu.VMEM(shape, dtype)


def in_vmem(array):
    return pltpu.with_memory_space_constraint(array, pltpu.VMEM)


def in_hbm(array):
    return pltpu.with_memory_space_constraint(array, pltpu.HBM)


def column_starts(place_ref, pieces, width):
    if pieces == 2:
        own = place_ref[1]
        return [pl.multiple_of(own * width, HD), pl.multiple_of((1 - own) * width, HD)]
    return [piece * width for piece in range(pieces)]


def split_kv(starts, group_width, kv_ref, out_refs):
    for start, out_ref in zip(starts, out_refs):
        first = out_ref.shape[1] - 2 * group_width
        out_ref[:, first : first + group_width] = kv_ref[:, 0, pl.ds(start, group_width)]
        out_ref[:, first + group_width :] = kv_ref[:, 1, pl.ds(start, group_width)]


def pair_kernel(spans, width, group_width, place_ref, kv_hbm, query_hbm, *refs):
    all_kv_ref, own_ref, sent_ref, kv_ref, query_ref, sems = refs
    rows = kv_ref.shape[0]
    get_kv = pltpu.make_async_copy(kv_hbm, kv_ref, sems.at[0])
    get_queries = pltpu.make_async_copy(query_hbm, query_ref, sems.at[1])
    get_kv.start()
    get_queries.start()
    get_kv.wait()
    for shard in range(2):
        columns = slice(shard * group_width, (shard + 1) * group_width)
        for half in range(2):
            piece = kv_ref[:, half, columns]
            for span in range(spans):
                first = (span * 2 + shard) * rows
                all_kv_ref[
                    first : first + rows, half * group_width : (half + 1) * group_width
                ] = piece
    get_queries.wait()
    own_start, sent_start = column_starts(place_ref, 2, width)
    own_ref[...] = query_ref[:, pl.ds(own_start, width)]
    sent_ref[...] = query_ref[:, pl.ds(sent_start, width)]


def split_pair(place, spans, key_value, queries, width, group_width):
    rows = queries.shape[0]
    return pl.pallas_call(
        functools.partial(pair_kernel, spans, width, group_width),
        out_shape=[
            vmem_out((2 * spans * rows, 2 * group_width), queries.dtype),
            vmem_out((rows, width), queries.dtype),
            vmem_out((rows, width), queries.dtype),
        ],
        in_specs=[SMEM, ANY, ANY],
        out_specs=[VMEM] * 3,
        scratch_shapes=[
            pltpu.VMEM(key_value.shape, key_value.dtype),
            pltpu.VMEM(queries.shape, queries.dtype),
            pltpu.SemaphoreType.DMA((2,)),
        ],
        compiler_params=pltpu.CompilerParams(vmem_limit_bytes=VMEM_LIMIT),
        cost_estimate=pl.CostEstimate(
            flops=0, bytes_accessed=4 * (queries.size + key_value.size), transcendentals=0
        ),
        name="split_pair",
    )(place, in_hbm(key_value), in_hbm(queries))


def all_kernel(group_width, copies, kv_ref, *out_refs):
    starts = [piece // copies * group_width for piece in range(len(out_refs))]
    split_kv(starts, group_width, kv_ref, out_refs)


def split_all(key_value, pieces, group_width, copies):
    shape = jax.ShapeDtypeStruct((key_value.shape[0], 2 * group_width), key_value.dtype)
    return pl.pallas_call(
        functools.partial(all_kernel, group_width, copies),
        out_shape=[shape] * pieces,
        in_specs=[VMEM],
        out_specs=[VMEM] * pieces,
        compiler_params=pltpu.CompilerParams(vmem_limit_bytes=VMEM_LIMIT),
        name="split_all",
    )(key_value)


def fetch_copies(weight_hbm, first, out_refs, sems):
    parts = FETCH_COPIES
    copies = []
    for k, out_ref in enumerate(out_refs):
        depth, count = out_ref.shape
        rows = depth // parts
        for i in range(parts):
            part = pl.ds(i * rows, rows)
            copies.append(
                pltpu.make_async_copy(
                    weight_hbm.at[part, pl.ds(first, count)],
                    out_ref.at[part, :],
                    sems.at[k * parts + i],
                )
            )
        first += count
    return copies


def late_fetch_kernel(first, weight_hbm, after_ref, out_ref, sems):
    pending = fetch_copies(weight_hbm, first, [out_ref], sems)
    for copy in pending:
        copy.start()
    for copy in pending:
        copy.wait()


def late_fetch(w_out, first, after):
    depth, columns = w_out.shape
    return pl.pallas_call(
        functools.partial(late_fetch_kernel, first),
        out_shape=vmem_out((depth, columns - first), w_out.dtype),
        in_specs=[ANY, ANY],
        out_specs=VMEM,
        scratch_shapes=[pltpu.SemaphoreType.DMA((FETCH_COPIES,))],
        compiler_params=pltpu.CompilerParams(vmem_limit_bytes=VMEM_LIMIT),
        cost_estimate=pl.CostEstimate(
            flops=0, bytes_accessed=4 * depth * (columns - first), transcendentals=0
        ),
        name="late_fetch",
    )(in_hbm(w_out), after)


def fetch_kernel(n_after, info_ref, gate_ref, weight_hbm, *refs):
    gate_row_ref, *out_refs, sems = refs[n_after:]
    pending = fetch_copies(weight_hbm, 0, out_refs, sems)
    for copy in pending:
        copy.start()
    level = info_ref[2 + info_ref[0]]
    chosen = lax.broadcasted_iota(jnp.int32, (gate_ref.shape[0], 1), 0) == level
    gate = jnp.where(chosen, gate_ref[...].astype(jnp.float32), 0.0)
    gate_row_ref[...] = jnp.sum(gate, axis=0, keepdims=True)
    for copy in pending:
        copy.wait()


def fetch(info, gate_table, w_out, counts, after):
    depth = w_out.shape[0]
    return pl.pallas_call(
        functools.partial(fetch_kernel, len(after)),
        out_shape=[
            vmem_out((1, gate_table.shape[1]), jnp.float32),
            *[vmem_out((depth, count), w_out.dtype) for count in counts],
        ],
        in_specs=[SMEM, VMEM] + [ANY] * (1 + len(after)),
        out_specs=[VMEM] * (1 + len(counts)),
        scratch_shapes=[pltpu.SemaphoreType.DMA((max(1, FETCH_COPIES * len(counts)),))],
        compiler_params=pltpu.CompilerParams(vmem_limit_bytes=VMEM_LIMIT),
        cost_estimate=pl.CostEstimate(
            flops=0, bytes_accessed=4 * depth * sum(counts), transcendentals=0
        ),
        name="fetch",
    )(info, gate_table, in_hbm(w_out), *after)


def softmax_block(query, keys, values, usable):
    scores = lax.dot_general(
        query, keys, (((1,), (1,)), ((), ())), preferred_element_type=jnp.float32
    )
    scores = jnp.where(usable, scores, NEG_FILL)
    highest = jnp.max(scores, axis=1, keepdims=True)
    weights = jnp.exp2((scores - highest) * EXP_SCALE)
    totals = jnp.sum(weights, axis=1, keepdims=True)
    summed = jnp.dot(weights.astype(jnp.bfloat16), values, preferred_element_type=jnp.float32)
    return summed / totals


def usable_row(spans, info_ref, span_rows, backward):
    own_span = info_ref[0]
    positions = lax.broadcasted_iota(jnp.int32, (1, span_rows), 1)
    row = []
    for i in range(spans):
        source = jnp.maximum(own_span - i, 0) if backward else i
        allowed = info_ref[2 + 2 * spans + own_span * spans + source] > 0
        if backward:
            allowed &= own_span >= i
        limit = jnp.where(allowed, info_ref[2 + spans + source], 0)
        row.append((positions < limit).astype(jnp.int32))
    return jnp.concatenate(row, axis=1) > 0


def attend(usable, groups, sharing, row_tile, query_refs, kv_refs, out_ref):
    group_width = groups * HD
    span = sharing * HD
    key_firsts = [r.shape[1] - 2 * group_width for r in kv_refs]
    value_firsts = [r.shape[1] - group_width for r in kv_refs]
    for g in range(groups):
        keys = jnp.concatenate(
            [r[:, a + g * HD : a + (g + 1) * HD] for r, a in zip(kv_refs, key_firsts)], axis=0
        )
        values = jnp.concatenate(
            [r[:, a + g * HD : a + (g + 1) * HD] for r, a in zip(kv_refs, value_firsts)], axis=0
        )
        done = 0
        for query_ref in query_refs:
            rows = query_ref.shape[0]
            for first in range(0, rows, row_tile):
                tile = min(row_tile, rows - first)
                query = jnp.concatenate(
                    [
                        query_ref[first : first + tile, g * span + h * HD : g * span + (h + 1) * HD]
                        for h in range(sharing)
                    ],
                    axis=0,
                )
                result = softmax_block(query, keys, values, usable).astype(jnp.bfloat16)
                for h in range(sharing):
                    out_ref[
                        done + first : done + first + tile,
                        g * span + h * HD : g * span + (h + 1) * HD,
                    ] = result[h * tile : (h + 1) * tile]
            done += rows


def attention_kernel(n_query, n_kv, spans, groups, sharing, row_tile, info_ref, *refs):
    query_refs, kv_refs, out_ref = refs[:n_query], refs[n_query : n_query + n_kv], refs[-1]
    span_rows = sum(r.shape[0] for r in kv_refs) // spans
    usable = usable_row(spans, info_ref, span_rows, n_kv == spans)
    attend(usable, groups, sharing, row_tile, query_refs, kv_refs, out_ref)


def attention(info, spans, query_pieces, kv_pieces, groups, sharing, after):
    rows = sum(p.shape[0] for p in query_pieces)
    keys = sum(p.shape[0] for p in kv_pieces)
    width = groups * sharing * HD
    row_tile = 64
    scores_bytes = 4 * sharing * row_tile * keys
    operands = [*query_pieces, *kv_pieces, *after]
    return pl.pallas_call(
        functools.partial(
            attention_kernel,
            len(query_pieces),
            len(kv_pieces),
            spans,
            groups,
            sharing,
            row_tile,
        ),
        out_shape=jax.ShapeDtypeStruct((rows, width), jnp.bfloat16),
        in_specs=[SMEM] + [VMEM] * len(operands),
        out_specs=VMEM,
        compiler_params=pltpu.CompilerParams(
            vmem_limit_bytes=max(VMEM_LIMIT, 12 * scores_bytes)
        ),
        cost_estimate=pl.CostEstimate(
            flops=4 * rows * width * keys,
            bytes_accessed=4 * rows * width + 4 * groups * HD * keys,
            transcendentals=rows * keys * groups * sharing,
        ),
        name="attention",
    )(info, *operands)


def project_kernel(own_rows, tile, attended_ref, weight_ref, *refs):
    own_ref, other_ref = refs[-2:]
    attended = attended_ref[...]
    for first in range(0, weight_ref.shape[1], tile):
        columns = slice(first, first + tile)
        product = jnp.dot(attended, weight_ref[:, columns], preferred_element_type=jnp.float32)
        own_ref[:, columns] = product[:own_rows]
        other_ref[:, columns] = product[own_rows:].astype(jnp.bfloat16)


def project(attended, weights, own_rows, after):
    rows, depth = attended.shape
    count = weights.shape[1]
    other_rows = rows - own_rows
    return pl.pallas_call(
        functools.partial(project_kernel, own_rows, 512),
        out_shape=[
            jax.ShapeDtypeStruct((own_rows, count), jnp.float32),
            jax.ShapeDtypeStruct((other_rows, count), jnp.bfloat16),
        ],
        in_specs=[VMEM, VMEM] + [ANY] * len(after),
        out_specs=[VMEM, VMEM],
        compiler_params=pltpu.CompilerParams(vmem_limit_bytes=VMEM_LIMIT),
        cost_estimate=pl.CostEstimate(
            flops=2 * rows * depth * count, bytes_accessed=2 * depth * count, transcendentals=0
        ),
        name="project",
    )(attended, in_vmem(weights), *after)


def combine_kernel(n_chunks, spans, info_ref, gate_ref, *refs):
    own_refs, other_refs, out_ref = refs[:n_chunks], refs[n_chunks : 2 * n_chunks], refs[-1]
    rows = out_ref.shape[0]
    own_span, own_shard = info_ref[0], info_ref[1]
    positions = own_shard * rows + lax.broadcasted_iota(jnp.int32, (rows, 1), 0)
    live = positions < info_ref[2 + spans + own_span]
    first = 0
    for own_ref, other_ref in zip(own_refs, other_refs):
        columns = slice(first, first + own_ref.shape[1])
        gated = (own_ref[...] + other_ref[...].astype(jnp.float32)) * gate_ref[:, columns]
        out_ref[:, columns] = jnp.where(live, gated, 0.0).astype(jnp.bfloat16)
        first += own_ref.shape[1]


def combine(info, spans, gate_row, own_parts, other_parts):
    rows = own_parts[0].shape[0]
    width = sum(p.shape[1] for p in own_parts)
    return pl.pallas_call(
        functools.partial(combine_kernel, len(own_parts), spans),
        out_shape=jax.ShapeDtypeStruct((rows, width), jnp.bfloat16),
        in_specs=[SMEM] + [VMEM] * (1 + 2 * len(own_parts)),
        out_specs=VMEM,
        compiler_params=pltpu.CompilerParams(vmem_limit_bytes=VMEM_LIMIT),
        cost_estimate=pl.CostEstimate(
            flops=2 * rows * width, bytes_accessed=8 * rows * width, transcendentals=0
        ),
        name="combine",
    )(info, gate_row, *own_parts, *other_parts)


def local(queries, key_value, w_out, gate_table, levels, span_mask, counts):
    tokens = queries.shape[0]
    shards = lax.axis_size("head")
    spans = lax.axis_size("span")
    place = jnp.stack([lax.axis_index("span"), lax.axis_index("head")]).astype(jnp.int32)
    info = jnp.concatenate([place, levels, counts, span_mask.reshape(-1)])
    head_count = HEADS // shards
    share = HEADS // KV_GROUPS
    sharing = min(share, head_count)
    copies = max(1, share // head_count)
    groups = head_count // sharing
    group_width = groups * HD
    width = head_count * HD
    columns = w_out.shape[1]

    if shards == 2:
        all_kv, own_queries, sent = split_pair(
            place, spans, key_value, queries, width, group_width
        )
        swap = [(0, 1), (1, 0)]
        blocks = lax.all_to_all(all_kv, ("span", "head"), split_axis=0, concat_axis=0, tiled=True)
        received = lax.ppermute(sent, "head", swap)
        chunks = [units * columns // 12 for units in (2, 3, 4, 3)]
        gate_row, *weights = fetch(info, gate_table, w_out, chunks[:-1], [sent])
        attended = attention(
            info, spans, [own_queries, received], [blocks], groups, sharing, [gate_row]
        )
        own_parts, other_parts = [], []
        for chunk in range(len(chunks)):
            if chunk == len(chunks) - 1:
                weights.append(late_fetch(w_out, columns - chunks[-1], other_parts[0]))
            after = other_parts[chunk - 2 : chunk - 1] if chunk >= 2 else []
            own, other = project(attended, weights[chunk], tokens, after)
            own_parts.append(own)
            other_parts.append(lax.ppermute(other, "head", swap))
    else:
        kv_parts = split_all(key_value, shards, group_width, copies)
        swapped = lax.all_to_all(jnp.stack(kv_parts), "head", split_axis=0, concat_axis=0)
        kv_piece = swapped.reshape(shards * tokens, 2 * group_width)
        by_shard = queries.reshape(tokens, shards, width).transpose(1, 0, 2)
        swapped = lax.all_to_all(by_shard, "head", split_axis=0, concat_axis=0)
        query_piece = swapped.reshape(shards * tokens, width)
        blocks = [kv_piece]
        for back in range(1, spans):
            upward = [(i, i + back) for i in range(spans - back)]
            blocks.append(lax.ppermute(kv_piece, "span", upward))
        (gate_row,) = fetch(info, gate_table, w_out, [], [])
        attended = attention(info, spans, [query_piece], blocks, groups, sharing, [])
        partial = jnp.dot(attended, w_out, preferred_element_type=jnp.float32)
        summed = lax.psum_scatter(
            partial.astype(jnp.bfloat16), "head", scatter_dimension=0, tiled=True
        )
        own_parts, other_parts = [jnp.zeros(summed.shape, jnp.float32)], [summed]
    return combine(info, spans, gate_row, own_parts, other_parts)


def solution(mesh):
    in_specs = (
        P(("rep", "span", "head"), None),
        P(("rep", "span", "head"), None, None),
        P("head", None),
        P(),
        P("rep"),
        P("rep", None),
        P("rep"),
    )
    out_specs = P(("rep", "span", "head"), None)
    return jax.shard_map(local, mesh=mesh, in_specs=in_specs, out_specs=out_specs, check_vma=False)
```

```python
import functools
import math

import jax
import jax.numpy as jnp
from jax import lax
from jax.experimental import pallas as pl
from jax.experimental.pallas import tpu as pltpu
from jax.sharding import PartitionSpec as P

HEADS = 48
HD = 128
KV_GROUPS = 8

NEG_FILL = -1e30
EXP_SCALE = HD ** (-0.5) * math.log2(math.e)
VMEM_LIMIT = 8 * 1024 * 1024

FETCH_COPIES = 8

VMEM = pl.BlockSpec(memory_space=pltpu.VMEM)
SMEM = pl.BlockSpec(memory_space=pltpu.SMEM)
ANY = pl.BlockSpec(memory_space=pl.ANY)


def vmem_out(shape, dtype):
    return pltpu.VMEM(shape, dtype)


def in_vmem(array):
    return pltpu.with_memory_space_constraint(array, pltpu.VMEM)


def in_hbm(array):
    return pltpu.with_memory_space_constraint(array, pltpu.HBM)


def column_starts(place_ref, pieces, width):
    if pieces == 2:
        own = place_ref[1]
        return [pl.multiple_of(own * width, HD), pl.multiple_of((1 - own) * width, HD)]
    return [piece * width for piece in range(pieces)]


def split_kv(starts, group_width, kv_ref, out_refs):
    for start, out_ref in zip(starts, out_refs):
        first = out_ref.shape[1] - 2 * group_width
        out_ref[:, first : first + group_width] = kv_ref[:, 0, pl.ds(start, group_width)]
        out_ref[:, first + group_width :] = kv_ref[:, 1, pl.ds(start, group_width)]


def pair_kv_kernel(group_width, place_ref, kv_hbm, own_ref, sent_ref, kv_ref, sem):
    get_kv = pltpu.make_async_copy(kv_hbm, kv_ref, sem)
    get_kv.start()
    get_kv.wait()
    starts = column_starts(place_ref, 2, group_width)
    split_kv([starts[1], starts[0]], group_width, kv_ref, [sent_ref, own_ref])


def pair_kv(place, key_value, group_width):
    shape = (key_value.shape[0], 2 * group_width)
    return pl.pallas_call(
        functools.partial(pair_kv_kernel, group_width),
        out_shape=[vmem_out(shape, key_value.dtype)] * 2,
        in_specs=[SMEM, ANY],
        out_specs=[VMEM] * 2,
        scratch_shapes=[
            pltpu.VMEM(key_value.shape, key_value.dtype),
            pltpu.SemaphoreType.DMA,
        ],
        compiler_params=pltpu.CompilerParams(vmem_limit_bytes=VMEM_LIMIT),
        cost_estimate=pl.CostEstimate(
            flops=0, bytes_accessed=4 * key_value.size, transcendentals=0
        ),
        name="pair_kv",
    )(place, in_hbm(key_value))


def pair_queries_kernel(width, place_ref, query_hbm, own_ref, sent_ref, sems):
    own_start, sent_start = column_starts(place_ref, 2, width)
    get_sent = pltpu.make_async_copy(
        query_hbm.at[:, pl.ds(sent_start, width)], sent_ref, sems.at[0]
    )
    get_own = pltpu.make_async_copy(query_hbm.at[:, pl.ds(own_start, width)], own_ref, sems.at[1])
    get_sent.start()
    get_own.start()
    get_sent.wait()
    get_own.wait()


def pair_queries(place, queries, width):
    shape = (queries.shape[0], width)
    return pl.pallas_call(
        functools.partial(pair_queries_kernel, width),
        out_shape=[vmem_out(shape, queries.dtype)] * 2,
        in_specs=[SMEM, ANY],
        out_specs=[VMEM] * 2,
        scratch_shapes=[pltpu.SemaphoreType.DMA((2,))],
        compiler_params=pltpu.CompilerParams(vmem_limit_bytes=VMEM_LIMIT),
        cost_estimate=pl.CostEstimate(
            flops=0, bytes_accessed=4 * queries.size, transcendentals=0
        ),
        name="pair_queries",
    )(place, in_hbm(queries))


def join_kernel(place_ref, own_ref, received_ref, out_ref):
    rows = own_ref.shape[0]
    own_first = pl.multiple_of(place_ref[1] * rows, rows)
    received_first = pl.multiple_of((1 - place_ref[1]) * rows, rows)
    out_ref[pl.ds(own_first, rows), :] = own_ref[...]
    out_ref[pl.ds(received_first, rows), :] = received_ref[...]


def join(place, own, received):
    rows, width = own.shape
    return pl.pallas_call(
        join_kernel,
        out_shape=vmem_out((2 * rows, width), own.dtype),
        in_specs=[SMEM, VMEM, VMEM],
        out_specs=VMEM,
        compiler_params=pltpu.CompilerParams(vmem_limit_bytes=VMEM_LIMIT),
        cost_estimate=pl.CostEstimate(flops=0, bytes_accessed=8 * own.size, transcendentals=0),
        name="join",
    )(place, own, received)


def all_kernel(group_width, copies, kv_ref, *out_refs):
    starts = [piece // copies * group_width for piece in range(len(out_refs))]
    split_kv(starts, group_width, kv_ref, out_refs)


def split_all(key_value, pieces, group_width, copies):
    shape = jax.ShapeDtypeStruct((key_value.shape[0], 2 * group_width), key_value.dtype)
    return pl.pallas_call(
        functools.partial(all_kernel, group_width, copies),
        out_shape=[shape] * pieces,
        in_specs=[VMEM],
        out_specs=[VMEM] * pieces,
        compiler_params=pltpu.CompilerParams(vmem_limit_bytes=VMEM_LIMIT),
        name="split_all",
    )(key_value)


def fetch_copies(weight_hbm, first, out_refs, sems):
    parts = FETCH_COPIES
    copies = []
    for k, out_ref in enumerate(out_refs):
        depth, count = out_ref.shape
        rows = depth // parts
        for i in range(parts):
            part = pl.ds(i * rows, rows)
            copies.append(
                pltpu.make_async_copy(
                    weight_hbm.at[part, pl.ds(first, count)],
                    out_ref.at[part, :],
                    sems.at[k * parts + i],
                )
            )
        first += count
    return copies


def late_fetch_kernel(first, weight_hbm, after_ref, out_ref, sems):
    pending = fetch_copies(weight_hbm, first, [out_ref], sems)
    for copy in pending:
        copy.start()
    for copy in pending:
        copy.wait()


def late_fetch(w_out, first, after):
    depth, columns = w_out.shape
    return pl.pallas_call(
        functools.partial(late_fetch_kernel, first),
        out_shape=vmem_out((depth, columns - first), w_out.dtype),
        in_specs=[ANY, ANY],
        out_specs=VMEM,
        scratch_shapes=[pltpu.SemaphoreType.DMA((FETCH_COPIES,))],
        compiler_params=pltpu.CompilerParams(vmem_limit_bytes=VMEM_LIMIT),
        cost_estimate=pl.CostEstimate(
            flops=0, bytes_accessed=4 * depth * (columns - first), transcendentals=0
        ),
        name="late_fetch",
    )(in_hbm(w_out), after)


def fetch_kernel(n_after, info_ref, gate_ref, weight_hbm, *refs):
    gate_row_ref, *out_refs, sems = refs[n_after:]
    pending = fetch_copies(weight_hbm, 0, out_refs, sems)
    for copy in pending:
        copy.start()
    level = info_ref[2 + info_ref[0]]
    chosen = lax.broadcasted_iota(jnp.int32, (gate_ref.shape[0], 1), 0) == level
    gate = jnp.where(chosen, gate_ref[...].astype(jnp.float32), 0.0)
    gate_row_ref[...] = jnp.sum(gate, axis=0, keepdims=True)
    for copy in pending:
        copy.wait()


def fetch(info, gate_table, w_out, counts, after):
    depth = w_out.shape[0]
    return pl.pallas_call(
        functools.partial(fetch_kernel, len(after)),
        out_shape=[
            vmem_out((1, gate_table.shape[1]), jnp.float32),
            *[vmem_out((depth, count), w_out.dtype) for count in counts],
        ],
        in_specs=[SMEM, VMEM] + [ANY] * (1 + len(after)),
        out_specs=[VMEM] * (1 + len(counts)),
        scratch_shapes=[pltpu.SemaphoreType.DMA((max(1, FETCH_COPIES * len(counts)),))],
        compiler_params=pltpu.CompilerParams(vmem_limit_bytes=VMEM_LIMIT),
        cost_estimate=pl.CostEstimate(
            flops=0, bytes_accessed=4 * depth * sum(counts), transcendentals=0
        ),
        name="fetch",
    )(info, gate_table, in_hbm(w_out), *after)


def softmax_block(query, keys, values, usable):
    scores = lax.dot_general(
        query, keys, (((1,), (1,)), ((), ())), preferred_element_type=jnp.float32
    )
    scores = jnp.where(usable, scores, NEG_FILL)
    highest = jnp.max(scores, axis=1, keepdims=True)
    weights = jnp.exp2((scores - highest) * EXP_SCALE)
    totals = jnp.sum(weights, axis=1, keepdims=True)
    summed = jnp.dot(weights.astype(jnp.bfloat16), values, preferred_element_type=jnp.float32)
    return summed / totals


def usable_row(spans, info_ref, span_rows):
    own_span = info_ref[0]
    positions = lax.broadcasted_iota(jnp.int32, (1, span_rows), 1)
    row = []
    for back in range(spans):
        source = jnp.maximum(own_span - back, 0)
        allowed = (info_ref[2 + 2 * spans + own_span * spans + source] > 0) & (own_span >= back)
        limit = jnp.where(allowed, info_ref[2 + spans + source], 0)
        row.append((positions < limit).astype(jnp.int32))
    return jnp.concatenate(row, axis=1) > 0


def attend(usable, groups, sharing, row_tile, query_refs, kv_refs, out_ref):
    group_width = groups * HD
    span = sharing * HD
    key_firsts = [r.shape[1] - 2 * group_width for r in kv_refs]
    value_firsts = [r.shape[1] - group_width for r in kv_refs]
    for g in range(groups):
        keys = jnp.concatenate(
            [r[:, a + g * HD : a + (g + 1) * HD] for r, a in zip(kv_refs, key_firsts)], axis=0
        )
        values = jnp.concatenate(
            [r[:, a + g * HD : a + (g + 1) * HD] for r, a in zip(kv_refs, value_firsts)], axis=0
        )
        done = 0
        for query_ref in query_refs:
            rows = query_ref.shape[0]
            for first in range(0, rows, row_tile):
                tile = min(row_tile, rows - first)
                query = jnp.concatenate(
                    [
                        query_ref[first : first + tile, g * span + h * HD : g * span + (h + 1) * HD]
                        for h in range(sharing)
                    ],
                    axis=0,
                )
                result = softmax_block(query, keys, values, usable).astype(jnp.bfloat16)
                for h in range(sharing):
                    out_ref[
                        done + first : done + first + tile,
                        g * span + h * HD : g * span + (h + 1) * HD,
                    ] = result[h * tile : (h + 1) * tile]
            done += rows


def attention_kernel(n_query, spans, groups, sharing, row_tile, info_ref, *refs):
    query_refs, kv_refs, out_ref = refs[:n_query], refs[n_query : n_query + spans], refs[-1]
    usable = usable_row(spans, info_ref, kv_refs[0].shape[0])
    attend(usable, groups, sharing, row_tile, query_refs, kv_refs, out_ref)


def attention(info, spans, query_pieces, kv_pieces, groups, sharing, after):
    rows = sum(p.shape[0] for p in query_pieces)
    keys = sum(p.shape[0] for p in kv_pieces)
    width = groups * sharing * HD
    row_tile = 64
    scores_bytes = 4 * sharing * row_tile * keys
    operands = [*query_pieces, *kv_pieces, *after]
    return pl.pallas_call(
        functools.partial(
            attention_kernel,
            len(query_pieces),
            spans,
            groups,
            sharing,
            row_tile,
        ),
        out_shape=jax.ShapeDtypeStruct((rows, width), jnp.bfloat16),
        in_specs=[SMEM] + [VMEM] * len(operands),
        out_specs=VMEM,
        compiler_params=pltpu.CompilerParams(
            vmem_limit_bytes=max(VMEM_LIMIT, 12 * scores_bytes)
        ),
        cost_estimate=pl.CostEstimate(
            flops=4 * rows * width * keys,
            bytes_accessed=4 * rows * width + 4 * groups * HD * keys,
            transcendentals=rows * keys * groups * sharing,
        ),
        name="attention",
    )(info, *operands)


def project_kernel(own_rows, tile, attended_ref, weight_ref, *refs):
    own_ref, other_ref = refs[-2:]
    attended = attended_ref[...]
    for first in range(0, weight_ref.shape[1], tile):
        columns = slice(first, first + tile)
        product = jnp.dot(attended, weight_ref[:, columns], preferred_element_type=jnp.float32)
        own_ref[:, columns] = product[:own_rows]
        other_ref[:, columns] = product[own_rows:].astype(jnp.bfloat16)


def project(attended, weights, own_rows, after):
    rows, depth = attended.shape
    count = weights.shape[1]
    other_rows = rows - own_rows
    return pl.pallas_call(
        functools.partial(project_kernel, own_rows, 512),
        out_shape=[
            jax.ShapeDtypeStruct((own_rows, count), jnp.float32),
            jax.ShapeDtypeStruct((other_rows, count), jnp.bfloat16),
        ],
        in_specs=[VMEM, VMEM] + [ANY] * len(after),
        out_specs=[VMEM, VMEM],
        compiler_params=pltpu.CompilerParams(vmem_limit_bytes=VMEM_LIMIT),
        cost_estimate=pl.CostEstimate(
            flops=2 * rows * depth * count, bytes_accessed=2 * depth * count, transcendentals=0
        ),
        name="project",
    )(attended, in_vmem(weights), *after)


def combine_kernel(n_chunks, spans, info_ref, gate_ref, *refs):
    own_refs, other_refs, out_ref = refs[:n_chunks], refs[n_chunks : 2 * n_chunks], refs[-1]
    rows = out_ref.shape[0]
    own_span, own_shard = info_ref[0], info_ref[1]
    positions = own_shard * rows + lax.broadcasted_iota(jnp.int32, (rows, 1), 0)
    live = positions < info_ref[2 + spans + own_span]
    first = 0
    for own_ref, other_ref in zip(own_refs, other_refs):
        columns = slice(first, first + own_ref.shape[1])
        gated = (own_ref[...] + other_ref[...].astype(jnp.float32)) * gate_ref[:, columns]
        out_ref[:, columns] = jnp.where(live, gated, 0.0).astype(jnp.bfloat16)
        first += own_ref.shape[1]


def combine(info, spans, gate_row, own_parts, other_parts):
    rows = own_parts[0].shape[0]
    width = sum(p.shape[1] for p in own_parts)
    return pl.pallas_call(
        functools.partial(combine_kernel, len(own_parts), spans),
        out_shape=jax.ShapeDtypeStruct((rows, width), jnp.bfloat16),
        in_specs=[SMEM] + [VMEM] * (1 + 2 * len(own_parts)),
        out_specs=VMEM,
        compiler_params=pltpu.CompilerParams(vmem_limit_bytes=VMEM_LIMIT),
        cost_estimate=pl.CostEstimate(
            flops=2 * rows * width, bytes_accessed=8 * rows * width, transcendentals=0
        ),
        name="combine",
    )(info, gate_row, *own_parts, *other_parts)


def upward_blocks(kv_piece, spans):
    blocks = [kv_piece]
    for back in range(1, spans):
        upward = [(i, i + back) for i in range(spans - back)]
        blocks.append(lax.ppermute(kv_piece, "span", upward))
    return blocks


def local(queries, key_value, w_out, gate_table, levels, span_mask, counts):
    tokens = queries.shape[0]
    shards = lax.axis_size("head")
    spans = lax.axis_size("span")
    place = jnp.stack([lax.axis_index("span"), lax.axis_index("head")]).astype(jnp.int32)
    info = jnp.concatenate([place, levels, counts, span_mask.reshape(-1)])
    head_count = HEADS // shards
    share = HEADS // KV_GROUPS
    sharing = min(share, head_count)
    copies = max(1, share // head_count)
    groups = head_count // sharing
    group_width = groups * HD
    width = head_count * HD
    columns = w_out.shape[1]

    if shards == 2:
        swap = [(0, 1), (1, 0)]
        own_kv, sent_kv = pair_kv(place, key_value, group_width)
        own_queries, sent_queries = pair_queries(place, queries, width)
        kv_piece = join(place, own_kv, lax.ppermute(sent_kv, "head", swap))
        received = lax.ppermute(sent_queries, "head", swap)
        blocks = upward_blocks(kv_piece, spans)
        chunks = [units * columns // 12 for units in (2, 3, 4, 3)]
        gate_row, *weights = fetch(info, gate_table, w_out, chunks[:-1], [kv_piece])
        attended = attention(
            info, spans, [own_queries, received], blocks, groups, sharing, [gate_row]
        )
        own_parts, other_parts = [], []
        for chunk in range(len(chunks)):
            if chunk == len(chunks) - 1:
                weights.append(late_fetch(w_out, columns - chunks[-1], other_parts[0]))
            after = other_parts[chunk - 2 : chunk - 1] if chunk >= 2 else []
            own, other = project(attended, weights[chunk], tokens, after)
            own_parts.append(own)
            other_parts.append(lax.ppermute(other, "head", swap))
    else:
        kv_parts = split_all(key_value, shards, group_width, copies)
        swapped = lax.all_to_all(jnp.stack(kv_parts), "head", split_axis=0, concat_axis=0)
        kv_piece = swapped.reshape(shards * tokens, 2 * group_width)
        by_shard = queries.reshape(tokens, shards, width).transpose(1, 0, 2)
        swapped = lax.all_to_all(by_shard, "head", split_axis=0, concat_axis=0)
        query_piece = swapped.reshape(shards * tokens, width)
        blocks = upward_blocks(kv_piece, spans)
        (gate_row,) = fetch(info, gate_table, w_out, [], [])
        attended = attention(info, spans, [query_piece], blocks, groups, sharing, [])
        partial = jnp.dot(attended, w_out, preferred_element_type=jnp.float32)
        summed = lax.psum_scatter(
            partial.astype(jnp.bfloat16), "head", scatter_dimension=0, tiled=True
        )
        own_parts, other_parts = [jnp.zeros(summed.shape, jnp.float32)], [summed]
    return combine(info, spans, gate_row, own_parts, other_parts)


def solution(mesh):
    in_specs = (
        P(("rep", "span", "head"), None),
        P(("rep", "span", "head"), None, None),
        P("head", None),
        P(),
        P("rep"),
        P("rep", None),
        P("rep"),
    )
    out_specs = P(("rep", "span", "head"), None)
    return jax.shard_map(local, mesh=mesh, in_specs=in_specs, out_specs=out_specs, check_vma=False)
```

```python
import functools
import math

import jax
import jax.numpy as jnp
from jax import lax
from jax.experimental import pallas as pl
from jax.experimental.pallas import tpu as pltpu
from jax.sharding import PartitionSpec as P

HEADS = 48
HD = 128
KV_GROUPS = 8

NEG_FILL = -1e30
EXP_SCALE = HD ** (-0.5) * math.log2(math.e)
VMEM_LIMIT = 8 * 1024 * 1024

FETCH_COPIES = 8
CHUNK_UNITS = (3, 5, 4)

VMEM = pl.BlockSpec(memory_space=pltpu.VMEM)
SMEM = pl.BlockSpec(memory_space=pltpu.SMEM)
ANY = pl.BlockSpec(memory_space=pl.ANY)


def vmem_out(shape, dtype):
    return pltpu.VMEM(shape, dtype)


def in_vmem(array):
    return pltpu.with_memory_space_constraint(array, pltpu.VMEM)


def in_hbm(array):
    return pltpu.with_memory_space_constraint(array, pltpu.HBM)


def column_starts(place_ref, pieces, width):
    if pieces == 2:
        own = place_ref[1]
        return [pl.multiple_of(own * width, HD), pl.multiple_of((1 - own) * width, HD)]
    return [piece * width for piece in range(pieces)]


def split_kv(starts, group_width, kv_ref, out_refs):
    for start, out_ref in zip(starts, out_refs):
        first = out_ref.shape[1] - 2 * group_width
        out_ref[:, first : first + group_width] = kv_ref[:, 0, pl.ds(start, group_width)]
        out_ref[:, first + group_width :] = kv_ref[:, 1, pl.ds(start, group_width)]


def pair_kernel(width, group_width, place_ref, kv_hbm, query_hbm, *refs):
    own_kv_ref, sent_kv_ref, own_ref, sent_ref, kv_ref, sems = refs
    own_start, sent_start = column_starts(place_ref, 2, width)
    get_kv = pltpu.make_async_copy(kv_hbm, kv_ref, sems.at[0])
    get_queries = [
        pltpu.make_async_copy(query_hbm.at[:, pl.ds(start, width)], ref, sems.at[i + 1])
        for i, (start, ref) in enumerate(((sent_start, sent_ref), (own_start, own_ref)))
    ]
    get_kv.start()
    for copy in get_queries:
        copy.start()
    get_kv.wait()
    starts = column_starts(place_ref, 2, group_width)
    split_kv(starts, group_width, kv_ref, [own_kv_ref, sent_kv_ref])
    for copy in get_queries:
        copy.wait()


def pair(place, key_value, queries, width, group_width):
    rows = queries.shape[0]
    widths = [2 * group_width, 2 * group_width, width, width]
    return pl.pallas_call(
        functools.partial(pair_kernel, width, group_width),
        out_shape=[vmem_out((rows, w), queries.dtype) for w in widths],
        in_specs=[SMEM, ANY, ANY],
        out_specs=[VMEM] * 4,
        scratch_shapes=[
            pltpu.VMEM(key_value.shape, key_value.dtype),
            pltpu.SemaphoreType.DMA((3,)),
        ],
        compiler_params=pltpu.CompilerParams(vmem_limit_bytes=VMEM_LIMIT),
        cost_estimate=pl.CostEstimate(
            flops=0, bytes_accessed=4 * (key_value.size + queries.size), transcendentals=0
        ),
        name="pair",
    )(place, in_hbm(key_value), in_hbm(queries))


def all_kernel(group_width, copies, kv_ref, *out_refs):
    starts = [piece // copies * group_width for piece in range(len(out_refs))]
    split_kv(starts, group_width, kv_ref, out_refs)


def split_all(key_value, pieces, group_width, copies):
    shape = jax.ShapeDtypeStruct((key_value.shape[0], 2 * group_width), key_value.dtype)
    return pl.pallas_call(
        functools.partial(all_kernel, group_width, copies),
        out_shape=[shape] * pieces,
        in_specs=[VMEM],
        out_specs=[VMEM] * pieces,
        compiler_params=pltpu.CompilerParams(vmem_limit_bytes=VMEM_LIMIT),
        name="split_all",
    )(key_value)


def fetch_copies(weight_hbm, first, out_refs, sems):
    parts = FETCH_COPIES
    copies = []
    for k, out_ref in enumerate(out_refs):
        depth, count = out_ref.shape
        rows = depth // parts
        for i in range(parts):
            part = pl.ds(i * rows, rows)
            copies.append(
                pltpu.make_async_copy(
                    weight_hbm.at[part, pl.ds(first, count)],
                    out_ref.at[part, :],
                    sems.at[k * parts + i],
                )
            )
        first += count
    return copies


def fetch_kernel(first, n_after, weight_hbm, *refs):
    out_ref, done_ref, sems = refs[n_after:]
    pending = fetch_copies(weight_hbm, first, [out_ref], sems)
    for copy in pending:
        copy.start()
    done_ref[...] = jnp.zeros_like(done_ref)
    for copy in pending:
        copy.wait()


def fetch(w_out, first, count, after):
    depth = w_out.shape[0]
    return pl.pallas_call(
        functools.partial(fetch_kernel, first, len(after)),
        out_shape=[vmem_out((depth, count), w_out.dtype), vmem_out((8, HD), jnp.int32)],
        in_specs=[ANY] * (1 + len(after)),
        out_specs=[VMEM] * 2,
        scratch_shapes=[pltpu.SemaphoreType.DMA((FETCH_COPIES,))],
        compiler_params=pltpu.CompilerParams(vmem_limit_bytes=VMEM_LIMIT),
        cost_estimate=pl.CostEstimate(
            flops=0, bytes_accessed=4 * depth * count, transcendentals=0
        ),
        name="fetch",
    )(in_hbm(w_out), *after)


def prepare_kernel(pieces, n_weights, n_after, place_ref, *refs):
    levels_hbm, mask_hbm, counts_hbm, gate_hbm, weight_hbm = refs[:5]
    usable_ref, live_ref, gate_row_ref, *weight_refs = refs[5 + n_after : 8 + n_after + n_weights]
    levels_ref, mask_ref, counts_ref, gate_ref, small_sems, sems = refs[8 + n_after + n_weights :]
    small = [
        pltpu.make_async_copy(levels_hbm, levels_ref, small_sems.at[0]),
        pltpu.make_async_copy(mask_hbm, mask_ref, small_sems.at[1]),
        pltpu.make_async_copy(counts_hbm, counts_ref, small_sems.at[2]),
    ]
    pending = fetch_copies(weight_hbm, 0, weight_refs, sems)
    for copy in small + pending:
        copy.start()
    for copy in small:
        copy.wait()
    own_span, own_shard = place_ref[0], place_ref[1]
    level = levels_ref[own_span]
    gate_rows = gate_ref.shape[0]
    first_row = pl.multiple_of(level // gate_rows * gate_rows, gate_rows)
    get_gate = pltpu.make_async_copy(
        gate_hbm.at[pl.ds(first_row, gate_rows), :], gate_ref, small_sems.at[3]
    )
    get_gate.start()

    spans = counts_ref.shape[0]
    piece_rows = usable_ref.shape[1] // (spans * pieces)
    ids = lax.broadcasted_iota(jnp.int32, (1, piece_rows), 1)
    for back in range(spans):
        source = jnp.maximum(own_span - back, 0)
        allowed = (mask_ref[own_span, source] > 0) & (own_span >= back)
        limit = jnp.where(allowed, counts_ref[source], 0)
        for piece in range(pieces):
            first = 0
            if pieces == 2:
                first = (own_shard if piece == 0 else 1 - own_shard) * piece_rows
            start = (back * pieces + piece) * piece_rows
            usable_ref[:, start : start + piece_rows] = (first + ids < limit).astype(jnp.int32)
    positions = own_shard * live_ref.shape[0] + lax.broadcasted_iota(jnp.int32, live_ref.shape, 0)
    live_ref[...] = (positions < counts_ref[own_span]).astype(jnp.int32)

    get_gate.wait()
    chosen = lax.broadcasted_iota(jnp.int32, (gate_rows, 1), 0) == level - first_row
    gate = jnp.where(chosen, gate_ref[...].astype(jnp.float32), 0.0)
    gate_row_ref[...] = jnp.sum(gate, axis=0, keepdims=True)
    for copy in pending:
        copy.wait()


def prepare(place, levels, span_mask, counts, gate_table, w_out, widths, keys, pieces, tokens, after):
    depth = w_out.shape[0]
    columns = gate_table.shape[1]
    gate_rows = 16
    return pl.pallas_call(
        functools.partial(prepare_kernel, pieces, len(widths), len(after)),
        out_shape=[
            vmem_out((1, keys), jnp.int32),
            vmem_out((tokens, HD), jnp.int32),
            vmem_out((1, columns), jnp.float32),
            *[vmem_out((depth, width), w_out.dtype) for width in widths],
        ],
        in_specs=[SMEM] + [ANY] * (5 + len(after)),
        out_specs=[VMEM] * (3 + len(widths)),
        scratch_shapes=[
            pltpu.SMEM(levels.shape, levels.dtype),
            pltpu.SMEM(span_mask.shape, span_mask.dtype),
            pltpu.SMEM(counts.shape, counts.dtype),
            pltpu.VMEM((gate_rows, columns), gate_table.dtype),
            pltpu.SemaphoreType.DMA((4,)),
            pltpu.SemaphoreType.DMA((max(1, FETCH_COPIES * len(widths)),)),
        ],
        compiler_params=pltpu.CompilerParams(vmem_limit_bytes=VMEM_LIMIT),
        cost_estimate=pl.CostEstimate(
            flops=0, bytes_accessed=4 * depth * sum(widths), transcendentals=0
        ),
        name="prepare",
    )(
        place,
        *[in_hbm(array) for array in (levels, span_mask, counts, gate_table, w_out)],
        *after,
    )


def softmax_block(query, keys, values, usable):
    scores = lax.dot_general(
        query, keys, (((1,), (1,)), ((), ())), preferred_element_type=jnp.float32
    )
    scores = jnp.where(usable, scores, NEG_FILL)
    highest = jnp.max(scores, axis=1, keepdims=True)
    weights = jnp.exp2((scores - highest) * EXP_SCALE)
    totals = jnp.sum(weights, axis=1, keepdims=True)
    summed = jnp.dot(weights.astype(jnp.bfloat16), values, preferred_element_type=jnp.float32)
    return summed / totals


def attend(usable, groups, sharing, row_tile, query_refs, kv_refs, out_ref):
    group_width = groups * HD
    span = sharing * HD
    key_firsts = [r.shape[1] - 2 * group_width for r in kv_refs]
    value_firsts = [r.shape[1] - group_width for r in kv_refs]
    for g in range(groups):
        keys = jnp.concatenate(
            [r[:, a + g * HD : a + (g + 1) * HD] for r, a in zip(kv_refs, key_firsts)], axis=0
        )
        values = jnp.concatenate(
            [r[:, a + g * HD : a + (g + 1) * HD] for r, a in zip(kv_refs, value_firsts)], axis=0
        )
        done = 0
        for query_ref in query_refs:
            rows = query_ref.shape[0]
            for first in range(0, rows, row_tile):
                tile = min(row_tile, rows - first)
                query = jnp.concatenate(
                    [
                        query_ref[first : first + tile, g * span + h * HD : g * span + (h + 1) * HD]
                        for h in range(sharing)
                    ],
                    axis=0,
                )
                result = softmax_block(query, keys, values, usable).astype(jnp.bfloat16)
                for h in range(sharing):
                    out_ref[
                        done + first : done + first + tile,
                        g * span + h * HD : g * span + (h + 1) * HD,
                    ] = result[h * tile : (h + 1) * tile]
            done += rows


def attention_kernel(n_query, n_kv, groups, sharing, row_tile, usable_ref, *refs):
    query_refs, kv_refs, out_ref = refs[:n_query], refs[n_query : n_query + n_kv], refs[-1]
    usable = usable_ref[...] > 0
    attend(usable, groups, sharing, row_tile, query_refs, kv_refs, out_ref)


def attention(usable, query_pieces, kv_pieces, groups, sharing, after):
    rows = sum(p.shape[0] for p in query_pieces)
    keys = usable.shape[1]
    width = groups * sharing * HD
    row_tile = 64
    scores_bytes = 4 * sharing * row_tile * keys
    operands = [usable, *query_pieces, *kv_pieces, *after]
    return pl.pallas_call(
        functools.partial(
            attention_kernel, len(query_pieces), len(kv_pieces), groups, sharing, row_tile
        ),
        out_shape=jax.ShapeDtypeStruct((rows, width), jnp.bfloat16),
        in_specs=[VMEM] * len(operands),
        out_specs=VMEM,
        compiler_params=pltpu.CompilerParams(
            vmem_limit_bytes=max(VMEM_LIMIT, 12 * scores_bytes)
        ),
        cost_estimate=pl.CostEstimate(
            flops=4 * rows * width * keys,
            bytes_accessed=4 * rows * width + 4 * groups * HD * keys,
            transcendentals=rows * keys * groups * sharing,
        ),
        name="attention",
    )(*operands)


def project_kernel(own_rows, tile, attended_ref, weight_ref, *refs):
    own_ref, other_ref = refs[-2:]
    attended = attended_ref[...]
    for first in range(0, weight_ref.shape[1], tile):
        columns = slice(first, first + tile)
        product = jnp.dot(attended, weight_ref[:, columns], preferred_element_type=jnp.float32)
        own_ref[:, columns] = product[:own_rows]
        other_ref[:, columns] = product[own_rows:].astype(jnp.bfloat16)


def project(attended, weights, own_rows, after):
    rows, depth = attended.shape
    count = weights.shape[1]
    other_rows = rows - own_rows
    return pl.pallas_call(
        functools.partial(project_kernel, own_rows, min(512, count)),
        out_shape=[
            jax.ShapeDtypeStruct((own_rows, count), jnp.float32),
            jax.ShapeDtypeStruct((other_rows, count), jnp.bfloat16),
        ],
        in_specs=[VMEM, VMEM] + [ANY] * len(after),
        out_specs=[VMEM, VMEM],
        compiler_params=pltpu.CompilerParams(vmem_limit_bytes=VMEM_LIMIT),
        cost_estimate=pl.CostEstimate(
            flops=2 * rows * depth * count, bytes_accessed=2 * depth * count, transcendentals=0
        ),
        name="project",
    )(attended, in_vmem(weights), *after)


def combine_kernel(n_chunks, live_ref, gate_ref, *refs):
    own_refs, other_refs, out_ref = refs[:n_chunks], refs[n_chunks : 2 * n_chunks], refs[-1]
    live = live_ref[:, :1] > 0
    first = 0
    for own_ref, other_ref in zip(own_refs, other_refs):
        columns = slice(first, first + own_ref.shape[1])
        gated = (own_ref[...] + other_ref[...].astype(jnp.float32)) * gate_ref[:, columns]
        out_ref[:, columns] = jnp.where(live, gated, 0.0).astype(jnp.bfloat16)
        first += own_ref.shape[1]


def combine(live, gate_row, own_parts, other_parts):
    rows = own_parts[0].shape[0]
    width = sum(p.shape[1] for p in own_parts)
    return pl.pallas_call(
        functools.partial(combine_kernel, len(own_parts)),
        out_shape=jax.ShapeDtypeStruct((rows, width), jnp.bfloat16),
        in_specs=[VMEM] * (2 + 2 * len(own_parts)),
        out_specs=VMEM,
        compiler_params=pltpu.CompilerParams(vmem_limit_bytes=VMEM_LIMIT),
        cost_estimate=pl.CostEstimate(
            flops=2 * rows * width, bytes_accessed=8 * rows * width, transcendentals=0
        ),
        name="combine",
    )(live, gate_row, *own_parts, *other_parts)


def relay(piece, spans):
    received = []
    for step in range(spans - 1):
        piece = lax.ppermute(piece, "span", [(i, i + 1) for i in range(step, spans - 1)])
        received.append(piece)
    return received


def local(queries, key_value, w_out, gate_table, levels, span_mask, counts):
    tokens = queries.shape[0]
    shards = lax.axis_size("head")
    spans = lax.axis_size("span")
    place = jnp.stack([lax.axis_index("span"), lax.axis_index("head")]).astype(jnp.int32)
    head_count = HEADS // shards
    share = HEADS // KV_GROUPS
    sharing = min(share, head_count)
    copies = max(1, share // head_count)
    groups = head_count // sharing
    group_width = groups * HD
    width = head_count * HD
    columns = w_out.shape[1]
    keys = spans * shards * tokens
    small = (place, levels, span_mask, counts, gate_table, w_out)

    if shards == 2:
        swap = [(0, 1), (1, 0)]
        own_kv, sent_kv, own_queries, sent_queries = pair(
            place, key_value, queries, width, group_width
        )
        other_kv = lax.ppermute(sent_kv, "head", swap)
        received = lax.ppermute(sent_queries, "head", swap)
        own_relay = relay(own_kv, spans)
        other_relay = relay(other_kv, spans)
        blocks = [own_kv, other_kv]
        for both in zip(own_relay, other_relay):
            blocks += both
        chunks = [units * columns // 12 for units in CHUNK_UNITS]
        firsts = [sum(chunks[:i]) for i in range(len(chunks))]
        usable, live, gate_row, *weights = prepare(
            *small, chunks[:1], keys, 2, tokens, [other_kv]
        )
        more, fetched = fetch(w_out, firsts[1], chunks[1], [live, own_relay[0]])
        weights.append(more)
        attended = attention(usable, [own_queries, received], blocks, groups, sharing, [fetched])
        own_parts, other_parts = [], []
        for chunk in range(len(chunks)):
            if chunk == len(chunks) - 1:
                more, _ = fetch(w_out, firsts[chunk], chunks[chunk], own_parts[1:2])
                weights.append(more)
            after = other_parts[chunk - 2 : chunk - 1] if chunk >= 2 else []
            own, other = project(attended, weights[chunk], tokens, after)
            own_parts.append(own)
            other_parts.append(lax.ppermute(other, "head", swap))
    else:
        kv_parts = split_all(key_value, shards, group_width, copies)
        swapped = lax.all_to_all(jnp.stack(kv_parts), "head", split_axis=0, concat_axis=0)
        kv_piece = swapped.reshape(shards * tokens, 2 * group_width)
        by_shard = queries.reshape(tokens, shards, width).transpose(1, 0, 2)
        swapped = lax.all_to_all(by_shard, "head", split_axis=0, concat_axis=0)
        query_piece = swapped.reshape(shards * tokens, width)
        blocks = [kv_piece]
        for back in range(1, spans):
            upward = [(i, i + back) for i in range(spans - back)]
            blocks.append(lax.ppermute(kv_piece, "span", upward))
        usable, live, gate_row = prepare(*small, [], keys, 1, tokens, [])
        attended = attention(usable, [query_piece], blocks, groups, sharing, [])
        partial = jnp.dot(attended, w_out, preferred_element_type=jnp.float32)
        summed = lax.psum_scatter(
            partial.astype(jnp.bfloat16), "head", scatter_dimension=0, tiled=True
        )
        own_parts, other_parts = [jnp.zeros(summed.shape, jnp.float32)], [summed]
    return combine(live, gate_row, own_parts, other_parts)


def solution(mesh):
    in_specs = (
        P(("rep", "span", "head"), None),
        P(("rep", "span", "head"), None, None),
        P("head", None),
        P(),
        P("rep"),
        P("rep", None),
        P("rep"),
    )
    out_specs = P(("rep", "span", "head"), None)
    return jax.shard_map(local, mesh=mesh, in_specs=in_specs, out_specs=out_specs, check_vma=False)
```

```python
import functools
import math

import jax
import jax.numpy as jnp
from jax import lax
from jax.experimental import pallas as pl
from jax.experimental.pallas import tpu as pltpu
from jax.sharding import PartitionSpec as P

HEADS = 48
HD = 128
KV_GROUPS = 8

NEG_FILL = -1e30
EXP_SCALE = HD ** (-0.5) * math.log2(math.e)
VMEM_LIMIT = 8 * 1024 * 1024

FETCH_COPIES = 8
FETCH_UNITS = ((2,), (1, 2), (3,), (4,))
CHUNK_PIECES = ((0, 2), (2, 4), (4, 5))

VMEM = pl.BlockSpec(memory_space=pltpu.VMEM)
SMEM = pl.BlockSpec(memory_space=pltpu.SMEM)
ANY = pl.BlockSpec(memory_space=pl.ANY)


def vmem_out(shape, dtype):
    return pltpu.VMEM(shape, dtype)


def in_vmem(array):
    return pltpu.with_memory_space_constraint(array, pltpu.VMEM)


def in_hbm(array):
    return pltpu.with_memory_space_constraint(array, pltpu.HBM)


def column_starts(place_ref, pieces, width):
    if pieces == 2:
        own = place_ref[1]
        return [pl.multiple_of(own * width, HD), pl.multiple_of((1 - own) * width, HD)]
    return [piece * width for piece in range(pieces)]


def split_kv(starts, group_width, kv_ref, out_refs):
    for start, out_ref in zip(starts, out_refs):
        first = out_ref.shape[1] - 2 * group_width
        out_ref[:, first : first + group_width] = kv_ref[:, 0, pl.ds(start, group_width)]
        out_ref[:, first + group_width :] = kv_ref[:, 1, pl.ds(start, group_width)]


def pair_kernel(width, group_width, place_ref, kv_hbm, query_hbm, *refs):
    own_kv_ref, sent_kv_ref, own_ref, sent_ref, kv_ref, sems = refs
    own_start, sent_start = column_starts(place_ref, 2, width)
    get_kv = pltpu.make_async_copy(kv_hbm, kv_ref, sems.at[0])
    get_queries = [
        pltpu.make_async_copy(query_hbm.at[:, pl.ds(start, width)], ref, sems.at[i + 1])
        for i, (start, ref) in enumerate(((sent_start, sent_ref), (own_start, own_ref)))
    ]
    get_kv.start()
    for copy in get_queries:
        copy.start()
    get_kv.wait()
    starts = column_starts(place_ref, 2, group_width)
    split_kv(starts, group_width, kv_ref, [own_kv_ref, sent_kv_ref])
    for copy in get_queries:
        copy.wait()


def pair(place, key_value, queries, width, group_width):
    rows = queries.shape[0]
    widths = [2 * group_width, 2 * group_width, width, width]
    return pl.pallas_call(
        functools.partial(pair_kernel, width, group_width),
        out_shape=[vmem_out((rows, w), queries.dtype) for w in widths],
        in_specs=[SMEM, ANY, ANY],
        out_specs=[VMEM] * 4,
        scratch_shapes=[
            pltpu.VMEM(key_value.shape, key_value.dtype),
            pltpu.SemaphoreType.DMA((3,)),
        ],
        compiler_params=pltpu.CompilerParams(vmem_limit_bytes=VMEM_LIMIT),
        cost_estimate=pl.CostEstimate(
            flops=0, bytes_accessed=4 * (key_value.size + queries.size), transcendentals=0
        ),
        name="pair",
    )(place, in_hbm(key_value), in_hbm(queries))


def all_kernel(group_width, copies, kv_ref, *out_refs):
    starts = [piece // copies * group_width for piece in range(len(out_refs))]
    split_kv(starts, group_width, kv_ref, out_refs)


def split_all(key_value, pieces, group_width, copies):
    shape = jax.ShapeDtypeStruct((key_value.shape[0], 2 * group_width), key_value.dtype)
    return pl.pallas_call(
        functools.partial(all_kernel, group_width, copies),
        out_shape=[shape] * pieces,
        in_specs=[VMEM],
        out_specs=[VMEM] * pieces,
        compiler_params=pltpu.CompilerParams(vmem_limit_bytes=VMEM_LIMIT),
        name="split_all",
    )(key_value)


def fetch_copies(weight_hbm, first, out_refs, sems):
    parts = FETCH_COPIES
    copies = []
    for k, out_ref in enumerate(out_refs):
        depth, count = out_ref.shape
        rows = depth // parts
        for i in range(parts):
            part = pl.ds(i * rows, rows)
            copies.append(
                pltpu.make_async_copy(
                    weight_hbm.at[part, pl.ds(first, count)],
                    out_ref.at[part, :],
                    sems.at[k * parts + i],
                )
            )
        first += count
    return copies


def fetch_kernel(first, n_after, weight_hbm, *refs):
    *out_refs, done_ref, sems = refs[n_after:]
    pending = fetch_copies(weight_hbm, first, out_refs, sems)
    for copy in pending:
        copy.start()
    done_ref[...] = jnp.zeros_like(done_ref)
    for copy in pending:
        copy.wait()


def fetch(w_out, first, widths, after):
    depth = w_out.shape[0]
    return pl.pallas_call(
        functools.partial(fetch_kernel, first, len(after)),
        out_shape=[
            *[vmem_out((depth, width), w_out.dtype) for width in widths],
            vmem_out((8, HD), jnp.int32),
        ],
        in_specs=[ANY] * (1 + len(after)),
        out_specs=[VMEM] * (1 + len(widths)),
        scratch_shapes=[pltpu.SemaphoreType.DMA((FETCH_COPIES * len(widths),))],
        compiler_params=pltpu.CompilerParams(vmem_limit_bytes=VMEM_LIMIT),
        cost_estimate=pl.CostEstimate(
            flops=0, bytes_accessed=4 * depth * sum(widths), transcendentals=0
        ),
        name="fetch",
    )(in_hbm(w_out), *after)


def prepare_kernel(pieces, n_weights, n_after, place_ref, *refs):
    levels_hbm, mask_hbm, counts_hbm, gate_hbm, weight_hbm = refs[:5]
    usable_ref, live_ref, gate_row_ref, *weight_refs = refs[5 + n_after : 8 + n_after + n_weights]
    levels_ref, mask_ref, counts_ref, gate_ref, small_sems, sems = refs[8 + n_after + n_weights :]
    small = [
        pltpu.make_async_copy(levels_hbm, levels_ref, small_sems.at[0]),
        pltpu.make_async_copy(mask_hbm, mask_ref, small_sems.at[1]),
        pltpu.make_async_copy(counts_hbm, counts_ref, small_sems.at[2]),
    ]
    pending = fetch_copies(weight_hbm, 0, weight_refs, sems)
    for copy in small + pending[:2]:
        copy.start()
    for copy in small:
        copy.wait()
    own_span, own_shard = place_ref[0], place_ref[1]
    level = levels_ref[own_span]
    gate_rows = gate_ref.shape[0]
    first_row = pl.multiple_of(level // gate_rows * gate_rows, gate_rows)
    get_gate = pltpu.make_async_copy(
        gate_hbm.at[pl.ds(first_row, gate_rows), :], gate_ref, small_sems.at[3]
    )
    get_gate.start()
    for copy in pending[2:]:
        copy.start()

    spans = counts_ref.shape[0]
    piece_rows = usable_ref.shape[1] // (spans * pieces)
    ids = lax.broadcasted_iota(jnp.int32, (1, piece_rows), 1)
    for back in range(spans):
        source = jnp.maximum(own_span - back, 0)
        allowed = (mask_ref[own_span, source] > 0) & (own_span >= back)
        limit = jnp.where(allowed, counts_ref[source], 0)
        for piece in range(pieces):
            first = 0
            if pieces == 2:
                first = (own_shard if piece == 0 else 1 - own_shard) * piece_rows
            start = (back * pieces + piece) * piece_rows
            usable_ref[:, start : start + piece_rows] = (first + ids < limit).astype(jnp.int32)
    positions = own_shard * live_ref.shape[0] + lax.broadcasted_iota(jnp.int32, live_ref.shape, 0)
    live_ref[...] = (positions < counts_ref[own_span]).astype(jnp.int32)

    get_gate.wait()
    chosen = lax.broadcasted_iota(jnp.int32, (gate_rows, 1), 0) == level - first_row
    gate = jnp.where(chosen, gate_ref[...].astype(jnp.float32), 0.0)
    gate_row_ref[...] = jnp.sum(gate, axis=0, keepdims=True)
    for copy in pending:
        copy.wait()


def prepare(place, levels, span_mask, counts, gate_table, w_out, widths, keys, pieces, tokens, after):
    depth = w_out.shape[0]
    columns = gate_table.shape[1]
    gate_rows = 16
    return pl.pallas_call(
        functools.partial(prepare_kernel, pieces, len(widths), len(after)),
        out_shape=[
            vmem_out((1, keys), jnp.int32),
            vmem_out((tokens, HD), jnp.int32),
            vmem_out((1, columns), jnp.float32),
            *[vmem_out((depth, width), w_out.dtype) for width in widths],
        ],
        in_specs=[SMEM] + [ANY] * (5 + len(after)),
        out_specs=[VMEM] * (3 + len(widths)),
        scratch_shapes=[
            pltpu.SMEM(levels.shape, levels.dtype),
            pltpu.SMEM(span_mask.shape, span_mask.dtype),
            pltpu.SMEM(counts.shape, counts.dtype),
            pltpu.VMEM((gate_rows, columns), gate_table.dtype),
            pltpu.SemaphoreType.DMA((4,)),
            pltpu.SemaphoreType.DMA((max(1, FETCH_COPIES * len(widths)),)),
        ],
        compiler_params=pltpu.CompilerParams(vmem_limit_bytes=VMEM_LIMIT),
        cost_estimate=pl.CostEstimate(
            flops=0, bytes_accessed=4 * depth * sum(widths), transcendentals=0
        ),
        name="prepare",
    )(
        place,
        *[in_hbm(array) for array in (levels, span_mask, counts, gate_table, w_out)],
        *after,
    )


def softmax_block(query, keys, values, usable):
    scores = lax.dot_general(
        query, keys, (((1,), (1,)), ((), ())), preferred_element_type=jnp.float32
    )
    scores = jnp.where(usable, scores, NEG_FILL)
    highest = jnp.max(scores, axis=1, keepdims=True)
    weights = jnp.exp2((scores - highest) * EXP_SCALE)
    totals = jnp.sum(weights, axis=1, keepdims=True)
    summed = jnp.dot(weights.astype(jnp.bfloat16), values, preferred_element_type=jnp.float32)
    return summed / totals


def attend(usable, groups, sharing, row_tile, query_refs, kv_refs, out_ref):
    group_width = groups * HD
    span = sharing * HD
    key_firsts = [r.shape[1] - 2 * group_width for r in kv_refs]
    value_firsts = [r.shape[1] - group_width for r in kv_refs]
    for g in range(groups):
        keys = jnp.concatenate(
            [r[:, a + g * HD : a + (g + 1) * HD] for r, a in zip(kv_refs, key_firsts)], axis=0
        )
        values = jnp.concatenate(
            [r[:, a + g * HD : a + (g + 1) * HD] for r, a in zip(kv_refs, value_firsts)], axis=0
        )
        done = 0
        for query_ref in query_refs:
            rows = query_ref.shape[0]
            for first in range(0, rows, row_tile):
                tile = min(row_tile, rows - first)
                query = jnp.concatenate(
                    [
                        query_ref[first : first + tile, g * span + h * HD : g * span + (h + 1) * HD]
                        for h in range(sharing)
                    ],
                    axis=0,
                )
                result = softmax_block(query, keys, values, usable).astype(jnp.bfloat16)
                for h in range(sharing):
                    out_ref[
                        done + first : done + first + tile,
                        g * span + h * HD : g * span + (h + 1) * HD,
                    ] = result[h * tile : (h + 1) * tile]
            done += rows


def attention_kernel(n_query, n_kv, groups, sharing, row_tile, usable_ref, *refs):
    query_refs, kv_refs, out_ref = refs[:n_query], refs[n_query : n_query + n_kv], refs[-1]
    usable = usable_ref[...] > 0
    attend(usable, groups, sharing, row_tile, query_refs, kv_refs, out_ref)


def attention(usable, query_pieces, kv_pieces, groups, sharing, after):
    rows = sum(p.shape[0] for p in query_pieces)
    keys = usable.shape[1]
    width = groups * sharing * HD
    row_tile = 64
    scores_bytes = 4 * sharing * row_tile * keys
    operands = [usable, *query_pieces, *kv_pieces, *after]
    return pl.pallas_call(
        functools.partial(
            attention_kernel, len(query_pieces), len(kv_pieces), groups, sharing, row_tile
        ),
        out_shape=jax.ShapeDtypeStruct((rows, width), jnp.bfloat16),
        in_specs=[VMEM] * len(operands),
        out_specs=VMEM,
        compiler_params=pltpu.CompilerParams(
            vmem_limit_bytes=max(VMEM_LIMIT, 12 * scores_bytes)
        ),
        cost_estimate=pl.CostEstimate(
            flops=4 * rows * width * keys,
            bytes_accessed=4 * rows * width + 4 * groups * HD * keys,
            transcendentals=rows * keys * groups * sharing,
        ),
        name="attention",
    )(*operands)


def project_kernel(own_rows, tile, n_weights, attended_ref, *refs):
    own_ref, other_ref = refs[-2:]
    attended = attended_ref[...]
    done = 0
    for weight_ref in refs[:n_weights]:
        for first in range(0, weight_ref.shape[1], tile):
            weights = weight_ref[:, first : first + tile]
            product = jnp.dot(attended, weights, preferred_element_type=jnp.float32)
            columns = slice(done + first, done + first + tile)
            own_ref[:, columns] = product[:own_rows]
            other_ref[:, columns] = product[own_rows:].astype(jnp.bfloat16)
        done += weight_ref.shape[1]


def project(attended, weights, own_rows, after):
    rows, depth = attended.shape
    count = sum(w.shape[1] for w in weights)
    other_rows = rows - own_rows
    return pl.pallas_call(
        functools.partial(project_kernel, own_rows, 512, len(weights)),
        out_shape=[
            jax.ShapeDtypeStruct((own_rows, count), jnp.float32),
            jax.ShapeDtypeStruct((other_rows, count), jnp.bfloat16),
        ],
        in_specs=[VMEM] * (1 + len(weights)) + [ANY] * len(after),
        out_specs=[VMEM, VMEM],
        compiler_params=pltpu.CompilerParams(vmem_limit_bytes=VMEM_LIMIT),
        cost_estimate=pl.CostEstimate(
            flops=2 * rows * depth * count, bytes_accessed=2 * depth * count, transcendentals=0
        ),
        name="project",
    )(attended, *[in_vmem(w) for w in weights], *after)


def combine_kernel(n_chunks, live_ref, gate_ref, *refs):
    own_refs, other_refs, out_ref = refs[:n_chunks], refs[n_chunks : 2 * n_chunks], refs[-1]
    live = live_ref[:, :1] > 0
    first = 0
    for own_ref, other_ref in zip(own_refs, other_refs):
        columns = slice(first, first + own_ref.shape[1])
        gated = (own_ref[...] + other_ref[...].astype(jnp.float32)) * gate_ref[:, columns]
        out_ref[:, columns] = jnp.where(live, gated, 0.0).astype(jnp.bfloat16)
        first += own_ref.shape[1]


def combine(live, gate_row, own_parts, other_parts):
    rows = own_parts[0].shape[0]
    width = sum(p.shape[1] for p in own_parts)
    return pl.pallas_call(
        functools.partial(combine_kernel, len(own_parts)),
        out_shape=jax.ShapeDtypeStruct((rows, width), jnp.bfloat16),
        in_specs=[VMEM] * (2 + 2 * len(own_parts)),
        out_specs=VMEM,
        compiler_params=pltpu.CompilerParams(vmem_limit_bytes=VMEM_LIMIT),
        cost_estimate=pl.CostEstimate(
            flops=2 * rows * width, bytes_accessed=8 * rows * width, transcendentals=0
        ),
        name="combine",
    )(live, gate_row, *own_parts, *other_parts)


def step_up(piece, step, spans):
    return lax.ppermute(piece, "span", [(i, i + 1) for i in range(step, spans - 1)])


def local(queries, key_value, w_out, gate_table, levels, span_mask, counts):
    tokens = queries.shape[0]
    shards = lax.axis_size("head")
    spans = lax.axis_size("span")
    place = jnp.stack([lax.axis_index("span"), lax.axis_index("head")]).astype(jnp.int32)
    head_count = HEADS // shards
    share = HEADS // KV_GROUPS
    sharing = min(share, head_count)
    copies = max(1, share // head_count)
    groups = head_count // sharing
    group_width = groups * HD
    width = head_count * HD
    columns = w_out.shape[1]
    keys = spans * shards * tokens
    small = (place, levels, span_mask, counts, gate_table, w_out)

    if shards == 2:
        swap = [(0, 1), (1, 0)]
        own_kv, sent_kv, own_queries, sent_queries = pair(
            place, key_value, queries, width, group_width
        )
        other_kv = lax.ppermute(sent_kv, "head", swap)
        received = lax.ppermute(sent_queries, "head", swap)
        unit = columns // 12
        fetches = [[units * unit for units in widths] for widths in FETCH_UNITS]
        firsts = [sum(sum(widths) for widths in fetches[:i]) for i in range(len(fetches))]
        own_relay = [step_up(own_kv, 0, spans)]
        other_relay = [step_up(other_kv, 0, spans)]
        usable, live, gate_row, *weights = prepare(
            *small, fetches[0], keys, 2, tokens, own_relay[:1]
        )
        fetched = live
        for step in range(1, spans - 1):
            own_relay.append(step_up(own_relay[-1], step, spans))
            other_relay[-1], _ = lax.optimization_barrier((other_relay[-1], fetched))
            other_relay.append(step_up(other_relay[-1], step, spans))
            *more, fetched = fetch(w_out, firsts[step], fetches[step], [fetched, own_relay[-1]])
            weights += more
        blocks = [own_kv, other_kv]
        for both in zip(own_relay, other_relay):
            blocks += both
        attended = attention(usable, [own_queries, received], blocks, groups, sharing, [fetched])
        own_parts, other_parts = [], []
        for chunk, (first, last) in enumerate(CHUNK_PIECES):
            if chunk == len(CHUNK_PIECES) - 1:
                *more, _ = fetch(w_out, firsts[-1], fetches[-1], own_parts[-1:])
                weights += more
            after = other_parts[chunk - 2 : chunk - 1] if chunk >= 2 else []
            own, other = project(attended, weights[first:last], tokens, after)
            own_parts.append(own)
            other_parts.append(lax.ppermute(other, "head", swap))
    else:
        kv_parts = split_all(key_value, shards, group_width, copies)
        swapped = lax.all_to_all(jnp.stack(kv_parts), "head", split_axis=0, concat_axis=0)
        kv_piece = swapped.reshape(shards * tokens, 2 * group_width)
        by_shard = queries.reshape(tokens, shards, width).transpose(1, 0, 2)
        swapped = lax.all_to_all(by_shard, "head", split_axis=0, concat_axis=0)
        query_piece = swapped.reshape(shards * tokens, width)
        blocks = [kv_piece]
        for back in range(1, spans):
            upward = [(i, i + back) for i in range(spans - back)]
            blocks.append(lax.ppermute(kv_piece, "span", upward))
        usable, live, gate_row = prepare(*small, [], keys, 1, tokens, [])
        attended = attention(usable, [query_piece], blocks, groups, sharing, [])
        partial = jnp.dot(attended, w_out, preferred_element_type=jnp.float32)
        summed = lax.psum_scatter(
            partial.astype(jnp.bfloat16), "head", scatter_dimension=0, tiled=True
        )
        own_parts, other_parts = [jnp.zeros(summed.shape, jnp.float32)], [summed]
    return combine(live, gate_row, own_parts, other_parts)


def solution(mesh):
    in_specs = (
        P(("rep", "span", "head"), None),
        P(("rep", "span", "head"), None, None),
        P("head", None),
        P(),
        P("rep"),
        P("rep", None),
        P("rep"),
    )
    out_specs = P(("rep", "span", "head"), None)
    return jax.shard_map(local, mesh=mesh, in_specs=in_specs, out_specs=out_specs, check_vma=False)
```

```python
import functools
import math

import jax
import jax.numpy as jnp
from jax import lax
from jax.experimental import pallas as pl
from jax.experimental.pallas import tpu as pltpu
from jax.sharding import PartitionSpec as P

HEADS = 48
HD = 128
KV_GROUPS = 8

NEG_FILL = -1e30
EXP_SCALE = HD ** (-0.5) * math.log2(math.e)
VMEM_LIMIT = 8 * 1024 * 1024

FETCH_COPIES = 8
FETCH_UNITS = ((2,), (1, 2), (3,), (4,))
CHUNK_PIECES = ((0, 2), (2, 4), (4, 5))

VMEM = pl.BlockSpec(memory_space=pltpu.VMEM)
SMEM = pl.BlockSpec(memory_space=pltpu.SMEM)
ANY = pl.BlockSpec(memory_space=pl.ANY)


def vmem_out(shape, dtype):
    return pltpu.VMEM(shape, dtype)


def in_vmem(array):
    return pltpu.with_memory_space_constraint(array, pltpu.VMEM)


def in_hbm(array):
    return pltpu.with_memory_space_constraint(array, pltpu.HBM)


def column_starts(place_ref, pieces, width):
    if pieces == 2:
        own = place_ref[1]
        return [pl.multiple_of(own * width, HD), pl.multiple_of((1 - own) * width, HD)]
    return [piece * width for piece in range(pieces)]


def split_kv(starts, group_width, kv_ref, out_refs):
    for start, out_ref in zip(starts, out_refs):
        first = out_ref.shape[1] - 2 * group_width
        out_ref[:, first : first + group_width] = kv_ref[:, 0, pl.ds(start, group_width)]
        out_ref[:, first + group_width :] = kv_ref[:, 1, pl.ds(start, group_width)]


def pair_kernel(width, group_width, place_ref, kv_hbm, query_hbm, *refs):
    own_kv_ref, sent_kv_ref, own_ref, sent_ref, kv_ref, sems = refs
    own_start, sent_start = column_starts(place_ref, 2, width)
    get_kv = pltpu.make_async_copy(kv_hbm, kv_ref, sems.at[0])
    get_queries = [
        pltpu.make_async_copy(query_hbm.at[:, pl.ds(start, width)], ref, sems.at[i + 1])
        for i, (start, ref) in enumerate(((sent_start, sent_ref), (own_start, own_ref)))
    ]
    get_kv.start()
    for copy in get_queries:
        copy.start()
    get_kv.wait()
    starts = column_starts(place_ref, 2, group_width)
    split_kv(starts, group_width, kv_ref, [own_kv_ref, sent_kv_ref])
    for copy in get_queries:
        copy.wait()


def pair(place, key_value, queries, width, group_width):
    rows = queries.shape[0]
    widths = [2 * group_width, 2 * group_width, width, width]
    return pl.pallas_call(
        functools.partial(pair_kernel, width, group_width),
        out_shape=[vmem_out((rows, w), queries.dtype) for w in widths],
        in_specs=[SMEM, ANY, ANY],
        out_specs=[VMEM] * 4,
        scratch_shapes=[
            pltpu.VMEM(key_value.shape, key_value.dtype),
            pltpu.SemaphoreType.DMA((3,)),
        ],
        compiler_params=pltpu.CompilerParams(vmem_limit_bytes=VMEM_LIMIT),
        cost_estimate=pl.CostEstimate(
            flops=0, bytes_accessed=4 * (key_value.size + queries.size), transcendentals=0
        ),
        name="pair",
    )(place, in_hbm(key_value), in_hbm(queries))


def all_kernel(group_width, copies, kv_ref, *out_refs):
    starts = [piece // copies * group_width for piece in range(len(out_refs))]
    split_kv(starts, group_width, kv_ref, out_refs)


def split_all(key_value, pieces, group_width, copies):
    shape = jax.ShapeDtypeStruct((key_value.shape[0], 2 * group_width), key_value.dtype)
    return pl.pallas_call(
        functools.partial(all_kernel, group_width, copies),
        out_shape=[shape] * pieces,
        in_specs=[VMEM],
        out_specs=[VMEM] * pieces,
        compiler_params=pltpu.CompilerParams(vmem_limit_bytes=VMEM_LIMIT),
        name="split_all",
    )(key_value)


def fetch_copies(weight_hbm, first, out_refs, sems):
    parts = FETCH_COPIES
    copies = []
    for k, out_ref in enumerate(out_refs):
        depth, count = out_ref.shape
        rows = depth // parts
        for i in range(parts):
            part = pl.ds(i * rows, rows)
            copies.append(
                pltpu.make_async_copy(
                    weight_hbm.at[part, pl.ds(first, count)],
                    out_ref.at[part, :],
                    sems.at[k * parts + i],
                )
            )
        first += count
    return copies


def fetch_kernel(first, n_after, weight_hbm, *refs):
    *out_refs, done_ref, sems = refs[n_after:]
    pending = fetch_copies(weight_hbm, first, out_refs, sems)
    for copy in pending:
        copy.start()
    done_ref[...] = jnp.zeros_like(done_ref)
    for copy in pending:
        copy.wait()


def fetch(w_out, first, widths, after):
    depth = w_out.shape[0]
    return pl.pallas_call(
        functools.partial(fetch_kernel, first, len(after)),
        out_shape=[
            *[vmem_out((depth, width), w_out.dtype) for width in widths],
            vmem_out((8, HD), jnp.int32),
        ],
        in_specs=[ANY] * (1 + len(after)),
        out_specs=[VMEM] * (1 + len(widths)),
        scratch_shapes=[pltpu.SemaphoreType.DMA((FETCH_COPIES * len(widths),))],
        compiler_params=pltpu.CompilerParams(vmem_limit_bytes=VMEM_LIMIT),
        cost_estimate=pl.CostEstimate(
            flops=0, bytes_accessed=4 * depth * sum(widths), transcendentals=0
        ),
        name="fetch",
    )(in_hbm(w_out), *after)


def prepare_kernel(pieces, place_ref, levels_hbm, mask_hbm, counts_hbm, gate_hbm, *refs):
    usable_ref, live_ref, gate_row_ref, levels_ref, mask_ref, counts_ref, gate_ref, sems = refs
    small = [
        pltpu.make_async_copy(levels_hbm, levels_ref, sems.at[0]),
        pltpu.make_async_copy(mask_hbm, mask_ref, sems.at[1]),
        pltpu.make_async_copy(counts_hbm, counts_ref, sems.at[2]),
    ]
    for copy in small:
        copy.start()
    for copy in small:
        copy.wait()
    own_span, own_shard = place_ref[0], place_ref[1]
    level = levels_ref[own_span]
    gate_rows = gate_ref.shape[0]
    first_row = pl.multiple_of(level // gate_rows * gate_rows, gate_rows)
    get_gate = pltpu.make_async_copy(
        gate_hbm.at[pl.ds(first_row, gate_rows), :], gate_ref, sems.at[3]
    )
    get_gate.start()

    spans = counts_ref.shape[0]
    piece_rows = usable_ref.shape[1] // (spans * pieces)
    ids = lax.broadcasted_iota(jnp.int32, (1, piece_rows), 1)
    for back in range(spans):
        source = jnp.maximum(own_span - back, 0)
        allowed = (mask_ref[own_span, source] > 0) & (own_span >= back)
        limit = jnp.where(allowed, counts_ref[source], 0)
        for piece in range(pieces):
            first = 0
            if pieces == 2:
                first = (own_shard if piece == 0 else 1 - own_shard) * piece_rows
            start = (back * pieces + piece) * piece_rows
            usable_ref[:, start : start + piece_rows] = (first + ids < limit).astype(jnp.int32)
    positions = own_shard * live_ref.shape[0] + lax.broadcasted_iota(jnp.int32, live_ref.shape, 0)
    live_ref[...] = (positions < counts_ref[own_span]).astype(jnp.int32)

    get_gate.wait()
    chosen = lax.broadcasted_iota(jnp.int32, (gate_rows, 1), 0) == level - first_row
    gate = jnp.where(chosen, gate_ref[...].astype(jnp.float32), 0.0)
    gate_row_ref[...] = jnp.sum(gate, axis=0, keepdims=True)


def prepare(place, levels, span_mask, counts, gate_table, keys, pieces, tokens):
    columns = gate_table.shape[1]
    gate_rows = 16
    return pl.pallas_call(
        functools.partial(prepare_kernel, pieces),
        out_shape=[
            vmem_out((1, keys), jnp.int32),
            vmem_out((tokens, HD), jnp.int32),
            vmem_out((1, columns), jnp.float32),
        ],
        in_specs=[SMEM] + [ANY] * 4,
        out_specs=[VMEM] * 3,
        scratch_shapes=[
            pltpu.SMEM(levels.shape, levels.dtype),
            pltpu.SMEM(span_mask.shape, span_mask.dtype),
            pltpu.SMEM(counts.shape, counts.dtype),
            pltpu.VMEM((gate_rows, columns), gate_table.dtype),
            pltpu.SemaphoreType.DMA((4,)),
        ],
        compiler_params=pltpu.CompilerParams(vmem_limit_bytes=VMEM_LIMIT),
        cost_estimate=pl.CostEstimate(
            flops=2 * gate_rows * columns,
            bytes_accessed=2 * gate_rows * columns,
            transcendentals=0,
        ),
        name="prepare",
    )(place, *[in_hbm(array) for array in (levels, span_mask, counts, gate_table)])


def softmax_block(query, keys, values, usable):
    scores = lax.dot_general(
        query, keys, (((1,), (1,)), ((), ())), preferred_element_type=jnp.float32
    )
    scores = jnp.where(usable, scores, NEG_FILL)
    highest = jnp.max(scores, axis=1, keepdims=True)
    weights = jnp.exp2((scores - highest) * EXP_SCALE)
    totals = jnp.sum(weights, axis=1, keepdims=True)
    summed = jnp.dot(weights.astype(jnp.bfloat16), values, preferred_element_type=jnp.float32)
    return summed / totals


def attend(usable, groups, sharing, row_tile, query_refs, kv_refs, out_ref):
    group_width = groups * HD
    span = sharing * HD
    key_firsts = [r.shape[1] - 2 * group_width for r in kv_refs]
    value_firsts = [r.shape[1] - group_width for r in kv_refs]
    for g in range(groups):
        keys = jnp.concatenate(
            [r[:, a + g * HD : a + (g + 1) * HD] for r, a in zip(kv_refs, key_firsts)], axis=0
        )
        values = jnp.concatenate(
            [r[:, a + g * HD : a + (g + 1) * HD] for r, a in zip(kv_refs, value_firsts)], axis=0
        )
        done = 0
        for query_ref in query_refs:
            rows = query_ref.shape[0]
            for first in range(0, rows, row_tile):
                tile = min(row_tile, rows - first)
                query = jnp.concatenate(
                    [
                        query_ref[first : first + tile, g * span + h * HD : g * span + (h + 1) * HD]
                        for h in range(sharing)
                    ],
                    axis=0,
                )
                result = softmax_block(query, keys, values, usable).astype(jnp.bfloat16)
                for h in range(sharing):
                    out_ref[
                        done + first : done + first + tile,
                        g * span + h * HD : g * span + (h + 1) * HD,
                    ] = result[h * tile : (h + 1) * tile]
            done += rows


def attention_kernel(n_query, n_kv, groups, sharing, row_tile, usable_ref, *refs):
    query_refs, kv_refs, out_ref = refs[:n_query], refs[n_query : n_query + n_kv], refs[-1]
    usable = usable_ref[...] > 0
    attend(usable, groups, sharing, row_tile, query_refs, kv_refs, out_ref)


def attention(usable, query_pieces, kv_pieces, groups, sharing, after):
    rows = sum(p.shape[0] for p in query_pieces)
    keys = usable.shape[1]
    width = groups * sharing * HD
    row_tile = 64
    scores_bytes = 4 * sharing * row_tile * keys
    operands = [usable, *query_pieces, *kv_pieces, *after]
    return pl.pallas_call(
        functools.partial(
            attention_kernel, len(query_pieces), len(kv_pieces), groups, sharing, row_tile
        ),
        out_shape=jax.ShapeDtypeStruct((rows, width), jnp.bfloat16),
        in_specs=[VMEM] * len(operands),
        out_specs=VMEM,
        compiler_params=pltpu.CompilerParams(
            vmem_limit_bytes=max(VMEM_LIMIT, 12 * scores_bytes)
        ),
        cost_estimate=pl.CostEstimate(
            flops=4 * rows * width * keys,
            bytes_accessed=4 * rows * width + 4 * groups * HD * keys,
            transcendentals=rows * keys * groups * sharing,
        ),
        name="attention",
    )(*operands)


def project_kernel(own_rows, tile, n_weights, attended_ref, *refs):
    own_ref, other_ref = refs[-2:]
    attended = attended_ref[...]
    done = 0
    for weight_ref in refs[:n_weights]:
        for first in range(0, weight_ref.shape[1], tile):
            weights = weight_ref[:, first : first + tile]
            product = jnp.dot(attended, weights, preferred_element_type=jnp.float32)
            columns = slice(done + first, done + first + tile)
            own_ref[:, columns] = product[:own_rows]
            other_ref[:, columns] = product[own_rows:].astype(jnp.bfloat16)
        done += weight_ref.shape[1]


def project(attended, weights, own_rows, after):
    rows, depth = attended.shape
    count = sum(w.shape[1] for w in weights)
    other_rows = rows - own_rows
    return pl.pallas_call(
        functools.partial(project_kernel, own_rows, 512, len(weights)),
        out_shape=[
            jax.ShapeDtypeStruct((own_rows, count), jnp.float32),
            jax.ShapeDtypeStruct((other_rows, count), jnp.bfloat16),
        ],
        in_specs=[VMEM] * (1 + len(weights)) + [ANY] * len(after),
        out_specs=[VMEM, VMEM],
        compiler_params=pltpu.CompilerParams(vmem_limit_bytes=VMEM_LIMIT),
        cost_estimate=pl.CostEstimate(
            flops=2 * rows * depth * count, bytes_accessed=2 * depth * count, transcendentals=0
        ),
        name="project",
    )(attended, *[in_vmem(w) for w in weights], *after)


def combine_kernel(n_chunks, live_ref, gate_ref, *refs):
    own_refs, other_refs, out_ref = refs[:n_chunks], refs[n_chunks : 2 * n_chunks], refs[-1]
    live = live_ref[:, :1] > 0
    first = 0
    for own_ref, other_ref in zip(own_refs, other_refs):
        columns = slice(first, first + own_ref.shape[1])
        gated = (own_ref[...] + other_ref[...].astype(jnp.float32)) * gate_ref[:, columns]
        out_ref[:, columns] = jnp.where(live, gated, 0.0).astype(jnp.bfloat16)
        first += own_ref.shape[1]


def combine(live, gate_row, own_parts, other_parts):
    rows = own_parts[0].shape[0]
    width = sum(p.shape[1] for p in own_parts)
    return pl.pallas_call(
        functools.partial(combine_kernel, len(own_parts)),
        out_shape=jax.ShapeDtypeStruct((rows, width), jnp.bfloat16),
        in_specs=[VMEM] * (2 + 2 * len(own_parts)),
        out_specs=VMEM,
        compiler_params=pltpu.CompilerParams(vmem_limit_bytes=VMEM_LIMIT),
        cost_estimate=pl.CostEstimate(
            flops=2 * rows * width, bytes_accessed=8 * rows * width, transcendentals=0
        ),
        name="combine",
    )(live, gate_row, *own_parts, *other_parts)


def send_up(piece, back, first, spans):
    return lax.ppermute(piece, "span", [(i, i + back) for i in range(first, spans - back)])


def local(queries, key_value, w_out, gate_table, levels, span_mask, counts):
    tokens = queries.shape[0]
    shards = lax.axis_size("head")
    spans = lax.axis_size("span")
    place = jnp.stack([lax.axis_index("span"), lax.axis_index("head")]).astype(jnp.int32)
    head_count = HEADS // shards
    share = HEADS // KV_GROUPS
    sharing = min(share, head_count)
    copies = max(1, share // head_count)
    groups = head_count // sharing
    group_width = groups * HD
    width = head_count * HD
    columns = w_out.shape[1]
    keys = spans * shards * tokens
    small = (place, levels, span_mask, counts, gate_table)

    if shards == 2:
        swap = [(0, 1), (1, 0)]
        own_kv, sent_kv, own_queries, sent_queries = pair(
            place, key_value, queries, width, group_width
        )
        usable, live, gate_row = prepare(*small, keys, 2, tokens)
        other_kv, live = lax.optimization_barrier((lax.ppermute(sent_kv, "head", swap), live))
        received = lax.ppermute(sent_queries, "head", swap)
        unit = columns // 12
        fetches = [[units * unit for units in widths] for widths in FETCH_UNITS]
        firsts = [sum(sum(widths) for widths in fetches[:i]) for i in range(len(fetches))]
        *weights, fetched = fetch(w_out, firsts[0], fetches[0], [other_kv])
        own_blocks, other_blocks = [own_kv], [other_kv]
        for pieces, step in ((own_blocks, 1), (other_blocks, 2)):
            pieces += [send_up(pieces[0], back, 0, spans) for back in range(1, min(spans, 3))]
            for back in range(3, spans):
                pieces[-1], fetched = lax.optimization_barrier((pieces[-1], fetched))
                pieces.append(send_up(pieces[-1], 1, back - 1, spans))
            *more, fetched = fetch(w_out, firsts[step], fetches[step], [fetched, pieces[2]])
            weights += more
        blocks = [piece for both in zip(own_blocks, other_blocks) for piece in both]
        attended = attention(usable, [own_queries, received], blocks, groups, sharing, [fetched])
        own_parts, other_parts = [], []
        for chunk, (first, last) in enumerate(CHUNK_PIECES):
            if chunk == len(CHUNK_PIECES) - 1:
                *more, _ = fetch(w_out, firsts[-1], fetches[-1], own_parts[-1:])
                weights += more
            after = other_parts[chunk - 2 : chunk - 1] if chunk >= 2 else []
            own, other = project(attended, weights[first:last], tokens, after)
            own_parts.append(own)
            other_parts.append(lax.ppermute(other, "head", swap))
    else:
        kv_parts = split_all(key_value, shards, group_width, copies)
        swapped = lax.all_to_all(jnp.stack(kv_parts), "head", split_axis=0, concat_axis=0)
        kv_piece = swapped.reshape(shards * tokens, 2 * group_width)
        by_shard = queries.reshape(tokens, shards, width).transpose(1, 0, 2)
        swapped = lax.all_to_all(by_shard, "head", split_axis=0, concat_axis=0)
        query_piece = swapped.reshape(shards * tokens, width)
        blocks = [kv_piece]
        for back in range(1, spans):
            blocks.append(send_up(kv_piece, back, 0, spans))
        usable, live, gate_row = prepare(*small, keys, 1, tokens)
        attended = attention(usable, [query_piece], blocks, groups, sharing, [])
        partial = jnp.dot(attended, w_out, preferred_element_type=jnp.float32)
        summed = lax.psum_scatter(
            partial.astype(jnp.bfloat16), "head", scatter_dimension=0, tiled=True
        )
        own_parts, other_parts = [jnp.zeros(summed.shape, jnp.float32)], [summed]
    return combine(live, gate_row, own_parts, other_parts)


def solution(mesh):
    in_specs = (
        P(("rep", "span", "head"), None),
        P(("rep", "span", "head"), None, None),
        P("head", None),
        P(),
        P("rep"),
        P("rep", None),
        P("rep"),
    )
    out_specs = P(("rep", "span", "head"), None)
    return jax.shard_map(local, mesh=mesh, in_specs=in_specs, out_specs=out_specs, check_vma=False)
```

```python
import functools
import math

import jax
import jax.numpy as jnp
from jax import lax
from jax.experimental import pallas as pl
from jax.experimental.pallas import tpu as pltpu
from jax.sharding import PartitionSpec as P

HEADS = 48
HD = 128
KV_GROUPS = 8

NEG_FILL = -1e30
EXP_SCALE = HD ** (-0.5) * math.log2(math.e)
VMEM_LIMIT = 8 * 1024 * 1024

FETCH_COPIES = 8
FETCH_UNITS = ((3,), (4,), (1,), (2,), (2,))
CHUNK_PIECES = ((0, 1), (1, 3), (3, 5))

VMEM = pl.BlockSpec(memory_space=pltpu.VMEM)
ANY = pl.BlockSpec(memory_space=pl.ANY)


def vmem_out(shape, dtype):
    return pltpu.VMEM(shape, dtype)


def in_vmem(array):
    return pltpu.with_memory_space_constraint(array, pltpu.VMEM)


def in_hbm(array):
    return pltpu.with_memory_space_constraint(array, pltpu.HBM)


def column_starts(width):
    own = lax.axis_index("head")
    return [pl.multiple_of(own * width, HD), pl.multiple_of((1 - own) * width, HD)]


def split_kv(starts, group_width, kv_ref, out_refs):
    for start, out_ref in zip(starts, out_refs):
        first = out_ref.shape[1] - 2 * group_width
        out_ref[:, first : first + group_width] = kv_ref[:, 0, pl.ds(start, group_width)]
        out_ref[:, first + group_width :] = kv_ref[:, 1, pl.ds(start, group_width)]


def pair_kernel(width, group_width, kv_hbm, query_hbm, *refs):
    own_kv_ref, sent_kv_ref, own_ref, sent_ref, kv_ref, sems = refs
    own_start, sent_start = column_starts(width)
    get_kv = pltpu.make_async_copy(kv_hbm, kv_ref, sems.at[0])
    get_queries = [
        pltpu.make_async_copy(query_hbm.at[:, pl.ds(start, width)], ref, sems.at[i + 1])
        for i, (start, ref) in enumerate(((sent_start, sent_ref), (own_start, own_ref)))
    ]
    get_kv.start()
    for copy in get_queries:
        copy.start()
    get_kv.wait()
    starts = column_starts(group_width)
    split_kv(starts, group_width, kv_ref, [own_kv_ref, sent_kv_ref])
    for copy in get_queries:
        copy.wait()


def pair(key_value, queries, width, group_width):
    rows = queries.shape[0]
    widths = [2 * group_width, 2 * group_width, width, width]
    return pl.pallas_call(
        functools.partial(pair_kernel, width, group_width),
        out_shape=[vmem_out((rows, w), queries.dtype) for w in widths],
        in_specs=[ANY, ANY],
        out_specs=[VMEM] * 4,
        scratch_shapes=[
            pltpu.VMEM(key_value.shape, key_value.dtype),
            pltpu.SemaphoreType.DMA((3,)),
        ],
        compiler_params=pltpu.CompilerParams(vmem_limit_bytes=VMEM_LIMIT),
        cost_estimate=pl.CostEstimate(
            flops=0, bytes_accessed=4 * (key_value.size + queries.size), transcendentals=0
        ),
        name="pair",
    )(in_hbm(key_value), in_hbm(queries))


def all_kernel(group_width, copies, kv_ref, *out_refs):
    starts = [piece // copies * group_width for piece in range(len(out_refs))]
    split_kv(starts, group_width, kv_ref, out_refs)


def split_all(key_value, pieces, group_width, copies):
    shape = jax.ShapeDtypeStruct((key_value.shape[0], 2 * group_width), key_value.dtype)
    return pl.pallas_call(
        functools.partial(all_kernel, group_width, copies),
        out_shape=[shape] * pieces,
        in_specs=[VMEM],
        out_specs=[VMEM] * pieces,
        compiler_params=pltpu.CompilerParams(vmem_limit_bytes=VMEM_LIMIT),
        name="split_all",
    )(key_value)


def fetch_copies(weight_hbm, first, out_refs, sems):
    parts = FETCH_COPIES
    copies = []
    for k, out_ref in enumerate(out_refs):
        depth, count = out_ref.shape
        rows = depth // parts
        for i in range(parts):
            part = pl.ds(i * rows, rows)
            copies.append(
                pltpu.make_async_copy(
                    weight_hbm.at[part, pl.ds(first, count)],
                    out_ref.at[part, :],
                    sems.at[k * parts + i],
                )
            )
        first += count
    return copies


def fetch_kernel(first, n_after, weight_hbm, *refs):
    *out_refs, done_ref, sems = refs[n_after:]
    pending = fetch_copies(weight_hbm, first, out_refs, sems)
    for copy in pending:
        copy.start()
    done_ref[...] = jnp.zeros_like(done_ref)
    for copy in pending:
        copy.wait()


def fetch(w_out, first, widths, after):
    depth = w_out.shape[0]
    return pl.pallas_call(
        functools.partial(fetch_kernel, first, len(after)),
        out_shape=[
            *[vmem_out((depth, width), w_out.dtype) for width in widths],
            vmem_out((8, HD), jnp.int32),
        ],
        in_specs=[ANY] * (1 + len(after)),
        out_specs=[VMEM] * (1 + len(widths)),
        scratch_shapes=[pltpu.SemaphoreType.DMA((FETCH_COPIES * len(widths),))],
        compiler_params=pltpu.CompilerParams(vmem_limit_bytes=VMEM_LIMIT),
        cost_estimate=pl.CostEstimate(
            flops=0, bytes_accessed=4 * depth * sum(widths), transcendentals=0
        ),
        name="fetch",
    )(in_hbm(w_out), *after)


def prepare_kernel(pieces, levels_hbm, mask_hbm, counts_hbm, gate_hbm, *refs):
    usable_ref, live_ref, gate_row_ref, levels_ref, mask_ref, counts_ref, gate_ref, sems = refs
    small = [
        pltpu.make_async_copy(levels_hbm, levels_ref, sems.at[0]),
        pltpu.make_async_copy(mask_hbm, mask_ref, sems.at[1]),
        pltpu.make_async_copy(counts_hbm, counts_ref, sems.at[2]),
    ]
    for copy in small:
        copy.start()
    for copy in small:
        copy.wait()
    own_span, own_shard = lax.axis_index("span"), lax.axis_index("head")
    level = levels_ref[own_span]
    gate_rows = gate_ref.shape[0]
    first_row = pl.multiple_of(level // gate_rows * gate_rows, gate_rows)
    get_gate = pltpu.make_async_copy(
        gate_hbm.at[pl.ds(first_row, gate_rows), :], gate_ref, sems.at[3]
    )
    get_gate.start()

    spans = counts_ref.shape[0]
    piece_rows = usable_ref.shape[1] // (spans * pieces)
    ids = lax.broadcasted_iota(jnp.int32, (1, piece_rows), 1)
    for back in range(spans):
        source = jnp.maximum(own_span - back, 0)
        allowed = (mask_ref[own_span, source] > 0) & (own_span >= back)
        limit = jnp.where(allowed, counts_ref[source], 0)
        for piece in range(pieces):
            first = 0
            if pieces == 2:
                first = (own_shard if piece == 0 else 1 - own_shard) * piece_rows
            start = (back * pieces + piece) * piece_rows
            usable_ref[:, start : start + piece_rows] = (first + ids < limit).astype(jnp.int32)
    positions = own_shard * live_ref.shape[0] + lax.broadcasted_iota(jnp.int32, live_ref.shape, 0)
    live_ref[...] = (positions < counts_ref[own_span]).astype(jnp.int32)

    get_gate.wait()
    chosen = lax.broadcasted_iota(jnp.int32, (gate_rows, 1), 0) == level - first_row
    gate = jnp.where(chosen, gate_ref[...].astype(jnp.float32), 0.0)
    gate_row_ref[...] = jnp.sum(gate, axis=0, keepdims=True)


def prepare(levels, span_mask, counts, gate_table, keys, pieces, tokens):
    columns = gate_table.shape[1]
    gate_rows = 16
    return pl.pallas_call(
        functools.partial(prepare_kernel, pieces),
        out_shape=[
            vmem_out((1, keys), jnp.int32),
            vmem_out((tokens, HD), jnp.int32),
            vmem_out((1, columns), jnp.float32),
        ],
        in_specs=[ANY] * 4,
        out_specs=[VMEM] * 3,
        scratch_shapes=[
            pltpu.SMEM(levels.shape, levels.dtype),
            pltpu.SMEM(span_mask.shape, span_mask.dtype),
            pltpu.SMEM(counts.shape, counts.dtype),
            pltpu.VMEM((gate_rows, columns), gate_table.dtype),
            pltpu.SemaphoreType.DMA((4,)),
        ],
        compiler_params=pltpu.CompilerParams(vmem_limit_bytes=VMEM_LIMIT),
        cost_estimate=pl.CostEstimate(
            flops=2 * gate_rows * columns,
            bytes_accessed=2 * gate_rows * columns,
            transcendentals=0,
        ),
        name="prepare",
    )(*[in_hbm(array) for array in (levels, span_mask, counts, gate_table)])


def softmax_block(query, keys, values, usable):
    scores = lax.dot_general(
        query, keys, (((1,), (1,)), ((), ())), preferred_element_type=jnp.float32
    )
    scores = jnp.where(usable, scores, NEG_FILL)
    highest = jnp.max(scores, axis=1, keepdims=True)
    weights = jnp.exp2((scores - highest) * EXP_SCALE)
    totals = jnp.sum(weights, axis=1, keepdims=True)
    summed = jnp.dot(weights.astype(jnp.bfloat16), values, preferred_element_type=jnp.float32)
    return summed / totals


def attend(usable, groups, sharing, row_tile, query_refs, kv_refs, out_ref):
    group_width = groups * HD
    span = sharing * HD
    key_firsts = [r.shape[1] - 2 * group_width for r in kv_refs]
    value_firsts = [r.shape[1] - group_width for r in kv_refs]
    for g in range(groups):
        keys = jnp.concatenate(
            [r[:, a + g * HD : a + (g + 1) * HD] for r, a in zip(kv_refs, key_firsts)], axis=0
        )
        values = jnp.concatenate(
            [r[:, a + g * HD : a + (g + 1) * HD] for r, a in zip(kv_refs, value_firsts)], axis=0
        )
        done = 0
        for query_ref in query_refs:
            rows = query_ref.shape[0]
            for first in range(0, rows, row_tile):
                tile = min(row_tile, rows - first)
                query = jnp.concatenate(
                    [
                        query_ref[first : first + tile, g * span + h * HD : g * span + (h + 1) * HD]
                        for h in range(sharing)
                    ],
                    axis=0,
                )
                result = softmax_block(query, keys, values, usable).astype(jnp.bfloat16)
                for h in range(sharing):
                    out_ref[
                        done + first : done + first + tile,
                        g * span + h * HD : g * span + (h + 1) * HD,
                    ] = result[h * tile : (h + 1) * tile]
            done += rows


def attention_kernel(n_query, n_kv, groups, sharing, row_tile, usable_ref, *refs):
    query_refs, kv_refs, out_ref = refs[:n_query], refs[n_query : n_query + n_kv], refs[-1]
    usable = usable_ref[...] > 0
    attend(usable, groups, sharing, row_tile, query_refs, kv_refs, out_ref)


def attention(usable, query_pieces, kv_pieces, groups, sharing, after):
    rows = sum(p.shape[0] for p in query_pieces)
    keys = usable.shape[1]
    width = groups * sharing * HD
    row_tile = 64
    scores_bytes = 4 * sharing * row_tile * keys
    operands = [usable, *query_pieces, *kv_pieces, *after]
    return pl.pallas_call(
        functools.partial(
            attention_kernel, len(query_pieces), len(kv_pieces), groups, sharing, row_tile
        ),
        out_shape=jax.ShapeDtypeStruct((rows, width), jnp.bfloat16),
        in_specs=[VMEM] * len(operands),
        out_specs=VMEM,
        compiler_params=pltpu.CompilerParams(
            vmem_limit_bytes=max(VMEM_LIMIT, 12 * scores_bytes)
        ),
        cost_estimate=pl.CostEstimate(
            flops=4 * rows * width * keys,
            bytes_accessed=4 * rows * width + 4 * groups * HD * keys,
            transcendentals=rows * keys * groups * sharing,
        ),
        name="attention",
    )(*operands)


def project_kernel(own_rows, tile, n_weights, n_after, fetch_first, attended_ref, *refs):
    weight_refs = refs[:n_weights]
    rest = refs[n_weights + n_after :]
    pending = []
    if fetch_first is None:
        own_ref, other_ref = rest
    else:
        weight_hbm, own_ref, other_ref, fetched_ref, sems = rest
        pending = fetch_copies(weight_hbm, fetch_first, [fetched_ref], sems)
    for copy in pending:
        copy.start()
    attended = attended_ref[...]
    done = 0
    for weight_ref in weight_refs:
        for first in range(0, weight_ref.shape[1], tile):
            weights = weight_ref[:, first : first + tile]
            product = jnp.dot(attended, weights, preferred_element_type=jnp.float32)
            columns = slice(done + first, done + first + tile)
            own_ref[:, columns] = product[:own_rows]
            other_ref[:, columns] = product[own_rows:].astype(jnp.bfloat16)
        done += weight_ref.shape[1]
    for copy in pending:
        copy.wait()


def project(attended, weights, own_rows, after, w_out=None, fetch_first=None, fetch_width=0):
    rows, depth = attended.shape
    count = sum(w.shape[1] for w in weights)
    other_rows = rows - own_rows
    out_shape = [
        jax.ShapeDtypeStruct((own_rows, count), jnp.float32),
        jax.ShapeDtypeStruct((other_rows, count), jnp.bfloat16),
    ]
    operands = [attended, *[in_vmem(w) for w in weights], *after]
    in_specs = [VMEM] * (1 + len(weights)) + [ANY] * len(after)
    scratch = []
    if fetch_first is not None:
        out_shape.append(vmem_out((depth, fetch_width), w_out.dtype))
        operands.append(in_hbm(w_out))
        in_specs.append(ANY)
        scratch.append(pltpu.SemaphoreType.DMA((FETCH_COPIES,)))
    return pl.pallas_call(
        functools.partial(
            project_kernel, own_rows, 512, len(weights), len(after), fetch_first
        ),
        out_shape=out_shape,
        in_specs=in_specs,
        out_specs=[VMEM] * len(out_shape),
        scratch_shapes=scratch,
        compiler_params=pltpu.CompilerParams(vmem_limit_bytes=VMEM_LIMIT),
        cost_estimate=pl.CostEstimate(
            flops=2 * rows * depth * count, bytes_accessed=2 * depth * count, transcendentals=0
        ),
        name="project",
    )(*operands)


def combine_kernel(n_chunks, live_ref, gate_ref, *refs):
    own_refs, other_refs, out_ref = refs[:n_chunks], refs[n_chunks : 2 * n_chunks], refs[-1]
    live = live_ref[:, :1] > 0
    first = 0
    for own_ref, other_ref in zip(own_refs, other_refs):
        columns = slice(first, first + own_ref.shape[1])
        gated = (own_ref[...] + other_ref[...].astype(jnp.float32)) * gate_ref[:, columns]
        out_ref[:, columns] = jnp.where(live, gated, 0.0).astype(jnp.bfloat16)
        first += own_ref.shape[1]


def combine(live, gate_row, own_parts, other_parts):
    rows = own_parts[0].shape[0]
    width = sum(p.shape[1] for p in own_parts)
    return pl.pallas_call(
        functools.partial(combine_kernel, len(own_parts)),
        out_shape=jax.ShapeDtypeStruct((rows, width), jnp.bfloat16),
        in_specs=[VMEM] * (2 + 2 * len(own_parts)),
        out_specs=VMEM,
        compiler_params=pltpu.CompilerParams(vmem_limit_bytes=VMEM_LIMIT),
        cost_estimate=pl.CostEstimate(
            flops=2 * rows * width, bytes_accessed=8 * rows * width, transcendentals=0
        ),
        name="combine",
    )(live, gate_row, *own_parts, *other_parts)


def send_up(piece, back, first, spans):
    return lax.ppermute(piece, "span", [(i, i + back) for i in range(first, spans - back)])


def local(queries, key_value, w_out, gate_table, levels, span_mask, counts):
    tokens = queries.shape[0]
    shards = lax.axis_size("head")
    spans = lax.axis_size("span")
    head_count = HEADS // shards
    share = HEADS // KV_GROUPS
    sharing = min(share, head_count)
    copies = max(1, share // head_count)
    groups = head_count // sharing
    group_width = groups * HD
    width = head_count * HD
    columns = w_out.shape[1]
    keys = spans * shards * tokens
    small = (levels, span_mask, counts, gate_table)

    if shards == 2:
        swap = [(0, 1), (1, 0)]
        own_kv, sent_kv, own_queries, sent_queries = pair(
            key_value, queries, width, group_width
        )
        usable, live, gate_row = prepare(*small, keys, 2, tokens)
        other_kv, live = lax.optimization_barrier((lax.ppermute(sent_kv, "head", swap), live))
        received = lax.ppermute(sent_queries, "head", swap)
        unit = columns // 12
        fetches = [[units * unit for units in widths] for widths in FETCH_UNITS]
        firsts = [sum(sum(widths) for widths in fetches[:i]) for i in range(len(fetches))]
        *weights, fetched = fetch(w_out, firsts[0], fetches[0], [other_kv])
        own_blocks, other_blocks = [own_kv], [other_kv]
        for pieces in (own_blocks, other_blocks):
            pieces += [send_up(pieces[0], back, 0, spans) for back in range(1, min(spans, 3))]
            for back in range(3, spans):
                pieces[-1], fetched = lax.optimization_barrier((pieces[-1], fetched))
                pieces.append(send_up(pieces[-1], 1, back - 1, spans))
        *more, fetched = fetch(w_out, firsts[1], fetches[1], [fetched, other_blocks[2]])
        weights += more
        blocks = [piece for both in zip(own_blocks, other_blocks) for piece in both]
        attended = attention(usable, [own_queries, received], blocks, groups, sharing, [fetched])
        own_parts, other_parts = [], []
        for chunk, (first, last) in enumerate(CHUNK_PIECES):
            if chunk < len(CHUNK_PIECES) - 1:
                step = chunk + 2
                more = (w_out, firsts[step], sum(fetches[step]))
            else:
                *late, _ = fetch(w_out, firsts[-1], fetches[-1], own_parts[-1:])
                weights += late
                more = ()
            after = other_parts[chunk - 2 : chunk - 1] if chunk >= 2 else []
            own, other, *fetched = project(attended, weights[first:last], tokens, after, *more)
            weights += fetched
            own_parts.append(own)
            other_parts.append(lax.ppermute(other, "head", swap))
    else:
        kv_parts = split_all(key_value, shards, group_width, copies)
        swapped = lax.all_to_all(jnp.stack(kv_parts), "head", split_axis=0, concat_axis=0)
        kv_piece = swapped.reshape(shards * tokens, 2 * group_width)
        by_shard = queries.reshape(tokens, shards, width).transpose(1, 0, 2)
        swapped = lax.all_to_all(by_shard, "head", split_axis=0, concat_axis=0)
        query_piece = swapped.reshape(shards * tokens, width)
        blocks = [kv_piece]
        for back in range(1, spans):
            blocks.append(send_up(kv_piece, back, 0, spans))
        usable, live, gate_row = prepare(*small, keys, 1, tokens)
        attended = attention(usable, [query_piece], blocks, groups, sharing, [])
        partial = jnp.dot(attended, w_out, preferred_element_type=jnp.float32)
        summed = lax.psum_scatter(
            partial.astype(jnp.bfloat16), "head", scatter_dimension=0, tiled=True
        )
        own_parts, other_parts = [jnp.zeros(summed.shape, jnp.float32)], [summed]
    return combine(live, gate_row, own_parts, other_parts)


def solution(mesh):
    in_specs = (
        P(("rep", "span", "head"), None),
        P(("rep", "span", "head"), None, None),
        P("head", None),
        P(),
        P("rep"),
        P("rep", None),
        P("rep"),
    )
    out_specs = P(("rep", "span", "head"), None)
    return jax.shard_map(local, mesh=mesh, in_specs=in_specs, out_specs=out_specs, check_vma=False)
```

```python
import functools
import math

import jax
import jax.numpy as jnp
from jax import lax
from jax.experimental import pallas as pl
from jax.experimental.pallas import tpu as pltpu
from jax.sharding import PartitionSpec as P

HEADS = 48
HD = 128
KV_GROUPS = 8

NEG_FILL = -1e30
EXP_SCALE = HD ** (-0.5) * math.log2(math.e)
VMEM_LIMIT = 6 * 1024 * 1024

FETCH_COPIES = 8
FETCH_UNITS = ((4,), (2, 2), (2,), (2,))

VMEM = pl.BlockSpec(memory_space=pltpu.VMEM)
ANY = pl.BlockSpec(memory_space=pl.ANY)


def vmem_out(shape, dtype):
    return pltpu.VMEM(shape, dtype)


def in_vmem(array):
    return pltpu.with_memory_space_constraint(array, pltpu.VMEM)


def in_hbm(array):
    return pltpu.with_memory_space_constraint(array, pltpu.HBM)


def column_starts(width):
    own = lax.axis_index("head")
    return [pl.multiple_of(own * width, HD), pl.multiple_of((1 - own) * width, HD)]


def split_kv(starts, group_width, kv_ref, out_refs):
    for start, out_ref in zip(starts, out_refs):
        first = out_ref.shape[1] - 2 * group_width
        out_ref[:, first : first + group_width] = kv_ref[:, 0, pl.ds(start, group_width)]
        out_ref[:, first + group_width :] = kv_ref[:, 1, pl.ds(start, group_width)]


def pair_kernel(width, group_width, kv_hbm, query_hbm, *refs):
    own_kv_ref, sent_kv_ref, own_ref, sent_ref, kv_ref, sems = refs
    own_start, sent_start = column_starts(width)
    get_kv = pltpu.make_async_copy(kv_hbm, kv_ref, sems.at[0])
    get_queries = [
        pltpu.make_async_copy(query_hbm.at[:, pl.ds(start, width)], ref, sems.at[i + 1])
        for i, (start, ref) in enumerate(((sent_start, sent_ref), (own_start, own_ref)))
    ]
    get_kv.start()
    for copy in get_queries:
        copy.start()
    get_kv.wait()
    starts = column_starts(group_width)
    split_kv(starts, group_width, kv_ref, [own_kv_ref, sent_kv_ref])
    for copy in get_queries:
        copy.wait()


def pair(key_value, queries, width, group_width):
    rows = queries.shape[0]
    widths = [2 * group_width, 2 * group_width, width, width]
    return pl.pallas_call(
        functools.partial(pair_kernel, width, group_width),
        out_shape=[vmem_out((rows, w), queries.dtype) for w in widths],
        in_specs=[ANY, ANY],
        out_specs=[VMEM] * 4,
        scratch_shapes=[
            pltpu.VMEM(key_value.shape, key_value.dtype),
            pltpu.SemaphoreType.DMA((3,)),
        ],
        compiler_params=pltpu.CompilerParams(vmem_limit_bytes=VMEM_LIMIT),
        cost_estimate=pl.CostEstimate(
            flops=0, bytes_accessed=4 * (key_value.size + queries.size), transcendentals=0
        ),
        name="pair",
    )(in_hbm(key_value), in_hbm(queries))


def all_kernel(group_width, copies, kv_ref, *out_refs):
    starts = [piece // copies * group_width for piece in range(len(out_refs))]
    split_kv(starts, group_width, kv_ref, out_refs)


def split_all(key_value, pieces, group_width, copies):
    shape = jax.ShapeDtypeStruct((key_value.shape[0], 2 * group_width), key_value.dtype)
    return pl.pallas_call(
        functools.partial(all_kernel, group_width, copies),
        out_shape=[shape] * pieces,
        in_specs=[VMEM],
        out_specs=[VMEM] * pieces,
        compiler_params=pltpu.CompilerParams(vmem_limit_bytes=VMEM_LIMIT),
        name="split_all",
    )(key_value)


def fetch_copies(weight_hbm, first, out_refs, sems):
    parts = FETCH_COPIES
    copies = []
    for k, out_ref in enumerate(out_refs):
        depth, count = out_ref.shape
        rows = depth // parts
        for i in range(parts):
            part = pl.ds(i * rows, rows)
            copies.append(
                pltpu.make_async_copy(
                    weight_hbm.at[part, pl.ds(first, count)],
                    out_ref.at[part, :],
                    sems.at[k * parts + i],
                )
            )
        first += count
    return copies


def fetch_kernel(first, n_after, weight_hbm, *refs):
    *out_refs, done_ref, sems = refs[n_after:]
    pending = fetch_copies(weight_hbm, first, out_refs, sems)
    for copy in pending:
        copy.start()
    done_ref[...] = jnp.zeros_like(done_ref)
    for copy in pending:
        copy.wait()


def fetch(w_out, first, widths, after):
    depth = w_out.shape[0]
    return pl.pallas_call(
        functools.partial(fetch_kernel, first, len(after)),
        out_shape=[
            *[vmem_out((depth, width), w_out.dtype) for width in widths],
            vmem_out((8, HD), jnp.int32),
        ],
        in_specs=[ANY] * (1 + len(after)),
        out_specs=[VMEM] * (1 + len(widths)),
        scratch_shapes=[pltpu.SemaphoreType.DMA((FETCH_COPIES * len(widths),))],
        compiler_params=pltpu.CompilerParams(vmem_limit_bytes=VMEM_LIMIT),
        cost_estimate=pl.CostEstimate(
            flops=0, bytes_accessed=4 * depth * sum(widths), transcendentals=0
        ),
        name="fetch",
    )(in_hbm(w_out), *after)


def prepare_kernel(pieces, levels_hbm, mask_hbm, counts_hbm, gate_hbm, *refs):
    usable_ref, live_ref, gate_row_ref, levels_ref, mask_ref, counts_ref, gate_ref, sems = refs
    small = [
        pltpu.make_async_copy(levels_hbm, levels_ref, sems.at[0]),
        pltpu.make_async_copy(mask_hbm, mask_ref, sems.at[1]),
        pltpu.make_async_copy(counts_hbm, counts_ref, sems.at[2]),
    ]
    for copy in small:
        copy.start()
    for copy in small:
        copy.wait()
    own_span, own_shard = lax.axis_index("span"), lax.axis_index("head")
    level = levels_ref[own_span]
    gate_rows = gate_ref.shape[0]
    first_row = pl.multiple_of(level // gate_rows * gate_rows, gate_rows)
    get_gate = pltpu.make_async_copy(
        gate_hbm.at[pl.ds(first_row, gate_rows), :], gate_ref, sems.at[3]
    )
    get_gate.start()

    spans = counts_ref.shape[0]
    piece_rows = usable_ref.shape[1] // (spans * pieces)
    ids = lax.broadcasted_iota(jnp.int32, (1, piece_rows), 1)
    for back in range(spans):
        source = jnp.maximum(own_span - back, 0)
        allowed = (mask_ref[own_span, source] > 0) & (own_span >= back)
        limit = jnp.where(allowed, counts_ref[source], 0)
        for piece in range(pieces):
            first = 0
            if pieces == 2:
                first = (own_shard if piece == 0 else 1 - own_shard) * piece_rows
            start = (back * pieces + piece) * piece_rows
            usable_ref[:, start : start + piece_rows] = (first + ids < limit).astype(jnp.int32)
    positions = own_shard * live_ref.shape[0] + lax.broadcasted_iota(jnp.int32, live_ref.shape, 0)
    live_ref[...] = (positions < counts_ref[own_span]).astype(jnp.int32)

    get_gate.wait()
    chosen = lax.broadcasted_iota(jnp.int32, (gate_rows, 1), 0) == level - first_row
    gate = jnp.where(chosen, gate_ref[...].astype(jnp.float32), 0.0)
    gate_row_ref[...] = jnp.sum(gate, axis=0, keepdims=True)


def prepare(levels, span_mask, counts, gate_table, keys, pieces, tokens):
    columns = gate_table.shape[1]
    gate_rows = 16
    return pl.pallas_call(
        functools.partial(prepare_kernel, pieces),
        out_shape=[
            vmem_out((1, keys), jnp.int32),
            vmem_out((tokens, HD), jnp.int32),
            vmem_out((1, columns), jnp.float32),
        ],
        in_specs=[ANY] * 4,
        out_specs=[VMEM] * 3,
        scratch_shapes=[
            pltpu.SMEM(levels.shape, levels.dtype),
            pltpu.SMEM(span_mask.shape, span_mask.dtype),
            pltpu.SMEM(counts.shape, counts.dtype),
            pltpu.VMEM((gate_rows, columns), gate_table.dtype),
            pltpu.SemaphoreType.DMA((4,)),
        ],
        compiler_params=pltpu.CompilerParams(vmem_limit_bytes=VMEM_LIMIT),
        cost_estimate=pl.CostEstimate(
            flops=2 * gate_rows * columns,
            bytes_accessed=2 * gate_rows * columns,
            transcendentals=0,
        ),
        name="prepare",
    )(*[in_hbm(array) for array in (levels, span_mask, counts, gate_table)])


def softmax_block(query, keys, values, usable):
    scores = lax.dot_general(
        query, keys, (((1,), (1,)), ((), ())), preferred_element_type=jnp.float32
    )
    scores = jnp.where(usable, scores, NEG_FILL)
    highest = jnp.max(scores, axis=1, keepdims=True)
    weights = jnp.exp2((scores - highest) * EXP_SCALE)
    totals = jnp.sum(weights, axis=1, keepdims=True)
    summed = jnp.dot(weights.astype(jnp.bfloat16), values, preferred_element_type=jnp.float32)
    return summed / totals


def attend(usable, groups, sharing, row_tile, query_refs, kv_refs, out_ref):
    group_width = groups * HD
    span = sharing * HD
    key_firsts = [r.shape[1] - 2 * group_width for r in kv_refs]
    value_firsts = [r.shape[1] - group_width for r in kv_refs]
    for g in range(groups):
        keys = jnp.concatenate(
            [r[:, a + g * HD : a + (g + 1) * HD] for r, a in zip(kv_refs, key_firsts)], axis=0
        )
        values = jnp.concatenate(
            [r[:, a + g * HD : a + (g + 1) * HD] for r, a in zip(kv_refs, value_firsts)], axis=0
        )
        done = 0
        for query_ref in query_refs:
            rows = query_ref.shape[0]
            for first in range(0, rows, row_tile):
                tile = min(row_tile, rows - first)
                query = jnp.concatenate(
                    [
                        query_ref[first : first + tile, g * span + h * HD : g * span + (h + 1) * HD]
                        for h in range(sharing)
                    ],
                    axis=0,
                )
                result = softmax_block(query, keys, values, usable).astype(jnp.bfloat16)
                for h in range(sharing):
                    out_ref[
                        done + first : done + first + tile,
                        g * span + h * HD : g * span + (h + 1) * HD,
                    ] = result[h * tile : (h + 1) * tile]
            done += rows


def attention_kernel(n_query, n_kv, groups, sharing, row_tile, usable_ref, *refs):
    query_refs, kv_refs, out_ref = refs[:n_query], refs[n_query : n_query + n_kv], refs[-1]
    usable = usable_ref[...] > 0
    attend(usable, groups, sharing, row_tile, query_refs, kv_refs, out_ref)


def attention(usable, query_pieces, kv_pieces, groups, sharing, after):
    rows = sum(p.shape[0] for p in query_pieces)
    keys = usable.shape[1]
    width = groups * sharing * HD
    row_tile = 64
    scores_bytes = 4 * sharing * row_tile * keys
    operands = [usable, *query_pieces, *kv_pieces, *after]
    return pl.pallas_call(
        functools.partial(
            attention_kernel, len(query_pieces), len(kv_pieces), groups, sharing, row_tile
        ),
        out_shape=jax.ShapeDtypeStruct((rows, width), jnp.bfloat16),
        in_specs=[VMEM] * len(operands),
        out_specs=VMEM,
        compiler_params=pltpu.CompilerParams(
            vmem_limit_bytes=max(VMEM_LIMIT, 12 * scores_bytes)
        ),
        cost_estimate=pl.CostEstimate(
            flops=4 * rows * width * keys,
            bytes_accessed=4 * rows * width + 4 * groups * HD * keys,
            transcendentals=rows * keys * groups * sharing,
        ),
        name="attention",
    )(*operands)


def project_kernel(tile, has_own, n_own, n_both, n_after, fetch_first, *refs):
    row_refs, rest = (refs[:2], refs[2:]) if has_own else (refs[:1], refs[1:])
    weight_refs = rest[: n_own + n_both]
    rest = rest[n_own + n_both + n_after :]
    pending = []
    if fetch_first is not None:
        weight_hbm, *rest, sems = rest
        *rest, fetched_ref = rest
        pending = fetch_copies(weight_hbm, fetch_first, [fetched_ref], sems)
    own_ref, other_ref = rest if has_own else (None, *rest)
    for copy in pending:
        copy.start()
    other_rows = other_ref.shape[0]
    both = jnp.concatenate([r[...] for r in row_refs], axis=0)
    own_rows = both.shape[0] - other_rows
    own_done, other_done = 0, 0
    for i, weight_ref in enumerate(weight_refs):
        rows = both[:own_rows] if i < n_own else both
        for first in range(0, weight_ref.shape[1], tile):
            weights = weight_ref[:, first : first + tile]
            product = jnp.dot(rows, weights, preferred_element_type=jnp.float32)
            if own_rows:
                own_ref[:, own_done : own_done + tile] = product[:own_rows]
                own_done += tile
            if i >= n_own:
                part = product[own_rows:].astype(jnp.bfloat16)
                other_ref[:, other_done : other_done + tile] = part
                other_done += tile
    for copy in pending:
        copy.wait()


def project(own, other, own_weights, weights, after, w_out=None, fetch_first=None, fetch_width=0):
    rows, depth = other.shape
    width = sum(w.shape[1] for w in weights)
    own_width = sum(w.shape[1] for w in own_weights) + width
    out_shape = [jax.ShapeDtypeStruct((rows, width), jnp.bfloat16)]
    operands = [other]
    if own is not None:
        out_shape.insert(0, jax.ShapeDtypeStruct((rows, own_width), jnp.float32))
        operands.insert(0, own)
    operands += [in_vmem(w) for w in (*own_weights, *weights)]
    in_specs = [VMEM] * len(operands) + [ANY] * len(after)
    operands += after
    scratch = []
    if fetch_first is not None:
        out_shape.append(vmem_out((depth, fetch_width), w_out.dtype))
        operands.append(in_hbm(w_out))
        in_specs.append(ANY)
        scratch.append(pltpu.SemaphoreType.DMA((FETCH_COPIES,)))
    return pl.pallas_call(
        functools.partial(
            project_kernel,
            512,
            own is not None,
            len(own_weights),
            len(weights),
            len(after),
            fetch_first,
        ),
        out_shape=out_shape,
        in_specs=in_specs,
        out_specs=[VMEM] * len(out_shape),
        scratch_shapes=scratch,
        compiler_params=pltpu.CompilerParams(vmem_limit_bytes=VMEM_LIMIT),
        cost_estimate=pl.CostEstimate(
            flops=2 * rows * depth * (width + (own_width if own is not None else 0)),
            bytes_accessed=2 * depth * own_width,
            transcendentals=0,
        ),
        name="project",
    )(*operands)


def combine_kernel(places, live_ref, gate_ref, *refs):
    other_refs, own_refs, out_ref = refs[: len(places)], refs[len(places) : -1], refs[-1]
    live = live_ref[:, :1] > 0
    first = 0
    for (own, start), other_ref in zip(places, other_refs):
        width = other_ref.shape[1]
        columns = slice(first, first + width)
        total = own_refs[own][:, start : start + width] + other_ref[...].astype(jnp.float32)
        gated = total * gate_ref[:, columns]
        out_ref[:, columns] = jnp.where(live, gated, 0.0).astype(jnp.bfloat16)
        first += width


def combine(live, gate_row, own_parts, other_parts, places):
    rows = own_parts[0].shape[0]
    width = sum(p.shape[1] for p in own_parts)
    return pl.pallas_call(
        functools.partial(combine_kernel, places),
        out_shape=jax.ShapeDtypeStruct((rows, width), jnp.bfloat16),
        in_specs=[VMEM] * (2 + len(own_parts) + len(other_parts)),
        out_specs=VMEM,
        compiler_params=pltpu.CompilerParams(vmem_limit_bytes=VMEM_LIMIT),
        cost_estimate=pl.CostEstimate(
            flops=2 * rows * width, bytes_accessed=8 * rows * width, transcendentals=0
        ),
        name="combine",
    )(live, gate_row, *other_parts, *own_parts)


def send_up(piece, back, first, spans):
    return lax.ppermute(piece, "span", [(i, i + back) for i in range(first, spans - back)])


def local(queries, key_value, w_out, gate_table, levels, span_mask, counts):
    tokens = queries.shape[0]
    shards = lax.axis_size("head")
    spans = lax.axis_size("span")
    head_count = HEADS // shards
    share = HEADS // KV_GROUPS
    sharing = min(share, head_count)
    copies = max(1, share // head_count)
    groups = head_count // sharing
    group_width = groups * HD
    width = head_count * HD
    columns = w_out.shape[1]
    keys = spans * shards * tokens
    small = (levels, span_mask, counts, gate_table)

    if shards == 2:
        swap = [(0, 1), (1, 0)]
        own_kv, sent_kv, own_queries, sent_queries = pair(
            key_value, queries, width, group_width
        )
        usable, live, gate_row = prepare(*small, keys, 2, tokens)
        other_kv, live = lax.optimization_barrier((lax.ppermute(sent_kv, "head", swap), live))
        received = lax.ppermute(sent_queries, "head", swap)
        unit = columns // 12
        fetches = [[units * unit for units in widths] for widths in FETCH_UNITS]
        firsts = [sum(sum(widths) for widths in fetches[:i]) for i in range(len(fetches))]
        *weights, fetched = fetch(w_out, firsts[0], fetches[0], [other_kv])
        own_blocks, other_blocks = [own_kv], [other_kv]
        for pieces in (own_blocks, other_blocks):
            pieces += [send_up(pieces[0], back, 0, spans) for back in range(1, min(spans, 3))]
            for back in range(3, spans):
                pieces[-1], fetched = lax.optimization_barrier((pieces[-1], fetched))
                pieces.append(send_up(pieces[-1], 1, back - 1, spans))
        *more, fetched = fetch(w_out, firsts[1], fetches[1], [fetched, other_blocks[2]])
        weights += more
        blocks = [piece for both in zip(own_blocks, other_blocks) for piece in both]
        def attend_piece(queries, after):
            return attention(usable, [queries], blocks, groups, sharing, after)

        other = attend_piece(received, [fetched])
        early = weights[: len(fetches[0])]
        (sent_0,) = project(None, other, [], early, [])
        part_0 = lax.ppermute(sent_0, "head", swap)
        own = attend_piece(own_queries, [sent_0])
        own_01, sent_1, inner = project(
            own, other, early, weights[len(early) :], [], w_out, firsts[2], fetches[2][0]
        )
        part_1 = lax.ppermute(sent_1, "head", swap)
        late, _ = fetch(w_out, firsts[3], fetches[3], [own_01])
        own_2, sent_2 = project(own, other, [], [inner, late], [part_0])
        part_2 = lax.ppermute(sent_2, "head", swap)
        own_parts, other_parts = [own_01, own_2], [part_0, part_1, part_2]
        places = ((0, 0), (0, part_0.shape[1]), (1, 0))
    else:
        kv_parts = split_all(key_value, shards, group_width, copies)
        swapped = lax.all_to_all(jnp.stack(kv_parts), "head", split_axis=0, concat_axis=0)
        kv_piece = swapped.reshape(shards * tokens, 2 * group_width)
        by_shard = queries.reshape(tokens, shards, width).transpose(1, 0, 2)
        swapped = lax.all_to_all(by_shard, "head", split_axis=0, concat_axis=0)
        query_piece = swapped.reshape(shards * tokens, width)
        blocks = [kv_piece]
        for back in range(1, spans):
            blocks.append(send_up(kv_piece, back, 0, spans))
        usable, live, gate_row = prepare(*small, keys, 1, tokens)
        attended = attention(usable, [query_piece], blocks, groups, sharing, [])
        partial = jnp.dot(attended, w_out, preferred_element_type=jnp.float32)
        summed = lax.psum_scatter(
            partial.astype(jnp.bfloat16), "head", scatter_dimension=0, tiled=True
        )
        own_parts, other_parts = [jnp.zeros(summed.shape, jnp.float32)], [summed]
        places = ((0, 0),)
    return combine(live, gate_row, own_parts, other_parts, places)


def solution(mesh):
    in_specs = (
        P(("rep", "span", "head"), None),
        P(("rep", "span", "head"), None, None),
        P("head", None),
        P(),
        P("rep"),
        P("rep", None),
        P("rep"),
    )
    out_specs = P(("rep", "span", "head"), None)
    return jax.shard_map(local, mesh=mesh, in_specs=in_specs, out_specs=out_specs, check_vma=False)
```

```python
import functools
import math

import jax
import jax.numpy as jnp
from jax import lax
from jax.experimental import pallas as pl
from jax.experimental.pallas import tpu as pltpu
from jax.sharding import PartitionSpec as P

HEADS = 48
HD = 128
KV_GROUPS = 8

NEG_FILL = -1e30
EXP_SCALE = HD ** (-0.5) * math.log2(math.e)
VMEM_LIMIT = 6 * 1024 * 1024

FETCH_COPIES = 8
FETCH_UNITS = ((3,), (4,), (1,), (2,), (2,))
CHUNK_PIECES = ((0, 1), (1, 3), (3, 5))

VMEM = pl.BlockSpec(memory_space=pltpu.VMEM)
ANY = pl.BlockSpec(memory_space=pl.ANY)


def vmem_out(shape, dtype):
    return pltpu.VMEM(shape, dtype)


def hbm_out(shape, dtype):
    return pltpu.HBM(shape, dtype)


def in_vmem(array):
    return pltpu.with_memory_space_constraint(array, pltpu.VMEM)


def in_hbm(array):
    return pltpu.with_memory_space_constraint(array, pltpu.HBM)


def column_starts(width):
    own = lax.axis_index("head")
    return [pl.multiple_of(own * width, HD), pl.multiple_of((1 - own) * width, HD)]


def split_kv(starts, group_width, kv_ref, out_refs):
    for start, out_ref in zip(starts, out_refs):
        first = out_ref.shape[1] - 2 * group_width
        out_ref[:, first : first + group_width] = kv_ref[:, 0, pl.ds(start, group_width)]
        out_ref[:, first + group_width :] = kv_ref[:, 1, pl.ds(start, group_width)]


def pair_kernel(width, group_width, kv_hbm, query_hbm, *refs):
    own_kv_ref, sent_kv_ref, own_ref, sent_ref, kv_ref, sems = refs
    own_start, sent_start = column_starts(width)
    get_kv = pltpu.make_async_copy(kv_hbm, kv_ref, sems.at[0])
    get_queries = [
        pltpu.make_async_copy(query_hbm.at[:, pl.ds(start, width)], ref, sems.at[i + 1])
        for i, (start, ref) in enumerate(((sent_start, sent_ref), (own_start, own_ref)))
    ]
    get_kv.start()
    for copy in get_queries:
        copy.start()
    get_kv.wait()
    starts = column_starts(group_width)
    split_kv(starts, group_width, kv_ref, [own_kv_ref, sent_kv_ref])
    for copy in get_queries:
        copy.wait()


def pair(key_value, queries, width, group_width):
    rows = queries.shape[0]
    widths = [2 * group_width, 2 * group_width, width, width]
    return pl.pallas_call(
        functools.partial(pair_kernel, width, group_width),
        out_shape=[vmem_out((rows, w), queries.dtype) for w in widths],
        in_specs=[ANY, ANY],
        out_specs=[VMEM] * 4,
        scratch_shapes=[
            pltpu.VMEM(key_value.shape, key_value.dtype),
            pltpu.SemaphoreType.DMA((3,)),
        ],
        compiler_params=pltpu.CompilerParams(vmem_limit_bytes=VMEM_LIMIT),
        cost_estimate=pl.CostEstimate(
            flops=0, bytes_accessed=4 * (key_value.size + queries.size), transcendentals=0
        ),
        name="pair",
    )(in_hbm(key_value), in_hbm(queries))


def all_kernel(group_width, copies, kv_ref, *out_refs):
    starts = [piece // copies * group_width for piece in range(len(out_refs))]
    split_kv(starts, group_width, kv_ref, out_refs)


def split_all(key_value, pieces, group_width, copies):
    shape = jax.ShapeDtypeStruct((key_value.shape[0], 2 * group_width), key_value.dtype)
    return pl.pallas_call(
        functools.partial(all_kernel, group_width, copies),
        out_shape=[shape] * pieces,
        in_specs=[VMEM],
        out_specs=[VMEM] * pieces,
        compiler_params=pltpu.CompilerParams(vmem_limit_bytes=VMEM_LIMIT),
        name="split_all",
    )(key_value)


def fetch_copies(weight_hbm, first, out_refs, sems):
    parts = FETCH_COPIES
    copies = []
    for k, out_ref in enumerate(out_refs):
        depth, count = out_ref.shape
        rows = depth // parts
        for i in range(parts):
            part = pl.ds(i * rows, rows)
            copies.append(
                pltpu.make_async_copy(
                    weight_hbm.at[part, pl.ds(first, count)],
                    out_ref.at[part, :],
                    sems.at[k * parts + i],
                )
            )
        first += count
    return copies


def fetch_kernel(first, n_after, weight_hbm, *refs):
    *out_refs, done_ref, sems = refs[n_after:]
    pending = fetch_copies(weight_hbm, first, out_refs, sems)
    for copy in pending:
        copy.start()
    done_ref[...] = jnp.zeros_like(done_ref)
    for copy in pending:
        copy.wait()


def fetch(w_out, first, widths, after):
    depth = w_out.shape[0]
    return pl.pallas_call(
        functools.partial(fetch_kernel, first, len(after)),
        out_shape=[
            *[vmem_out((depth, width), w_out.dtype) for width in widths],
            vmem_out((8, HD), jnp.int32),
        ],
        in_specs=[ANY] * (1 + len(after)),
        out_specs=[VMEM] * (1 + len(widths)),
        scratch_shapes=[pltpu.SemaphoreType.DMA((FETCH_COPIES * len(widths),))],
        compiler_params=pltpu.CompilerParams(vmem_limit_bytes=VMEM_LIMIT),
        cost_estimate=pl.CostEstimate(
            flops=0, bytes_accessed=4 * depth * sum(widths), transcendentals=0
        ),
        name="fetch",
    )(in_hbm(w_out), *after)


def prepare_kernel(pieces, n_after, n_weights, fetch_first, *refs):
    levels_hbm, mask_hbm, counts_hbm, gate_hbm, weight_hbm = refs[:5]
    usable_ref, live_ref, gate_row_ref, *weight_refs = refs[5 + n_after : 8 + n_after + n_weights]
    levels_ref, mask_ref, counts_ref, gate_ref, sems, fetch_sems = refs[8 + n_after + n_weights :]
    pending = fetch_copies(weight_hbm, fetch_first, weight_refs, fetch_sems)
    small = [
        pltpu.make_async_copy(levels_hbm, levels_ref, sems.at[0]),
        pltpu.make_async_copy(mask_hbm, mask_ref, sems.at[1]),
        pltpu.make_async_copy(counts_hbm, counts_ref, sems.at[2]),
    ]
    for copy in small + pending:
        copy.start()
    for copy in small:
        copy.wait()
    own_span, own_shard = lax.axis_index("span"), lax.axis_index("head")
    level = levels_ref[own_span]
    gate_rows = gate_ref.shape[0]
    first_row = pl.multiple_of(level // gate_rows * gate_rows, gate_rows)
    get_gate = pltpu.make_async_copy(
        gate_hbm.at[pl.ds(first_row, gate_rows), :], gate_ref, sems.at[3]
    )
    get_gate.start()

    spans = counts_ref.shape[0]
    piece_rows = usable_ref.shape[1] // (spans * pieces)
    ids = lax.broadcasted_iota(jnp.int32, (1, piece_rows), 1)
    for back in range(spans):
        source = jnp.maximum(own_span - back, 0)
        allowed = (mask_ref[own_span, source] > 0) & (own_span >= back)
        limit = jnp.where(allowed, counts_ref[source], 0)
        for piece in range(pieces):
            first = 0
            if pieces == 2:
                first = (own_shard if piece == 0 else 1 - own_shard) * piece_rows
            start = (back * pieces + piece) * piece_rows
            usable_ref[:, start : start + piece_rows] = (first + ids < limit).astype(jnp.int32)
    positions = own_shard * live_ref.shape[0] + lax.broadcasted_iota(jnp.int32, live_ref.shape, 0)
    live_ref[...] = (positions < counts_ref[own_span]).astype(jnp.int32)

    get_gate.wait()
    chosen = lax.broadcasted_iota(jnp.int32, (gate_rows, 1), 0) == level - first_row
    gate = jnp.where(chosen, gate_ref[...].astype(jnp.float32), 0.0)
    gate_row_ref[...] = jnp.sum(gate, axis=0, keepdims=True)
    for copy in pending:
        copy.wait()


def prepare(levels, span_mask, counts, gate_table, w_out, keys, pieces, tokens, first, widths, after):
    depth = w_out.shape[0]
    columns = gate_table.shape[1]
    gate_rows = 16
    return pl.pallas_call(
        functools.partial(prepare_kernel, pieces, len(after), len(widths), first),
        out_shape=[
            vmem_out((1, keys), jnp.int32),
            vmem_out((tokens, HD), jnp.int32),
            vmem_out((1, columns), jnp.float32),
            *[vmem_out((depth, width), w_out.dtype) for width in widths],
        ],
        in_specs=[ANY] * (5 + len(after)),
        out_specs=[VMEM] * (3 + len(widths)),
        scratch_shapes=[
            pltpu.SMEM(levels.shape, levels.dtype),
            pltpu.SMEM(span_mask.shape, span_mask.dtype),
            pltpu.SMEM(counts.shape, counts.dtype),
            pltpu.VMEM((gate_rows, columns), gate_table.dtype),
            pltpu.SemaphoreType.DMA((4,)),
            pltpu.SemaphoreType.DMA((max(1, FETCH_COPIES * len(widths)),)),
        ],
        compiler_params=pltpu.CompilerParams(vmem_limit_bytes=VMEM_LIMIT),
        cost_estimate=pl.CostEstimate(
            flops=2 * gate_rows * columns,
            bytes_accessed=2 * gate_rows * columns + 4 * depth * sum(widths),
            transcendentals=0,
        ),
        name="prepare",
    )(*[in_hbm(array) for array in (levels, span_mask, counts, gate_table, w_out)], *after)


def softmax_block(query, keys, values, usable):
    scores = lax.dot_general(
        query, keys, (((1,), (1,)), ((), ())), preferred_element_type=jnp.float32
    )
    scores = jnp.where(usable, scores, NEG_FILL)
    highest = jnp.max(scores, axis=1, keepdims=True)
    weights = jnp.exp2((scores - highest) * EXP_SCALE)
    totals = jnp.sum(weights, axis=1, keepdims=True)
    summed = jnp.dot(weights.astype(jnp.bfloat16), values, preferred_element_type=jnp.float32)
    return summed / totals


def attend(usable, groups, sharing, row_tile, query_refs, kv_refs, out_ref):
    group_width = groups * HD
    span = sharing * HD
    key_firsts = [r.shape[1] - 2 * group_width for r in kv_refs]
    value_firsts = [r.shape[1] - group_width for r in kv_refs]
    for g in range(groups):
        keys = jnp.concatenate(
            [r[:, a + g * HD : a + (g + 1) * HD] for r, a in zip(kv_refs, key_firsts)], axis=0
        )
        values = jnp.concatenate(
            [r[:, a + g * HD : a + (g + 1) * HD] for r, a in zip(kv_refs, value_firsts)], axis=0
        )
        done = 0
        for query_ref in query_refs:
            rows = query_ref.shape[0]
            for first in range(0, rows, row_tile):
                tile = min(row_tile, rows - first)
                query = jnp.concatenate(
                    [
                        query_ref[first : first + tile, g * span + h * HD : g * span + (h + 1) * HD]
                        for h in range(sharing)
                    ],
                    axis=0,
                )
                result = softmax_block(query, keys, values, usable).astype(jnp.bfloat16)
                for h in range(sharing):
                    out_ref[
                        done + first : done + first + tile,
                        g * span + h * HD : g * span + (h + 1) * HD,
                    ] = result[h * tile : (h + 1) * tile]
            done += rows


def attention_kernel(n_query, n_kv, groups, sharing, row_tile, usable_ref, *refs):
    query_refs, kv_refs, out_ref = refs[:n_query], refs[n_query : n_query + n_kv], refs[-1]
    usable = usable_ref[...] > 0
    attend(usable, groups, sharing, row_tile, query_refs, kv_refs, out_ref)


def attention(usable, query_pieces, kv_pieces, groups, sharing, after):
    rows = sum(p.shape[0] for p in query_pieces)
    keys = usable.shape[1]
    width = groups * sharing * HD
    row_tile = 64
    scores_bytes = 4 * sharing * row_tile * keys
    operands = [usable, *query_pieces, *kv_pieces, *after]
    return pl.pallas_call(
        functools.partial(
            attention_kernel, len(query_pieces), len(kv_pieces), groups, sharing, row_tile
        ),
        out_shape=jax.ShapeDtypeStruct((rows, width), jnp.bfloat16),
        in_specs=[VMEM] * len(operands),
        out_specs=VMEM,
        compiler_params=pltpu.CompilerParams(
            vmem_limit_bytes=max(VMEM_LIMIT, 12 * scores_bytes)
        ),
        cost_estimate=pl.CostEstimate(
            flops=4 * rows * width * keys,
            bytes_accessed=4 * rows * width + 4 * groups * HD * keys,
            transcendentals=rows * keys * groups * sharing,
        ),
        name="attention",
    )(*operands)


def project_kernel(own_rows, tile, n_weights, n_after, fetch_first, attended_ref, *refs):
    weight_refs = refs[:n_weights]
    rest = refs[n_weights + n_after :]
    pending = []
    if fetch_first is None:
        own_ref, other_ref = rest
    else:
        weight_hbm, own_ref, other_ref, fetched_ref, sems = rest
        pending = fetch_copies(weight_hbm, fetch_first, [fetched_ref], sems)
    for copy in pending:
        copy.start()
    attended = attended_ref[...]
    done = 0
    for weight_ref in weight_refs:
        for first in range(0, weight_ref.shape[1], tile):
            weights = weight_ref[:, first : first + tile]
            product = jnp.dot(attended, weights, preferred_element_type=jnp.float32)
            columns = slice(done + first, done + first + tile)
            own_ref[:, columns] = product[:own_rows]
            other_ref[:, columns] = product[own_rows:].astype(jnp.bfloat16)
        done += weight_ref.shape[1]
    for copy in pending:
        copy.wait()


def project(attended, weights, own_rows, after, w_out=None, fetch_first=None, fetch_width=0):
    rows, depth = attended.shape
    count = sum(w.shape[1] for w in weights)
    other_rows = rows - own_rows
    out_shape = [
        jax.ShapeDtypeStruct((own_rows, count), jnp.float32),
        jax.ShapeDtypeStruct((other_rows, count), jnp.bfloat16),
    ]
    operands = [attended, *[in_vmem(w) for w in weights], *after]
    in_specs = [VMEM] * (1 + len(weights)) + [ANY] * len(after)
    scratch = []
    if fetch_first is not None:
        out_shape.append(vmem_out((depth, fetch_width), w_out.dtype))
        operands.append(in_hbm(w_out))
        in_specs.append(ANY)
        scratch.append(pltpu.SemaphoreType.DMA((FETCH_COPIES,)))
    return pl.pallas_call(
        functools.partial(
            project_kernel, own_rows, 512, len(weights), len(after), fetch_first
        ),
        out_shape=out_shape,
        in_specs=in_specs,
        out_specs=[VMEM] * len(out_shape),
        scratch_shapes=scratch,
        compiler_params=pltpu.CompilerParams(vmem_limit_bytes=VMEM_LIMIT),
        cost_estimate=pl.CostEstimate(
            flops=2 * rows * depth * count, bytes_accessed=2 * depth * count, transcendentals=0
        ),
        name="project",
    )(*operands)


def combine_kernel(first, n_chunks, has_done, live_ref, gate_ref, *refs):
    own_refs, other_refs = refs[:n_chunks], refs[n_chunks : 2 * n_chunks]
    out_hbm, part_ref, sem = refs[2 * n_chunks + has_done :]
    live = live_ref[:, :1] > 0
    start = 0
    for own_ref, other_ref in zip(own_refs, other_refs):
        width = own_ref.shape[1]
        gate = gate_ref[:, first + start : first + start + width]
        gated = (own_ref[...] + other_ref[...].astype(jnp.float32)) * gate
        part_ref[:, start : start + width] = jnp.where(live, gated, 0.0).astype(jnp.bfloat16)
        start += width
    put = pltpu.make_async_copy(part_ref, out_hbm.at[:, pl.ds(first, start)], sem)
    put.start()
    put.wait()


def combine(live, gate_row, own_parts, other_parts, first, done):
    rows = own_parts[0].shape[0]
    width = sum(p.shape[1] for p in own_parts)
    operands = [live, gate_row, *own_parts, *other_parts]
    return pl.pallas_call(
        functools.partial(combine_kernel, first, len(own_parts), len(done)),
        out_shape=hbm_out((rows, gate_row.shape[1]), jnp.bfloat16),
        in_specs=[VMEM] * len(operands) + [ANY] * len(done),
        out_specs=ANY,
        input_output_aliases={len(operands): 0} if done else {},
        scratch_shapes=[pltpu.VMEM((rows, width), jnp.bfloat16), pltpu.SemaphoreType.DMA],
        compiler_params=pltpu.CompilerParams(vmem_limit_bytes=VMEM_LIMIT),
        cost_estimate=pl.CostEstimate(
            flops=2 * rows * width, bytes_accessed=8 * rows * width, transcendentals=0
        ),
        name="combine",
    )(*operands, *[in_hbm(array) for array in done])


def send_up(piece, back, first, spans):
    return lax.ppermute(piece, "span", [(i, i + back) for i in range(first, spans - back)])


def local(queries, key_value, w_out, gate_table, levels, span_mask, counts):
    tokens = queries.shape[0]
    shards = lax.axis_size("head")
    spans = lax.axis_size("span")
    head_count = HEADS // shards
    share = HEADS // KV_GROUPS
    sharing = min(share, head_count)
    copies = max(1, share // head_count)
    groups = head_count // sharing
    group_width = groups * HD
    width = head_count * HD
    columns = w_out.shape[1]
    keys = spans * shards * tokens
    small = (levels, span_mask, counts, gate_table, w_out)

    if shards == 2:
        swap = [(0, 1), (1, 0)]
        own_kv, sent_kv, own_queries, sent_queries = pair(
            key_value, queries, width, group_width
        )
        other_kv = lax.ppermute(sent_kv, "head", swap)
        received = lax.ppermute(sent_queries, "head", swap)
        unit = columns // 12
        fetches = [[units * unit for units in widths] for widths in FETCH_UNITS]
        firsts = [sum(sum(widths) for widths in fetches[:i]) for i in range(len(fetches))]
        *weights, fetched = fetch(w_out, firsts[0], fetches[0], [other_kv])
        own_blocks, other_blocks = [own_kv], [other_kv]
        for pieces in (own_blocks, other_blocks):
            pieces += [send_up(pieces[0], back, 0, spans) for back in range(1, min(spans, 3))]
            for back in range(3, spans):
                pieces[-1], fetched = lax.optimization_barrier((pieces[-1], fetched))
                pieces.append(send_up(pieces[-1], 1, back - 1, spans))
        usable, live, gate_row, *more = prepare(
            *small, keys, 2, tokens, firsts[1], fetches[1], [fetched, other_blocks[2]]
        )
        weights += more
        blocks = [piece for both in zip(own_blocks, other_blocks) for piece in both]
        attended = attention(usable, [own_queries, received], blocks, groups, sharing, [])
        own_parts, other_parts = [], []
        for chunk, (first, last) in enumerate(CHUNK_PIECES):
            if chunk < len(CHUNK_PIECES) - 1:
                step = chunk + 2
                more = (w_out, firsts[step], sum(fetches[step]))
            else:
                *late, _ = fetch(w_out, firsts[-1], fetches[-1], own_parts[-1:])
                weights += late
                more = ()
            after = other_parts[chunk - 2 : chunk - 1] if chunk >= 2 else []
            own, other, *fetched = project(attended, weights[first:last], tokens, after, *more)
            weights += fetched
            own_parts.append(own)
            other_parts.append(lax.ppermute(other, "head", swap))
    else:
        kv_parts = split_all(key_value, shards, group_width, copies)
        swapped = lax.all_to_all(jnp.stack(kv_parts), "head", split_axis=0, concat_axis=0)
        kv_piece = swapped.reshape(shards * tokens, 2 * group_width)
        by_shard = queries.reshape(tokens, shards, width).transpose(1, 0, 2)
        swapped = lax.all_to_all(by_shard, "head", split_axis=0, concat_axis=0)
        query_piece = swapped.reshape(shards * tokens, width)
        blocks = [kv_piece]
        for back in range(1, spans):
            blocks.append(send_up(kv_piece, back, 0, spans))
        usable, live, gate_row = prepare(*small, keys, 1, tokens, 0, [], [])
        attended = attention(usable, [query_piece], blocks, groups, sharing, [])
        partial = jnp.dot(attended, w_out, preferred_element_type=jnp.float32)
        summed = lax.psum_scatter(
            partial.astype(jnp.bfloat16), "head", scatter_dimension=0, tiled=True
        )
        own_parts, other_parts = [jnp.zeros(summed.shape, jnp.float32)], [summed]
    done, first = [], 0
    if len(own_parts) > 1:
        done = [combine(live, gate_row, own_parts[:-1], other_parts[:-1], 0, [])]
        first = sum(part.shape[1] for part in own_parts[:-1])
    return combine(live, gate_row, own_parts[-1:], other_parts[-1:], first, done)


def solution(mesh):
    in_specs = (
        P(("rep", "span", "head"), None),
        P(("rep", "span", "head"), None, None),
        P("head", None),
        P(),
        P("rep"),
        P("rep", None),
        P("rep"),
    )
    out_specs = P(("rep", "span", "head"), None)
    return jax.shard_map(local, mesh=mesh, in_specs=in_specs, out_specs=out_specs, check_vma=False)
```

```python
import functools
import math

import jax
import jax.numpy as jnp
from jax import lax
from jax.experimental import pallas as pl
from jax.experimental.pallas import tpu as pltpu
from jax.sharding import PartitionSpec as P

HEADS = 48
HD = 128
KV_GROUPS = 8

NEG_FILL = -1e30
EXP_SCALE = HD ** (-0.5) * math.log2(math.e)
VMEM_LIMIT = 6 * 1024 * 1024

FETCH_COPIES = 8
FETCH_UNITS = ((3,), (4,), (1,), (2,), (2,))
CHUNK_PIECES = ((0, 1), (1, 3), (3, 5))

VMEM = pl.BlockSpec(memory_space=pltpu.VMEM)
ANY = pl.BlockSpec(memory_space=pl.ANY)


def vmem_out(shape, dtype):
    return pltpu.VMEM(shape, dtype)


def hbm_out(shape, dtype):
    return pltpu.HBM(shape, dtype)


def in_vmem(array):
    return pltpu.with_memory_space_constraint(array, pltpu.VMEM)


def in_hbm(array):
    return pltpu.with_memory_space_constraint(array, pltpu.HBM)


def column_starts(width):
    own = lax.axis_index("head")
    return [pl.multiple_of(own * width, HD), pl.multiple_of((1 - own) * width, HD)]


def split_kv(starts, group_width, kv_ref, out_refs):
    for start, out_ref in zip(starts, out_refs):
        first = out_ref.shape[1] - 2 * group_width
        out_ref[:, first : first + group_width] = kv_ref[:, 0, pl.ds(start, group_width)]
        out_ref[:, first + group_width :] = kv_ref[:, 1, pl.ds(start, group_width)]


def pair_kernel(width, group_width, kv_hbm, query_hbm, *refs):
    own_kv_ref, sent_kv_ref, own_ref, sent_ref, kv_ref, sems = refs
    own_start, sent_start = column_starts(width)
    get_kv = pltpu.make_async_copy(kv_hbm, kv_ref, sems.at[0])
    get_queries = [
        pltpu.make_async_copy(query_hbm.at[:, pl.ds(start, width)], ref, sems.at[i + 1])
        for i, (start, ref) in enumerate(((sent_start, sent_ref), (own_start, own_ref)))
    ]
    get_kv.start()
    for copy in get_queries:
        copy.start()
    get_kv.wait()
    starts = column_starts(group_width)
    split_kv(starts, group_width, kv_ref, [own_kv_ref, sent_kv_ref])
    for copy in get_queries:
        copy.wait()


def pair(key_value, queries, width, group_width):
    rows = queries.shape[0]
    widths = [2 * group_width, 2 * group_width, width, width]
    return pl.pallas_call(
        functools.partial(pair_kernel, width, group_width),
        out_shape=[vmem_out((rows, w), queries.dtype) for w in widths],
        in_specs=[ANY, ANY],
        out_specs=[VMEM] * 4,
        scratch_shapes=[
            pltpu.VMEM(key_value.shape, key_value.dtype),
            pltpu.SemaphoreType.DMA((3,)),
        ],
        compiler_params=pltpu.CompilerParams(vmem_limit_bytes=VMEM_LIMIT),
        cost_estimate=pl.CostEstimate(
            flops=0, bytes_accessed=4 * (key_value.size + queries.size), transcendentals=0
        ),
        name="pair",
    )(in_hbm(key_value), in_hbm(queries))


def all_kernel(group_width, copies, kv_ref, *out_refs):
    starts = [piece // copies * group_width for piece in range(len(out_refs))]
    split_kv(starts, group_width, kv_ref, out_refs)


def split_all(key_value, pieces, group_width, copies):
    shape = jax.ShapeDtypeStruct((key_value.shape[0], 2 * group_width), key_value.dtype)
    return pl.pallas_call(
        functools.partial(all_kernel, group_width, copies),
        out_shape=[shape] * pieces,
        in_specs=[VMEM],
        out_specs=[VMEM] * pieces,
        compiler_params=pltpu.CompilerParams(vmem_limit_bytes=VMEM_LIMIT),
        name="split_all",
    )(key_value)


def fetch_copies(weight_hbm, first, out_refs, sems):
    parts = FETCH_COPIES
    copies = []
    for k, out_ref in enumerate(out_refs):
        depth, count = out_ref.shape
        rows = depth // parts
        for i in range(parts):
            part = pl.ds(i * rows, rows)
            copies.append(
                pltpu.make_async_copy(
                    weight_hbm.at[part, pl.ds(first, count)],
                    out_ref.at[part, :],
                    sems.at[k * parts + i],
                )
            )
        first += count
    return copies


def fetch_kernel(first, n_after, weight_hbm, *refs):
    *out_refs, done_ref, sems = refs[n_after:]
    pending = fetch_copies(weight_hbm, first, out_refs, sems)
    for copy in pending:
        copy.start()
    done_ref[...] = jnp.zeros_like(done_ref)
    for copy in pending:
        copy.wait()


def fetch(w_out, first, widths, after):
    depth = w_out.shape[0]
    return pl.pallas_call(
        functools.partial(fetch_kernel, first, len(after)),
        out_shape=[
            *[vmem_out((depth, width), w_out.dtype) for width in widths],
            vmem_out((8, HD), jnp.int32),
        ],
        in_specs=[ANY] * (1 + len(after)),
        out_specs=[VMEM] * (1 + len(widths)),
        scratch_shapes=[pltpu.SemaphoreType.DMA((FETCH_COPIES * len(widths),))],
        compiler_params=pltpu.CompilerParams(vmem_limit_bytes=VMEM_LIMIT),
        cost_estimate=pl.CostEstimate(
            flops=0, bytes_accessed=4 * depth * sum(widths), transcendentals=0
        ),
        name="fetch",
    )(in_hbm(w_out), *after)


def prepare_kernel(pieces, n_after, n_weights, fetch_first, *refs):
    levels_hbm, mask_hbm, counts_hbm, gate_hbm, weight_hbm = refs[:5]
    usable_ref, live_ref, gate_row_ref, *weight_refs = refs[5 + n_after : 8 + n_after + n_weights]
    levels_ref, mask_ref, counts_ref, gate_ref, sems, fetch_sems = refs[8 + n_after + n_weights :]
    pending = fetch_copies(weight_hbm, fetch_first, weight_refs, fetch_sems)
    small = [
        pltpu.make_async_copy(levels_hbm, levels_ref, sems.at[0]),
        pltpu.make_async_copy(mask_hbm, mask_ref, sems.at[1]),
        pltpu.make_async_copy(counts_hbm, counts_ref, sems.at[2]),
    ]
    for copy in small + pending:
        copy.start()
    for copy in small:
        copy.wait()
    own_span, own_shard = lax.axis_index("span"), lax.axis_index("head")
    level = levels_ref[own_span]
    gate_rows = gate_ref.shape[0]
    first_row = pl.multiple_of(level // gate_rows * gate_rows, gate_rows)
    get_gate = pltpu.make_async_copy(
        gate_hbm.at[pl.ds(first_row, gate_rows), :], gate_ref, sems.at[3]
    )
    get_gate.start()

    spans = counts_ref.shape[0]
    piece_rows = usable_ref.shape[1] // (spans * pieces)
    ids = lax.broadcasted_iota(jnp.int32, (1, piece_rows), 1)
    for back in range(spans):
        source = jnp.maximum(own_span - back, 0)
        allowed = (mask_ref[own_span, source] > 0) & (own_span >= back)
        limit = jnp.where(allowed, counts_ref[source], 0)
        for piece in range(pieces):
            first = 0
            if pieces == 2:
                first = (own_shard if piece == 0 else 1 - own_shard) * piece_rows
            start = (back * pieces + piece) * piece_rows
            usable_ref[:, start : start + piece_rows] = (first + ids < limit).astype(jnp.int32)
    positions = own_shard * live_ref.shape[0] + lax.broadcasted_iota(jnp.int32, live_ref.shape, 0)
    live_ref[...] = (positions < counts_ref[own_span]).astype(jnp.int32)

    get_gate.wait()
    chosen = lax.broadcasted_iota(jnp.int32, (gate_rows, 1), 0) == level - first_row
    gate = jnp.where(chosen, gate_ref[...].astype(jnp.float32), 0.0)
    gate_row_ref[...] = jnp.sum(gate, axis=0, keepdims=True)
    for copy in pending:
        copy.wait()


def prepare(levels, span_mask, counts, gate_table, w_out, keys, pieces, tokens, first, widths, after):
    depth = w_out.shape[0]
    columns = gate_table.shape[1]
    gate_rows = 16
    return pl.pallas_call(
        functools.partial(prepare_kernel, pieces, len(after), len(widths), first),
        out_shape=[
            vmem_out((1, keys), jnp.int32),
            vmem_out((tokens, HD), jnp.int32),
            vmem_out((1, columns), jnp.float32),
            *[vmem_out((depth, width), w_out.dtype) for width in widths],
        ],
        in_specs=[ANY] * (5 + len(after)),
        out_specs=[VMEM] * (3 + len(widths)),
        scratch_shapes=[
            pltpu.SMEM(levels.shape, levels.dtype),
            pltpu.SMEM(span_mask.shape, span_mask.dtype),
            pltpu.SMEM(counts.shape, counts.dtype),
            pltpu.VMEM((gate_rows, columns), gate_table.dtype),
            pltpu.SemaphoreType.DMA((4,)),
            pltpu.SemaphoreType.DMA((max(1, FETCH_COPIES * len(widths)),)),
        ],
        compiler_params=pltpu.CompilerParams(vmem_limit_bytes=VMEM_LIMIT),
        cost_estimate=pl.CostEstimate(
            flops=2 * gate_rows * columns,
            bytes_accessed=2 * gate_rows * columns + 4 * depth * sum(widths),
            transcendentals=0,
        ),
        name="prepare",
    )(*[in_hbm(array) for array in (levels, span_mask, counts, gate_table, w_out)], *after)


def softmax_block(query, keys, values, usable):
    scores = lax.dot_general(
        query, keys, (((1,), (1,)), ((), ())), preferred_element_type=jnp.float32
    )
    scores = jnp.where(usable, scores, NEG_FILL)
    highest = jnp.max(scores, axis=1, keepdims=True)
    weights = jnp.exp2((scores - highest) * EXP_SCALE)
    totals = jnp.sum(weights, axis=1, keepdims=True)
    summed = jnp.dot(weights.astype(jnp.bfloat16), values, preferred_element_type=jnp.float32)
    return summed / totals


def attend(usable, groups, sharing, row_tile, query_refs, kv_refs, out_ref):
    group_width = groups * HD
    span = sharing * HD
    key_firsts = [r.shape[1] - 2 * group_width for r in kv_refs]
    value_firsts = [r.shape[1] - group_width for r in kv_refs]
    for g in range(groups):
        keys = jnp.concatenate(
            [r[:, a + g * HD : a + (g + 1) * HD] for r, a in zip(kv_refs, key_firsts)], axis=0
        )
        values = jnp.concatenate(
            [r[:, a + g * HD : a + (g + 1) * HD] for r, a in zip(kv_refs, value_firsts)], axis=0
        )
        done = 0
        for query_ref in query_refs:
            rows = query_ref.shape[0]
            for first in range(0, rows, row_tile):
                tile = min(row_tile, rows - first)
                query = jnp.concatenate(
                    [
                        query_ref[first : first + tile, g * span + h * HD : g * span + (h + 1) * HD]
                        for h in range(sharing)
                    ],
                    axis=0,
                )
                result = softmax_block(query, keys, values, usable).astype(jnp.bfloat16)
                for h in range(sharing):
                    out_ref[
                        done + first : done + first + tile,
                        g * span + h * HD : g * span + (h + 1) * HD,
                    ] = result[h * tile : (h + 1) * tile]
            done += rows


def attention_kernel(n_query, n_kv, groups, sharing, row_tile, usable_ref, *refs):
    query_refs, kv_refs, out_ref = refs[:n_query], refs[n_query : n_query + n_kv], refs[-1]
    usable = usable_ref[...] > 0
    attend(usable, groups, sharing, row_tile, query_refs, kv_refs, out_ref)


def attention(usable, query_pieces, kv_pieces, groups, sharing, after):
    rows = sum(p.shape[0] for p in query_pieces)
    keys = usable.shape[1]
    width = groups * sharing * HD
    row_tile = 64
    scores_bytes = 4 * sharing * row_tile * keys
    operands = [usable, *query_pieces, *kv_pieces, *after]
    return pl.pallas_call(
        functools.partial(
            attention_kernel, len(query_pieces), len(kv_pieces), groups, sharing, row_tile
        ),
        out_shape=jax.ShapeDtypeStruct((rows, width), jnp.bfloat16),
        in_specs=[VMEM] * len(operands),
        out_specs=VMEM,
        compiler_params=pltpu.CompilerParams(
            vmem_limit_bytes=max(VMEM_LIMIT, 12 * scores_bytes)
        ),
        cost_estimate=pl.CostEstimate(
            flops=4 * rows * width * keys,
            bytes_accessed=4 * rows * width + 4 * groups * HD * keys,
            transcendentals=rows * keys * groups * sharing,
        ),
        name="attention",
    )(*operands)


def project_kernel(own_rows, tile, n_weights, n_after, fetch_first, attended_ref, *refs):
    weight_refs = refs[:n_weights]
    rest = refs[n_weights + n_after :]
    pending = []
    if fetch_first is None:
        own_ref, other_ref = rest
    else:
        weight_hbm, own_ref, other_ref, fetched_ref, sems = rest
        pending = fetch_copies(weight_hbm, fetch_first, [fetched_ref], sems)
    for copy in pending:
        copy.start()
    attended = attended_ref[...]
    done = 0
    for weight_ref in weight_refs:
        for first in range(0, weight_ref.shape[1], tile):
            weights = weight_ref[:, first : first + tile]
            product = jnp.dot(attended, weights, preferred_element_type=jnp.float32)
            columns = slice(done + first, done + first + tile)
            own_ref[:, columns] = product[:own_rows]
            other_ref[:, columns] = product[own_rows:].astype(jnp.bfloat16)
        done += weight_ref.shape[1]
    for copy in pending:
        copy.wait()


def project(attended, weights, own_rows, after, w_out=None, fetch_first=None, fetch_width=0):
    rows, depth = attended.shape
    count = sum(w.shape[1] for w in weights)
    other_rows = rows - own_rows
    out_shape = [
        jax.ShapeDtypeStruct((own_rows, count), jnp.float32),
        jax.ShapeDtypeStruct((other_rows, count), jnp.bfloat16),
    ]
    operands = [attended, *[in_vmem(w) for w in weights], *after]
    in_specs = [VMEM] * (1 + len(weights)) + [ANY] * len(after)
    scratch = []
    if fetch_first is not None:
        out_shape.append(vmem_out((depth, fetch_width), w_out.dtype))
        operands.append(in_hbm(w_out))
        in_specs.append(ANY)
        scratch.append(pltpu.SemaphoreType.DMA((FETCH_COPIES,)))
    return pl.pallas_call(
        functools.partial(
            project_kernel, own_rows, 512, len(weights), len(after), fetch_first
        ),
        out_shape=out_shape,
        in_specs=in_specs,
        out_specs=[VMEM] * len(out_shape),
        scratch_shapes=scratch,
        compiler_params=pltpu.CompilerParams(vmem_limit_bytes=VMEM_LIMIT),
        cost_estimate=pl.CostEstimate(
            flops=2 * rows * depth * count, bytes_accessed=2 * depth * count, transcendentals=0
        ),
        name="project",
    )(*operands)


def combine_kernel(first, n_chunks, has_done, live_ref, gate_ref, *refs):
    own_refs, other_refs = refs[:n_chunks], refs[n_chunks : 2 * n_chunks]
    out_hbm, part_ref, sem = refs[2 * n_chunks + has_done :]
    live = live_ref[:, :1] > 0
    start = 0
    for own_ref, other_ref in zip(own_refs, other_refs):
        width = own_ref.shape[1]
        gate = gate_ref[:, first + start : first + start + width]
        gated = (own_ref[...] + other_ref[...].astype(jnp.float32)) * gate
        part_ref[:, start : start + width] = jnp.where(live, gated, 0.0).astype(jnp.bfloat16)
        start += width
    put = pltpu.make_async_copy(part_ref, out_hbm.at[:, pl.ds(first, start)], sem)
    put.start()
    put.wait()


def combine(live, gate_row, own_parts, other_parts, first, done):
    rows = own_parts[0].shape[0]
    width = sum(p.shape[1] for p in own_parts)
    operands = [live, gate_row, *own_parts, *other_parts]
    return pl.pallas_call(
        functools.partial(combine_kernel, first, len(own_parts), len(done)),
        out_shape=hbm_out((rows, gate_row.shape[1]), jnp.bfloat16),
        in_specs=[VMEM] * len(operands) + [ANY] * len(done),
        out_specs=ANY,
        input_output_aliases={len(operands): 0} if done else {},
        scratch_shapes=[pltpu.VMEM((rows, width), jnp.bfloat16), pltpu.SemaphoreType.DMA],
        compiler_params=pltpu.CompilerParams(vmem_limit_bytes=VMEM_LIMIT),
        cost_estimate=pl.CostEstimate(
            flops=2 * rows * width, bytes_accessed=8 * rows * width, transcendentals=0
        ),
        name="combine",
    )(*operands, *[in_hbm(array) for array in done])


def send_up(piece, back, first, spans):
    return lax.ppermute(piece, "span", [(i, i + back) for i in range(first, spans - back)])


def local(queries, key_value, w_out, gate_table, levels, span_mask, counts):
    tokens = queries.shape[0]
    shards = lax.axis_size("head")
    spans = lax.axis_size("span")
    head_count = HEADS // shards
    share = HEADS // KV_GROUPS
    sharing = min(share, head_count)
    copies = max(1, share // head_count)
    groups = head_count // sharing
    group_width = groups * HD
    width = head_count * HD
    columns = w_out.shape[1]
    keys = spans * shards * tokens
    small = (levels, span_mask, counts, gate_table, w_out)

    if shards == 2:
        swap = [(0, 1), (1, 0)]
        own_kv, sent_kv, own_queries, sent_queries = pair(
            key_value, queries, width, group_width
        )
        other_kv = lax.ppermute(sent_kv, "head", swap)
        received = lax.ppermute(sent_queries, "head", swap)
        unit = columns // 12
        fetches = [[units * unit for units in widths] for widths in FETCH_UNITS]
        firsts = [sum(sum(widths) for widths in fetches[:i]) for i in range(len(fetches))]
        *weights, fetched = fetch(w_out, firsts[0], fetches[0], [other_kv])
        own_blocks, other_blocks = [own_kv], [other_kv]
        for pieces in (own_blocks, other_blocks):
            pieces += [send_up(pieces[0], back, 0, spans) for back in range(1, min(spans, 3))]
            for back in range(3, spans):
                pieces[-1], fetched = lax.optimization_barrier((pieces[-1], fetched))
                pieces.append(send_up(pieces[-1], 1, back - 1, spans))
        usable, live, gate_row, *more = prepare(
            *small, keys, 2, tokens, firsts[1], fetches[1], [fetched, other_blocks[1], other_blocks[2]]
        )
        weights += more
        blocks = [piece for both in zip(own_blocks, other_blocks) for piece in both]
        attended = attention(usable, [own_queries, received], blocks, groups, sharing, [])
        own_parts, other_parts = [], []
        for chunk, (first, last) in enumerate(CHUNK_PIECES):
            if chunk < len(CHUNK_PIECES) - 1:
                step = chunk + 2
                more = (w_out, firsts[step], sum(fetches[step]))
            else:
                *late, _ = fetch(w_out, firsts[-1], fetches[-1], own_parts[-1:])
                weights += late
                more = ()
            after = other_parts[chunk - 2 : chunk - 1] if chunk >= 2 else []
            own, other, *fetched = project(attended, weights[first:last], tokens, after, *more)
            weights += fetched
            own_parts.append(own)
            other_parts.append(lax.ppermute(other, "head", swap))
    else:
        kv_parts = split_all(key_value, shards, group_width, copies)
        swapped = lax.all_to_all(jnp.stack(kv_parts), "head", split_axis=0, concat_axis=0)
        kv_piece = swapped.reshape(shards * tokens, 2 * group_width)
        by_shard = queries.reshape(tokens, shards, width).transpose(1, 0, 2)
        swapped = lax.all_to_all(by_shard, "head", split_axis=0, concat_axis=0)
        query_piece = swapped.reshape(shards * tokens, width)
        blocks = [kv_piece]
        for back in range(1, spans):
            blocks.append(send_up(kv_piece, back, 0, spans))
        usable, live, gate_row = prepare(*small, keys, 1, tokens, 0, [], [])
        attended = attention(usable, [query_piece], blocks, groups, sharing, [])
        partial = jnp.dot(attended, w_out, preferred_element_type=jnp.float32)
        summed = lax.psum_scatter(
            partial.astype(jnp.bfloat16), "head", scatter_dimension=0, tiled=True
        )
        own_parts, other_parts = [jnp.zeros(summed.shape, jnp.float32)], [summed]
    done, first = [], 0
    if len(own_parts) > 1:
        done = [combine(live, gate_row, own_parts[:-1], other_parts[:-1], 0, [])]
        first = sum(part.shape[1] for part in own_parts[:-1])
    return combine(live, gate_row, own_parts[-1:], other_parts[-1:], first, done)


def solution(mesh):
    in_specs = (
        P(("rep", "span", "head"), None),
        P(("rep", "span", "head"), None, None),
        P("head", None),
        P(),
        P("rep"),
        P("rep", None),
        P("rep"),
    )
    out_specs = P(("rep", "span", "head"), None)
    return jax.shard_map(local, mesh=mesh, in_specs=in_specs, out_specs=out_specs, check_vma=False)
```

```python
import functools
import math

import jax
import jax.numpy as jnp
from jax import lax
from jax.experimental import pallas as pl
from jax.experimental.pallas import tpu as pltpu
from jax.sharding import PartitionSpec as P

HEADS = 48
HD = 128
KV_GROUPS = 8

NEG_FILL = -1e30
EXP_SCALE = HD ** (-0.5) * math.log2(math.e)
VMEM_LIMIT = 6 * 1024 * 1024

FETCH_COPIES = 8
FETCH_UNITS = ((3,), (4,), (1,), (2,), (2,))
CHUNK_PIECES = ((0, 1), (1, 3), (3, 5))

VMEM = pl.BlockSpec(memory_space=pltpu.VMEM)
ANY = pl.BlockSpec(memory_space=pl.ANY)


def vmem_out(shape, dtype):
    return pltpu.VMEM(shape, dtype)


def hbm_out(shape, dtype):
    return pltpu.HBM(shape, dtype)


def in_vmem(array):
    return pltpu.with_memory_space_constraint(array, pltpu.VMEM)


def in_hbm(array):
    return pltpu.with_memory_space_constraint(array, pltpu.HBM)


def column_starts(width):
    own = lax.axis_index("head")
    return [pl.multiple_of(own * width, HD), pl.multiple_of((1 - own) * width, HD)]


def split_kv(starts, group_width, kv_ref, out_refs):
    for start, out_ref in zip(starts, out_refs):
        first = out_ref.shape[1] - 2 * group_width
        out_ref[:, first : first + group_width] = kv_ref[:, 0, pl.ds(start, group_width)]
        out_ref[:, first + group_width :] = kv_ref[:, 1, pl.ds(start, group_width)]


def pair_kernel(width, group_width, kv_hbm, query_hbm, *refs):
    own_kv_ref, sent_kv_ref, own_ref, sent_ref, kv_ref, sems = refs
    own_start, sent_start = column_starts(width)
    get_kv = pltpu.make_async_copy(kv_hbm, kv_ref, sems.at[0])
    get_queries = [
        pltpu.make_async_copy(query_hbm.at[:, pl.ds(start, width)], ref, sems.at[i + 1])
        for i, (start, ref) in enumerate(((sent_start, sent_ref), (own_start, own_ref)))
    ]
    get_kv.start()
    for copy in get_queries:
        copy.start()
    get_kv.wait()
    starts = column_starts(group_width)
    split_kv(starts, group_width, kv_ref, [own_kv_ref, sent_kv_ref])
    for copy in get_queries:
        copy.wait()


def pair(key_value, queries, width, group_width):
    rows = queries.shape[0]
    widths = [2 * group_width, 2 * group_width, width, width]
    return pl.pallas_call(
        functools.partial(pair_kernel, width, group_width),
        out_shape=[vmem_out((rows, w), queries.dtype) for w in widths],
        in_specs=[ANY, ANY],
        out_specs=[VMEM] * 4,
        scratch_shapes=[
            pltpu.VMEM(key_value.shape, key_value.dtype),
            pltpu.SemaphoreType.DMA((3,)),
        ],
        compiler_params=pltpu.CompilerParams(vmem_limit_bytes=VMEM_LIMIT),
        cost_estimate=pl.CostEstimate(
            flops=0, bytes_accessed=4 * (key_value.size + queries.size), transcendentals=0
        ),
        name="pair",
    )(in_hbm(key_value), in_hbm(queries))


def all_kernel(group_width, copies, kv_ref, *out_refs):
    starts = [piece // copies * group_width for piece in range(len(out_refs))]
    split_kv(starts, group_width, kv_ref, out_refs)


def split_all(key_value, pieces, group_width, copies):
    shape = jax.ShapeDtypeStruct((key_value.shape[0], 2 * group_width), key_value.dtype)
    return pl.pallas_call(
        functools.partial(all_kernel, group_width, copies),
        out_shape=[shape] * pieces,
        in_specs=[VMEM],
        out_specs=[VMEM] * pieces,
        compiler_params=pltpu.CompilerParams(vmem_limit_bytes=VMEM_LIMIT),
        name="split_all",
    )(key_value)


def fetch_copies(weight_hbm, first, out_refs, sems):
    parts = FETCH_COPIES
    copies = []
    for k, out_ref in enumerate(out_refs):
        depth, count = out_ref.shape
        rows = depth // parts
        for i in range(parts):
            part = pl.ds(i * rows, rows)
            copies.append(
                pltpu.make_async_copy(
                    weight_hbm.at[part, pl.ds(first, count)],
                    out_ref.at[part, :],
                    sems.at[k * parts + i],
                )
            )
        first += count
    return copies


def fetch_kernel(first, n_after, weight_hbm, *refs):
    *out_refs, done_ref, sems = refs[n_after:]
    pending = fetch_copies(weight_hbm, first, out_refs, sems)
    for copy in pending:
        copy.start()
    done_ref[...] = jnp.zeros_like(done_ref)
    for copy in pending:
        copy.wait()


def fetch(w_out, first, widths, after):
    depth = w_out.shape[0]
    return pl.pallas_call(
        functools.partial(fetch_kernel, first, len(after)),
        out_shape=[
            *[vmem_out((depth, width), w_out.dtype) for width in widths],
            vmem_out((8, HD), jnp.int32),
        ],
        in_specs=[ANY] * (1 + len(after)),
        out_specs=[VMEM] * (1 + len(widths)),
        scratch_shapes=[pltpu.SemaphoreType.DMA((FETCH_COPIES * len(widths),))],
        compiler_params=pltpu.CompilerParams(vmem_limit_bytes=VMEM_LIMIT),
        cost_estimate=pl.CostEstimate(
            flops=0, bytes_accessed=4 * depth * sum(widths), transcendentals=0
        ),
        name="fetch",
    )(in_hbm(w_out), *after)


def prepare_kernel(pieces, n_after, n_weights, fetch_first, *refs):
    levels_hbm, mask_hbm, counts_hbm, gate_hbm, weight_hbm = refs[:5]
    usable_ref, live_ref, gate_row_ref, *weight_refs = refs[5 + n_after : 8 + n_after + n_weights]
    levels_ref, mask_ref, counts_ref, gate_ref, sems, fetch_sems = refs[8 + n_after + n_weights :]
    pending = fetch_copies(weight_hbm, fetch_first, weight_refs, fetch_sems)
    small = [
        pltpu.make_async_copy(levels_hbm, levels_ref, sems.at[0]),
        pltpu.make_async_copy(mask_hbm, mask_ref, sems.at[1]),
        pltpu.make_async_copy(counts_hbm, counts_ref, sems.at[2]),
    ]
    for copy in small + pending:
        copy.start()
    for copy in small:
        copy.wait()
    own_span, own_shard = lax.axis_index("span"), lax.axis_index("head")
    level = levels_ref[own_span]
    gate_rows = gate_ref.shape[0]
    first_row = pl.multiple_of(level // gate_rows * gate_rows, gate_rows)
    get_gate = pltpu.make_async_copy(
        gate_hbm.at[pl.ds(first_row, gate_rows), :], gate_ref, sems.at[3]
    )
    get_gate.start()

    spans = counts_ref.shape[0]
    piece_rows = usable_ref.shape[1] // (spans * pieces)
    ids = lax.broadcasted_iota(jnp.int32, (1, piece_rows), 1)
    for back in range(spans):
        source = jnp.maximum(own_span - back, 0)
        allowed = (mask_ref[own_span, source] > 0) & (own_span >= back)
        limit = jnp.where(allowed, counts_ref[source], 0)
        for piece in range(pieces):
            first = 0
            if pieces == 2:
                first = (own_shard if piece == 0 else 1 - own_shard) * piece_rows
            start = (back * pieces + piece) * piece_rows
            usable_ref[:, start : start + piece_rows] = (first + ids < limit).astype(jnp.int32)
    positions = own_shard * live_ref.shape[0] + lax.broadcasted_iota(jnp.int32, live_ref.shape, 0)
    live_ref[...] = (positions < counts_ref[own_span]).astype(jnp.int32)

    get_gate.wait()
    chosen = lax.broadcasted_iota(jnp.int32, (gate_rows, 1), 0) == level - first_row
    gate = jnp.where(chosen, gate_ref[...].astype(jnp.float32), 0.0)
    gate_row_ref[...] = jnp.sum(gate, axis=0, keepdims=True)
    for copy in pending:
        copy.wait()


def prepare(levels, span_mask, counts, gate_table, w_out, keys, pieces, tokens, first, widths, after):
    depth = w_out.shape[0]
    columns = gate_table.shape[1]
    gate_rows = 16
    return pl.pallas_call(
        functools.partial(prepare_kernel, pieces, len(after), len(widths), first),
        out_shape=[
            vmem_out((1, keys), jnp.int32),
            vmem_out((tokens, HD), jnp.int32),
            vmem_out((1, columns), jnp.float32),
            *[vmem_out((depth, width), w_out.dtype) for width in widths],
        ],
        in_specs=[ANY] * (5 + len(after)),
        out_specs=[VMEM] * (3 + len(widths)),
        scratch_shapes=[
            pltpu.SMEM(levels.shape, levels.dtype),
            pltpu.SMEM(span_mask.shape, span_mask.dtype),
            pltpu.SMEM(counts.shape, counts.dtype),
            pltpu.VMEM((gate_rows, columns), gate_table.dtype),
            pltpu.SemaphoreType.DMA((4,)),
            pltpu.SemaphoreType.DMA((max(1, FETCH_COPIES * len(widths)),)),
        ],
        compiler_params=pltpu.CompilerParams(vmem_limit_bytes=VMEM_LIMIT),
        cost_estimate=pl.CostEstimate(
            flops=2 * gate_rows * columns,
            bytes_accessed=2 * gate_rows * columns + 4 * depth * sum(widths),
            transcendentals=0,
        ),
        name="prepare",
    )(*[in_hbm(array) for array in (levels, span_mask, counts, gate_table, w_out)], *after)


def softmax_block(query, keys, values, usable):
    scores = lax.dot_general(
        query, keys, (((1,), (1,)), ((), ())), preferred_element_type=jnp.float32
    )
    scores = jnp.where(usable, scores, NEG_FILL)
    highest = jnp.max(scores, axis=1, keepdims=True)
    weights = jnp.exp2((scores - highest) * EXP_SCALE)
    totals = jnp.sum(weights, axis=1, keepdims=True)
    summed = jnp.dot(weights.astype(jnp.bfloat16), values, preferred_element_type=jnp.float32)
    return summed / totals


def attend(usable, groups, sharing, row_tile, query_refs, kv_refs, out_ref):
    group_width = groups * HD
    span = sharing * HD
    key_firsts = [r.shape[1] - 2 * group_width for r in kv_refs]
    value_firsts = [r.shape[1] - group_width for r in kv_refs]
    for g in range(groups):
        keys = jnp.concatenate(
            [r[:, a + g * HD : a + (g + 1) * HD] for r, a in zip(kv_refs, key_firsts)], axis=0
        )
        values = jnp.concatenate(
            [r[:, a + g * HD : a + (g + 1) * HD] for r, a in zip(kv_refs, value_firsts)], axis=0
        )
        done = 0
        for query_ref in query_refs:
            rows = query_ref.shape[0]
            for first in range(0, rows, row_tile):
                tile = min(row_tile, rows - first)
                query = jnp.concatenate(
                    [
                        query_ref[first : first + tile, g * span + h * HD : g * span + (h + 1) * HD]
                        for h in range(sharing)
                    ],
                    axis=0,
                )
                result = softmax_block(query, keys, values, usable).astype(jnp.bfloat16)
                for h in range(sharing):
                    out_ref[
                        done + first : done + first + tile,
                        g * span + h * HD : g * span + (h + 1) * HD,
                    ] = result[h * tile : (h + 1) * tile]
            done += rows


def attention_kernel(n_query, n_kv, groups, sharing, row_tile, usable_ref, *refs):
    query_refs, kv_refs, out_ref = refs[:n_query], refs[n_query : n_query + n_kv], refs[-1]
    usable = usable_ref[...] > 0
    attend(usable, groups, sharing, row_tile, query_refs, kv_refs, out_ref)


def attention(usable, query_pieces, kv_pieces, groups, sharing, after):
    rows = sum(p.shape[0] for p in query_pieces)
    keys = usable.shape[1]
    width = groups * sharing * HD
    row_tile = 64
    scores_bytes = 4 * sharing * row_tile * keys
    operands = [usable, *query_pieces, *kv_pieces, *after]
    return pl.pallas_call(
        functools.partial(
            attention_kernel, len(query_pieces), len(kv_pieces), groups, sharing, row_tile
        ),
        out_shape=jax.ShapeDtypeStruct((rows, width), jnp.bfloat16),
        in_specs=[VMEM] * len(operands),
        out_specs=VMEM,
        compiler_params=pltpu.CompilerParams(
            vmem_limit_bytes=max(VMEM_LIMIT, 12 * scores_bytes)
        ),
        cost_estimate=pl.CostEstimate(
            flops=4 * rows * width * keys,
            bytes_accessed=4 * rows * width + 4 * groups * HD * keys,
            transcendentals=rows * keys * groups * sharing,
        ),
        name="attention",
    )(*operands)


def project_kernel(own_rows, tile, n_weights, n_after, fetch_first, attended_ref, *refs):
    weight_refs = refs[:n_weights]
    rest = refs[n_weights + n_after :]
    pending = []
    if fetch_first is None:
        own_ref, other_ref = rest
    else:
        weight_hbm, own_ref, other_ref, fetched_ref, sems = rest
        pending = fetch_copies(weight_hbm, fetch_first, [fetched_ref], sems)
    for copy in pending:
        copy.start()
    attended = attended_ref[...]
    done = 0
    for weight_ref in weight_refs:
        for first in range(0, weight_ref.shape[1], tile):
            weights = weight_ref[:, first : first + tile]
            product = jnp.dot(attended, weights, preferred_element_type=jnp.float32)
            columns = slice(done + first, done + first + tile)
            own_ref[:, columns] = product[:own_rows]
            other_ref[:, columns] = product[own_rows:].astype(jnp.bfloat16)
        done += weight_ref.shape[1]
    for copy in pending:
        copy.wait()


def project(attended, weights, own_rows, after, w_out=None, fetch_first=None, fetch_width=0):
    rows, depth = attended.shape
    count = sum(w.shape[1] for w in weights)
    other_rows = rows - own_rows
    out_shape = [
        jax.ShapeDtypeStruct((own_rows, count), jnp.float32),
        jax.ShapeDtypeStruct((other_rows, count), jnp.bfloat16),
    ]
    operands = [attended, *[in_vmem(w) for w in weights], *after]
    in_specs = [VMEM] * (1 + len(weights)) + [ANY] * len(after)
    scratch = []
    if fetch_first is not None:
        out_shape.append(vmem_out((depth, fetch_width), w_out.dtype))
        operands.append(in_hbm(w_out))
        in_specs.append(ANY)
        scratch.append(pltpu.SemaphoreType.DMA((FETCH_COPIES,)))
    return pl.pallas_call(
        functools.partial(
            project_kernel, own_rows, 512, len(weights), len(after), fetch_first
        ),
        out_shape=out_shape,
        in_specs=in_specs,
        out_specs=[VMEM] * len(out_shape),
        scratch_shapes=scratch,
        compiler_params=pltpu.CompilerParams(vmem_limit_bytes=VMEM_LIMIT),
        cost_estimate=pl.CostEstimate(
            flops=2 * rows * depth * count, bytes_accessed=2 * depth * count, transcendentals=0
        ),
        name="project",
    )(*operands)


def combine_kernel(first, n_chunks, has_done, live_ref, gate_ref, *refs):
    own_refs, other_refs = refs[:n_chunks], refs[n_chunks : 2 * n_chunks]
    out_hbm, part_ref, sem = refs[2 * n_chunks + has_done :]
    live = live_ref[:, :1] > 0
    start = 0
    for own_ref, other_ref in zip(own_refs, other_refs):
        width = own_ref.shape[1]
        gate = gate_ref[:, first + start : first + start + width]
        gated = (own_ref[...] + other_ref[...].astype(jnp.float32)) * gate
        part_ref[:, start : start + width] = jnp.where(live, gated, 0.0).astype(jnp.bfloat16)
        start += width
    put = pltpu.make_async_copy(part_ref, out_hbm.at[:, pl.ds(first, start)], sem)
    put.start()
    put.wait()


def combine(live, gate_row, own_parts, other_parts, first, done):
    rows = own_parts[0].shape[0]
    width = sum(p.shape[1] for p in own_parts)
    operands = [live, gate_row, *own_parts, *other_parts]
    return pl.pallas_call(
        functools.partial(combine_kernel, first, len(own_parts), len(done)),
        out_shape=hbm_out((rows, gate_row.shape[1]), jnp.bfloat16),
        in_specs=[VMEM] * len(operands) + [ANY] * len(done),
        out_specs=ANY,
        input_output_aliases={len(operands): 0} if done else {},
        scratch_shapes=[pltpu.VMEM((rows, width), jnp.bfloat16), pltpu.SemaphoreType.DMA],
        compiler_params=pltpu.CompilerParams(vmem_limit_bytes=VMEM_LIMIT),
        cost_estimate=pl.CostEstimate(
            flops=2 * rows * width, bytes_accessed=8 * rows * width, transcendentals=0
        ),
        name="combine",
    )(*operands, *[in_hbm(array) for array in done])


def send_up(piece, back, first, spans):
    return lax.ppermute(piece, "span", [(i, i + back) for i in range(first, spans - back)])


def local(queries, key_value, w_out, gate_table, levels, span_mask, counts):
    tokens = queries.shape[0]
    shards = lax.axis_size("head")
    spans = lax.axis_size("span")
    head_count = HEADS // shards
    share = HEADS // KV_GROUPS
    sharing = min(share, head_count)
    copies = max(1, share // head_count)
    groups = head_count // sharing
    group_width = groups * HD
    width = head_count * HD
    columns = w_out.shape[1]
    keys = spans * shards * tokens
    small = (levels, span_mask, counts, gate_table, w_out)

    if shards == 2:
        swap = [(0, 1), (1, 0)]
        own_kv, sent_kv, own_queries, sent_queries = pair(
            key_value, queries, width, group_width
        )
        usable, live, gate_row = prepare(*small, keys, 2, tokens, 0, [], [])
        other_kv, live = lax.optimization_barrier((lax.ppermute(sent_kv, "head", swap), live))
        received = lax.ppermute(sent_queries, "head", swap)
        unit = columns // 12
        fetches = [[units * unit for units in widths] for widths in FETCH_UNITS]
        firsts = [sum(sum(widths) for widths in fetches[:i]) for i in range(len(fetches))]
        *weights, fetched = fetch(w_out, firsts[0], fetches[0], [other_kv])
        own_blocks, other_blocks = [own_kv], [other_kv]
        for pieces in (own_blocks, other_blocks):
            pieces += [send_up(pieces[0], back, 0, spans) for back in range(1, min(spans, 3))]
            for back in range(3, spans):
                pieces[-1], fetched = lax.optimization_barrier((pieces[-1], fetched))
                pieces.append(send_up(pieces[-1], 1, back - 1, spans))
        *more, fetched = fetch(w_out, firsts[1], fetches[1], [fetched, other_blocks[2]])
        weights += more
        blocks = [piece for both in zip(own_blocks, other_blocks) for piece in both]
        attended = attention(usable, [own_queries, received], blocks, groups, sharing, [fetched])
        own_parts, other_parts = [], []
        for chunk, (first, last) in enumerate(CHUNK_PIECES):
            if chunk < len(CHUNK_PIECES) - 1:
                step = chunk + 2
                more = (w_out, firsts[step], sum(fetches[step]))
            else:
                *late, _ = fetch(w_out, firsts[-1], fetches[-1], own_parts[-1:])
                weights += late
                more = ()
            after = other_parts[chunk - 2 : chunk - 1] if chunk >= 2 else []
            own, other, *fetched = project(attended, weights[first:last], tokens, after, *more)
            weights += fetched
            own_parts.append(own)
            other_parts.append(lax.ppermute(other, "head", swap))
    else:
        kv_parts = split_all(key_value, shards, group_width, copies)
        swapped = lax.all_to_all(jnp.stack(kv_parts), "head", split_axis=0, concat_axis=0)
        kv_piece = swapped.reshape(shards * tokens, 2 * group_width)
        by_shard = queries.reshape(tokens, shards, width).transpose(1, 0, 2)
        swapped = lax.all_to_all(by_shard, "head", split_axis=0, concat_axis=0)
        query_piece = swapped.reshape(shards * tokens, width)
        blocks = [kv_piece]
        for back in range(1, spans):
            blocks.append(send_up(kv_piece, back, 0, spans))
        usable, live, gate_row = prepare(*small, keys, 1, tokens, 0, [], [])
        attended = attention(usable, [query_piece], blocks, groups, sharing, [])
        partial = jnp.dot(attended, w_out, preferred_element_type=jnp.float32)
        summed = lax.psum_scatter(
            partial.astype(jnp.bfloat16), "head", scatter_dimension=0, tiled=True
        )
        own_parts, other_parts = [jnp.zeros(summed.shape, jnp.float32)], [summed]
    done, first = [], 0
    if len(own_parts) > 1:
        done = [combine(live, gate_row, own_parts[:-1], other_parts[:-1], 0, [])]
        first = sum(part.shape[1] for part in own_parts[:-1])
    return combine(live, gate_row, own_parts[-1:], other_parts[-1:], first, done)


def solution(mesh):
    in_specs = (
        P(("rep", "span", "head"), None),
        P(("rep", "span", "head"), None, None),
        P("head", None),
        P(),
        P("rep"),
        P("rep", None),
        P("rep"),
    )
    out_specs = P(("rep", "span", "head"), None)
    return jax.shard_map(local, mesh=mesh, in_specs=in_specs, out_specs=out_specs, check_vma=False)
```
